256 devices in a mesh: slope: 32 (over z_lo, x, core), cross: 8 (over y, z_hi).
Axes of the slice: x: 4, y: 4, z: 8 (z_hi: 2, z_lo: 4; z = z_hi * 4 + z_lo), core: 2. Of those that a mesh axis runs over, the one named last changes fastest.
Arguments:
- offsets: float32 [3, 32, 8, 4096], P(None, 'slope', 'cross'), may hold values from 0.5 to 4.5
- velocity: float32 [3, 32, 8, 4096], P(None, 'slope', 'cross'), may hold values from -4 to 4
- affine: float32 [9, 32, 8, 4096], P(None, 'slope', 'cross'), may hold values from -4 to 4
- strain: float32 [9, 32, 8, 4096], P(None, 'slope', 'cross'), may hold values from -1.5 to 1.5
- particle_mass: float32 [32, 8, 4096], P('slope', 'cross'), may hold values from 0.5 to 2
- plastic_ratio: float32 [32, 8, 4096], P('slope', 'cross'), may hold values from 0.85 to 1.15
- block_counts: int32 [32, 8, 8], P('slope', 'cross'), may hold values from 1 to 512, as said below
Outputs:
- offsets_out: float32 [3, 32, 8, 4096], P(None, 'slope', 'cross')
- velocity_out: float32 [3, 32, 8, 4096], P(None, 'slope', 'cross')
- affine_out: float32 [9, 32, 8, 4096], P(None, 'slope', 'cross')
- deformation: float32 [9, 32, 8, 4096], P(None, 'slope', 'cross')
The draws below stay inside these ranges and needn't reach their ends.
Inputs may be any that keep to these rules, and one draw needn't show every extreme that they name: `block_counts`: the lowest block (k = 0) of every column holds 512 live particles.
All inputs are finite; a program needn't handle non-finite values.
Results may differ from the reference program's by a relative error of at most 0.0003.
Values sent between devices are 32-bit elements; how exact they have to be, the bound alone decides.
A program may use at most 64 MiB of HBM per device.

```python
import math
import jax
import jax.numpy as jnp
from jax import lax

BZ = 8
CAP = 512
STEPS = 5
NBX = 32
NBY = 8
NX = 128
NY = 32
NZ = 32


def draw_block_counts(key, part):
    key = jax.random.fold_in(key, 11)
    leading_entry, second = jax.random.split(key)
    column = jnp.arange(NBX, dtype=jnp.int32)[:, None, None]
    height = jnp.arange(BZ, dtype=jnp.int32)[None, None, :]
    depth = jnp.maximum(1, BZ * (NBX + 2 * column) // (4 * NBX))
    dense = CAP - jax.random.randint(leading_entry, (NBX, NBY, BZ), 0, CAP // 4 + 1)
    sparse = jax.random.randint(second, (NBX, NBY, BZ), 1, 3)
    counts = jnp.where(height < depth, dense, sparse)
    return jnp.where(height == 0, CAP, counts).astype(jnp.int32)


def levels(key, dims, cuts, smallest, largest):
    factor_of = 1.0
    for axis_at, blocks in cuts:
        draws = jax.random.uniform(jax.random.fold_in(jax.random.fold_in(key, 6), axis_at), (blocks,), jnp.float32, smallest / len(cuts), largest / len(cuts))
        factor_of = factor_of * jnp.repeat(jnp.exp(draws), dims[axis_at] // blocks).reshape((-1,) + (1,) * (len(dims) - 1 - axis_at))
    return factor_of


def normal_values(key, dims, scale, most, shards=(), held_as=jnp.bfloat16):
    level = levels(key, dims, shards, -0.22, 0.18) if shards else 1.0
    entries = jax.random.normal(key, dims, jnp.float32) * scale * level
    return jnp.minimum(jnp.maximum(entries, -most), most).astype(held_as)


def setup_inputs(seed: int = 0) -> dict:
    seeds = jax.random.split(jax.random.key(seed), 8)
    return {
        "offsets": jnp.clip(0.5 + 4.0 * jax.random.uniform(seeds[0], (3, NBX, NBY, BZ * CAP), jnp.float32) ** levels(seeds[0], (3, NBX, NBY, BZ * CAP), ((1, 32), (2, 8)), -0.2, 0.2), 0.5, 4.5),
        "velocity": normal_values(seeds[1], (3, NBX, NBY, BZ * CAP), 1.0, 4.0, ((1, 32), (2, 8)), jnp.float32),
        "affine": normal_values(seeds[2], (9, NBX, NBY, BZ * CAP), 0.5, 4.0, ((1, 32), (2, 8)), jnp.float32),
        "strain": normal_values(seeds[3], (9, NBX, NBY, BZ * CAP), 0.1, 1.5, ((1, 32), (2, 8)), jnp.float32),
        "particle_mass": jnp.clip(jnp.exp(math.log(2.0) - 1.3862944 * jax.random.uniform(seeds[4], (NBX, NBY, BZ * CAP), jnp.float32) ** levels(seeds[4], (NBX, NBY, BZ * CAP), ((0, 32), (1, 8)), -0.2, 0.2)), 0.5, 2.0),
        "plastic_ratio": jnp.clip(0.85 + 0.29999995 * jax.random.uniform(seeds[5], (NBX, NBY, BZ * CAP), jnp.float32) ** levels(seeds[5], (NBX, NBY, BZ * CAP), ((0, 32), (1, 8)), -0.2, 0.2), 0.85, 1.15),
        "block_counts": draw_block_counts(jax.random.fold_in(seeds[7], 71), 0),
    }


time_step = 0.02
shear_modulus = 4.0
lame_lambda = 4.0
hardening = 10.0
mass_floor = 0.25
gravity_slope = 1.5
gravity_vertical = -2.5


def spline(dist):
    reach = jnp.abs(dist)
    return jnp.where(reach < 0.5, 0.75 - reach * reach, 0.5 * jnp.square(jnp.maximum(1.5 - reach, 0.0)))


def node_offsets():
    nodes = jnp.arange(216, dtype=jnp.int32)
    return ((nodes // 36).astype(jnp.float32), ((nodes // 6) % 6).astype(jnp.float32), (nodes % 6).astype(jnp.float32))


def weight_lookup(offset_values):
    places = jnp.arange(6, dtype=jnp.float32)
    along_x = spline(offset_values[0][..., None] - places)
    along_y = spline(offset_values[1][..., None] - places)
    along_z = spline(offset_values[2][..., None] - places)
    lookup_rows = along_x[..., :, None, None] * along_y[..., None, :, None] * along_z[..., None, None, :]
    return lookup_rows.reshape(offset_values.shape[1], offset_values.shape[2], 216)


def stress_terms(offset_values, vel, affine, frame, mass, plastic, live):
    det = (frame[0] * (frame[4] * frame[8] - frame[5] * frame[7])
           - frame[1] * (frame[3] * frame[8] - frame[5] * frame[6])
           + frame[2] * (frame[3] * frame[7] - frame[4] * frame[6]))
    harden = jnp.exp(hardening * (1.0 - plastic))
    weighted = mass * live
    rows = []
    for leading_entry in range(3):
        for second in range(3):
            stretch = frame[3 * leading_entry] * frame[3 * second] + frame[3 * leading_entry + 1] * frame[3 * second + 1] + frame[3 * leading_entry + 2] * frame[3 * second + 2]
            unit = 1.0 if leading_entry == second else 0.0
            tau = harden * (shear_modulus * (stretch - unit) + lame_lambda * (det - 1.0) * det * unit)
            rows.append(weighted * affine[3 * leading_entry + second] - 4.0 * time_step * live * tau)
    momentum = []
    for leading_entry in range(3):
        moved = rows[3 * leading_entry] * offset_values[0] + rows[3 * leading_entry + 1] * offset_values[1] + rows[3 * leading_entry + 2] * offset_values[2]
        momentum.append(weighted * vel[leading_entry] - moved)
    return jnp.stack([weighted] + momentum + rows)


def deposit(offset_values, feats):
    lookup_rows = weight_lookup(offset_values)
    summed = jnp.einsum("fgp,gpn->fgn", feats, lookup_rows, precision=lax.Precision.HIGHEST)
    lattice_node_x, lattice_node_y, lattice_node_z = node_offsets()
    parts = [summed[0]]
    for leading_entry in range(3):
        parts.append(summed[1 + leading_entry] + summed[4 + 3 * leading_entry] * lattice_node_x + summed[5 + 3 * leading_entry] * lattice_node_y + summed[6 + 3 * leading_entry] * lattice_node_z)
    return jnp.stack(parts), lookup_rows


def return_gather(offset_values, lookup_rows, external_velocity):
    point_velocity = jnp.einsum("iwk,wvk->iwv", external_velocity, lookup_rows, precision=lax.Precision.HIGHEST)
    lattice_node_x, lattice_node_y, lattice_node_z = node_offsets()
    momentum_sum = jnp.stack([external_velocity[leading_entry] * location for leading_entry in range(3) for location in (lattice_node_x, lattice_node_y, lattice_node_z)])
    paired = jnp.einsum("iwk,wvk->iwv", momentum_sum, lookup_rows, precision=lax.Precision.HIGHEST)
    rows = []
    for leading_entry in range(3):
        for second in range(3):
            rows.append(4.0 * (paired[3 * leading_entry + second] - point_velocity[leading_entry] * offset_values[second]))
    return point_velocity, jnp.stack(rows)


def advance(offset_values, frame, point_velocity, updated_affine):
    moved = offset_values + time_step * point_velocity
    rows = []
    for leading_entry in range(3):
        for second in range(3):
            change = updated_affine[3 * leading_entry] * frame[second] + updated_affine[3 * leading_entry + 1] * frame[3 + second] + updated_affine[3 * leading_entry + 2] * frame[6 + second]
            rows.append(frame[3 * leading_entry + second] + time_step * change)
    return moved, jnp.stack(rows)


def fold_pair(arr, axis):
    moved = jnp.moveaxis(arr, (axis, axis + 1), (-2, -1))
    count = moved.shape[-2]
    lead = moved.shape[:-2]
    keep = [(0, 0)] * len(lead)
    lower = moved[..., :4].reshape(lead + (4 * count,))
    upper = jnp.pad(moved[..., 4:], keep + [(0, 0), (0, 2)]).reshape(lead + (4 * count,))
    total = jnp.pad(lower, keep + [(0, 4)]) + jnp.pad(upper, keep + [(4, 0)])
    return jnp.moveaxis(total[..., :4 * count + 2], -1, axis)


def unfold_pair(arr, axis):
    moved = jnp.moveaxis(arr, axis, -1)
    count = (moved.shape[-1] - 2) // 4
    lead = moved.shape[:-1]
    keep = [(0, 0)] * len(lead)
    lower = moved[..., :4 * count].reshape(lead + (count, 4))
    upper = jnp.pad(moved[..., 4:], keep + [(0, 2)]).reshape(lead + (count, 4))[..., :2]
    joined = jnp.concatenate([lower, upper], axis=-1)
    return jnp.moveaxis(joined, (-2, -1), (axis, axis + 1))


def grid_velocity(grid, x_start, y_start, full_x, full_y):
    scale = jnp.maximum(grid[0], mass_floor)
    speed_x = grid[1] / scale + time_step * gravity_slope
    speed_y = grid[2] / scale
    speed_z = grid[3] / scale + time_step * gravity_vertical
    place_x = x_start + jnp.arange(grid.shape[1], dtype=jnp.int32)[:, None, None]
    place_y = y_start + jnp.arange(grid.shape[2], dtype=jnp.int32)[None, :, None]
    place_z = jnp.arange(grid.shape[3], dtype=jnp.int32)[None, None, :]
    speed_x = jnp.where(place_x < 2, jnp.maximum(speed_x, 0.0), speed_x)
    speed_x = jnp.where(place_x >= full_x - 2, jnp.minimum(speed_x, 0.0), speed_x)
    speed_y = jnp.where(place_y < 2, jnp.maximum(speed_y, 0.0), speed_y)
    speed_y = jnp.where(place_y >= full_y - 2, jnp.minimum(speed_y, 0.0), speed_y)
    speed_z = jnp.where(place_z >= grid.shape[3] - 2, jnp.minimum(speed_z, 0.0), speed_z)
    grounded = place_z < 2
    return jnp.stack([jnp.where(grounded, 0.0, speed_x), jnp.where(grounded, 0.0, speed_y), jnp.where(grounded, 0.0, speed_z)])


def reference(offsets, velocity, affine, strain, particle_mass, plastic_ratio, block_counts):
    column_list = NBY * BZ
    slots = jnp.arange(CAP, dtype=jnp.int32)
    live = (slots < block_counts[..., None]).astype(jnp.float32).reshape(NBX, column_list, CAP)
    offset_values = offsets.reshape(3, NBX, column_list, CAP)
    vel = velocity.reshape(3, NBX, column_list, CAP)
    aff = affine.reshape(9, NBX, column_list, CAP)
    frame = strain.reshape(9, NBX, column_list, CAP) + jnp.eye(3, dtype=jnp.float32).reshape(9, 1, 1, 1)
    mass = particle_mass.reshape(NBX, column_list, CAP)
    plastic = plastic_ratio.reshape(NBX, column_list, CAP)
    starts = 4 * jnp.arange(NBX, dtype=jnp.int32)
    for step in range(STEPS):
        feats = stress_terms(offset_values, vel, aff, frame, mass, plastic, live)

        def slab_deposit(index_couple):
            nodes, lookup_rows = deposit(index_couple[0], index_couple[1])
            shaped = nodes.reshape(4, NBY, BZ, 6, 6, 6).transpose(0, 3, 1, 4, 2, 5)
            return fold_pair(fold_pair(shaped, 4), 2)

        slabs = lax.map(slab_deposit, (jnp.moveaxis(offset_values, 1, 0), jnp.moveaxis(feats, 1, 0)))
        grid = fold_pair(jnp.moveaxis(slabs, 0, 1), 1)[:, :NX, :NY, :NZ]
        speed = grid_velocity(grid, 0, 0, NX, NY)
        padded = jnp.pad(speed, ((0, 0), (0, 2), (0, 2), (0, 2)))

        def slab_gather(index_couple):
            stencil_window = lax.dynamic_slice_in_dim(padded, index_couple[0], 6, 1)
            stencil_window = unfold_pair(unfold_pair(stencil_window, 3), 2)
            external_velocity = stencil_window.transpose(0, 2, 4, 1, 3, 5).reshape(3, column_list, 216)
            return return_gather(index_couple[1], weight_lookup(index_couple[1]), external_velocity)

        point_velocity, updated_affine = lax.map(slab_gather, (starts, jnp.moveaxis(offset_values, 1, 0)))
        point_velocity = jnp.moveaxis(point_velocity, 0, 1)
        updated_affine = jnp.moveaxis(updated_affine, 0, 1)
        offset_values, frame = advance(offset_values, frame, point_velocity, updated_affine)
        vel = point_velocity
        aff = updated_affine
    offsets_out = (offset_values * live).reshape(3, NBX, NBY, BZ * CAP)
    velocity_out = (vel * live).reshape(3, NBX, NBY, BZ * CAP)
    affine_out = (aff * live).reshape(9, NBX, NBY, BZ * CAP)
    deformation = (frame * live).reshape(9, NBX, NBY, BZ * CAP)
    return (offsets_out, velocity_out, affine_out, deformation)
```

```python
import functools

import jax
import jax.numpy as jnp
from jax import lax
from jax.experimental import pallas as pl
from jax.experimental.pallas import tpu as pltpu
from jax.sharding import PartitionSpec as P

STEPS = 5
BLOCKS = 8
ROWS = 32
CHUNKS = 4
TILES = 4
VMEM_BYTES = 60 * 1024 * 1024
MESH = pl.DeviceIdType.MESH

time_step = 0.02
shear_modulus = 4.0
lame_lambda = 4.0
hardening = 10.0
mass_floor = 0.25
gravity_slope = 1.5
gravity_vertical = -2.5
CENTRE = 2.5

DIRECTIONS = [(0, -1), (0, 1), (-1, -1), (-1, 1), (1, -1), (1, 1), (-1, 0), (1, 0)]


def iota(shape, dim):
    return lax.broadcasted_iota(jnp.int32, shape, dim)


def axis_weights(position):
    base = jnp.floor(position + 0.5)
    dist = position - base
    lower = 0.5 * (0.5 - dist) * (0.5 - dist)
    middle = 0.75 - dist * dist
    upper = 0.5 * (0.5 + dist) * (0.5 + dist)
    at = {e: base == float(e) for e in range(-1, 7)}
    return [
        jnp.where(at[e], middle, jnp.where(at[e + 1], lower, jnp.where(at[e - 1], upper, 0.0)))
        for e in range(6)
    ]


def split(values):
    high = values.astype(jnp.bfloat16)
    low = (values - high.astype(jnp.float32)).astype(jnp.bfloat16)
    return high, low


def kernel(
    nx, ny,
    counts, off_hbm, vel_hbm, aff_hbm, strain_hbm, mass_hbm, plastic_hbm,
    off, vel, aff, frame,
    strain_in, mass_in, plastic_in, live_ref, mw_ref, hard_ref, wx, wy, wz, feats, bs, us, gathered,
    send_x, send_low, send_high, recv_x, recv_low, recv_high, diag_low, diag_high,
    load_sem, send_sem, recv_sem,
):
    ix = lax.axis_index("slope")
    iy = lax.axis_index("cross")

    def present(dx, dy):
        ok = None
        for d, i, n in ((dx, ix, nx), (dy, iy, ny)):
            if d == 0:
                continue
            here = (i + d >= 0) & (i + d < n)
            ok = here if ok is None else ok & here
        return ok

    loads = [
        pltpu.make_async_copy(source, target, load_sem.at[i])
        for i, (source, target) in enumerate((
            (mass_hbm, mass_in), (plastic_hbm, plastic_in), (off_hbm, off), (vel_hbm, vel),
            (aff_hbm, aff), (strain_hbm, strain_in),
        ))
    ]
    for load in loads:
        load.start()

    for ref in (recv_x, recv_low, recv_high, diag_low, diag_high, wx, wz, us, bs):
        ref[...] = jnp.zeros(ref.shape, ref.dtype)

    barrier = pltpu.get_barrier_semaphore()
    around = jnp.int32(0)
    for dx, dy in DIRECTIONS:
        ok = present(dx, dy)

        @pl.when(ok)
        def _():
            pl.semaphore_signal(barrier, inc=1, device_id=(ix + dx, iy + dy), device_id_type=MESH)

        around = around + jnp.where(ok, 1, 0).astype(jnp.int32)

    row = iota((ROWS, 128), 0)
    slot = (row % CHUNKS) * 128 + iota((ROWS, 128), 1)
    limit = jnp.zeros((ROWS, 128), jnp.int32)
    for k in range(BLOCKS):
        limit = jnp.where(row // CHUNKS == k, counts[k], limit)
    live = jnp.where(slot < limit, 1.0, 0.0).astype(jnp.float32)
    live_ref[...] = live
    for load in loads:
        load.wait()
    mw_ref[...] = mass_in[...] * live
    hard_ref[...] = 4.0 * time_step * live * jnp.exp(hardening * (1.0 - plastic_in[...]))
    for i in range(9):
        frame[i] = strain_in[i] + (1.0 if i % 4 == 0 else 0.0)

    pl.semaphore_wait(barrier, around)

    lane = iota((8, 128), 1)
    sub = iota((8, 128), 0)
    half = lane < 64
    r3 = lane % 8
    e2 = (lane % 64) // 8
    e3 = jnp.where(half, r3, (r3 + 4) % 8)
    ex = sub.astype(jnp.float32) - CENTRE
    ey = e2.astype(jnp.float32) - CENTRE
    ez = e3.astype(jnp.float32) - CENTRE
    own = half | (r3 >= 4)
    group = (lane % 64) // 16

    def copy_to(step, d):
        dx, dy = DIRECTIONS[d]
        back = DIRECTIONS.index((-dx, -dy))
        if dy == 0:
            source, target = send_x, recv_x
        elif dx == 0:
            source, target = (send_low, recv_high) if dy < 0 else (send_high, recv_low)
        else:
            source, target = (send_low, diag_high) if dy < 0 else (send_high, diag_low)
        source, target = source.at[step], target.at[step]
        if dx != 0:
            source = source.at[:, pl.ds(0 if dx < 0 else 4, 2), :]
            target = target.at[:, pl.ds(4 if dx < 0 else 0, 2), :]
        else:
            source = source.at[:, pl.ds(0, 6), :]
            target = target.at[:, pl.ds(0, 6), :]
        return pltpu.make_async_remote_copy(
            src_ref=source, dst_ref=target,
            send_sem=send_sem.at[step, d], recv_sem=recv_sem.at[step, back],
            device_id=(ix + dx, iy + dy), device_id_type=MESH,
        )

    def spread(ref, at):
        return jnp.broadcast_to(ref[pl.ds(at, 1), :], (8, 128))

    def one_step(step, carry):
        o = [off[i] for i in range(3)]
        f = [frame[i] for i in range(9)]
        det = (
            f[0] * (f[4] * f[8] - f[5] * f[7])
            - f[1] * (f[3] * f[8] - f[5] * f[6])
            + f[2] * (f[3] * f[7] - f[4] * f[6])
        )
        bulk = lame_lambda * (det - 1.0) * det
        mw = mw_ref[...]
        hard = hard_ref[...]
        centred = [v - CENTRE for v in o]
        terms = [[None] * 3 for _ in range(3)]
        for a in range(3):
            for b in range(a, 3):
                stretch = f[3 * a] * f[3 * b] + f[3 * a + 1] * f[3 * b + 1] + f[3 * a + 2] * f[3 * b + 2]
                if a == b:
                    tau = hard * (shear_modulus * (stretch - 1.0) + bulk)
                else:
                    tau = hard * (shear_modulus * stretch)
                terms[a][b] = mw * aff[3 * a + b] - tau
                if a != b:
                    terms[b][a] = mw * aff[3 * b + a] - tau
        feats[pl.ds(0, ROWS), :] = mw
        for a in range(3):
            moved = terms[a][0] * centred[0] + terms[a][1] * centred[1] + terms[a][2] * centred[2]
            feats[pl.ds((1 + a) * ROWS, ROWS), :] = mw * vel[a] - moved
            for b in range(3):
                feats[pl.ds((4 + 3 * b + a) * ROWS, ROWS), :] = terms[a][b]
        for e, w in enumerate(axis_weights(o[0])):
            wx[pl.ds(e * ROWS, ROWS), :] = w
        for e, w in enumerate(axis_weights(o[1])):
            wy[pl.ds(e * ROWS, ROWS), :] = w
        for e, w in enumerate(axis_weights(o[2])):
            wz[pl.ds((4 + e) * ROWS, ROWS), :] = w
            if e >= 4:
                wz[pl.ds((e - 4) * ROWS, ROWS), :] = w

        summed = []
        for k in range(BLOCKS):
            sides, planes = [], []
            for c in range(CHUNKS):
                r = CHUNKS * k + c
                wxs = wx[pl.ds(r, 8, stride=ROWS), :]
                wzs = wz[pl.ds(r + (4 * ROWS if k % 2 == 0 else 0), 8, stride=ROWS), :]
                planes.append(
                    jnp.concatenate([spread(wy, e * ROWS + r) * wzs for e in range(6)], axis=0)
                )
                part = [spread(feats, i * ROWS + r) for i in range(13)]
                side = [part[0] * wxs]
                side += [(part[1 + a] + part[4 + a] * ex) * wxs for a in range(3)]
                side += [part[7 + i] * wxs for i in range(6)]
                sides.append(jnp.concatenate(side, axis=0))
            plane_high, plane_low = split(jnp.concatenate(planes, axis=1))
            bs[k, 0:48, :] = plane_high
            bs[k, 64:112, :] = plane_low
            side_high, side_low = split(jnp.concatenate(sides, axis=1))
            dots = lax.dot_general(
                jnp.concatenate([side_high, side_low], axis=0), bs[k],
                (((1,), (1,)), ((), ())), preferred_element_type=jnp.float32,
            )
            total = dots[:80] + dots[80:]
            summed.append(total + pltpu.roll(total, 64, 1))

        fields = []
        for j in range(TILES):
            pair = [
                jnp.where(half, summed[2 * j][8 * i : 8 * i + 8], summed[2 * j + 1][8 * i : 8 * i + 8])
                for i in range(10)
            ]
            fields.append(
                [pair[0]] + [pair[1 + a] + ey * pair[4 + a] + ez * pair[7 + a] for a in range(3)]
            )
        zero = jnp.zeros((8, 128), jnp.float32)
        shifted = [
            [jnp.where(own, fields[j][i], fields[j - 1][i] if j else zero) for i in range(4)]
            for j in range(TILES)
        ]
        mine = {}
        for p in range(2):
            for i in range(4):
                first, second = shifted[2 * p][i], shifted[2 * p + 1][i]
                mine[i, p] = jnp.where(half, first, second) + pltpu.roll(
                    jnp.where(half, second, first), 64, 1
                )
                send_x[step, 2 * i + p] = mine[i, p]
            low, high = zero, zero
            for i in range(4):
                to_low = mine[i, p] if i == 0 else pltpu.roll(mine[i, p], 16 * i, 1)
                shift = (16 * i - 32) % 128
                to_high = mine[i, p] if shift == 0 else pltpu.roll(mine[i, p], shift, 1)
                low = jnp.where(group == i, to_low, low)
                high = jnp.where(group == i, to_high, high)
            send_low[step, p] = low
            send_high[step, p] = high

        for d, (dx, dy) in enumerate(DIRECTIONS):

            @pl.when(present(dx, dy))
            def _():
                copy_to(step, d).start()

        for d, (dx, dy) in enumerate(DIRECTIONS):

            @pl.when(present(dx, dy))
            def _():
                copy_to(step, DIRECTIONS.index((-dx, -dy))).wait_recv()

        velocity = {}
        place_x = 4 * ix + sub
        place_y = 4 * iy + e2
        outside = (place_x >= 4 * nx) | (place_y >= 4 * ny)
        for p in range(2):
            below = recv_low[step, p] + diag_low[step, p]
            above = recv_high[step, p] + diag_high[step, p]
            total = []
            for i in range(4):
                from_low = below if i == 0 else pltpu.roll(below, 128 - 16 * i, 1)
                shift = (32 - 16 * i) % 128
                from_high = above if shift == 0 else pltpu.roll(above, shift, 1)
                extra = jnp.where(group == 0, from_low, jnp.where(group == 2, from_high, 0.0))
                total.append(mine[i, p] + recv_x[step, 2 * i + p] + extra)
            scale = 1.0 / jnp.maximum(total[0], mass_floor)
            speed_x = total[1] * scale + time_step * gravity_slope
            speed_y = total[2] * scale
            speed_z = total[3] * scale + time_step * gravity_vertical
            place_z = 16 * p + jnp.where(half, 0, 8) + r3
            speed_x = jnp.where(place_x < 2, jnp.maximum(speed_x, 0.0), speed_x)
            speed_x = jnp.where(place_x >= 4 * nx - 2, jnp.minimum(speed_x, 0.0), speed_x)
            speed_y = jnp.where(place_y < 2, jnp.maximum(speed_y, 0.0), speed_y)
            speed_y = jnp.where(place_y >= 4 * ny - 2, jnp.minimum(speed_y, 0.0), speed_y)
            speed_z = jnp.where(place_z >= 8 * TILES - 2, jnp.minimum(speed_z, 0.0), speed_z)
            still = outside | (place_z < 2)
            for a, speed in enumerate((speed_x, speed_y, speed_z)):
                velocity[a, p] = jnp.where(still, 0.0, speed)

        turned = {key: pltpu.roll(value, 64, 1) for key, value in velocity.items()}
        for a in range(3):
            turned[a, 2] = zero
        for j in range(TILES):
            p = j // 2
            for a in range(3):
                if j % 2 == 0:
                    window = jnp.where(half | (r3 < 4), velocity[a, p], turned[a, p])
                else:
                    window = jnp.where(
                        half, turned[a, p], jnp.where(r3 >= 4, velocity[a, p], turned[a, p + 1])
                    )
                for b, factor in enumerate((None, ex, ey, ez)):
                    q = 3 * b + a
                    value = window if factor is None else window * factor
                    if q < 8:
                        us[j, pl.ds(q, 6, stride=8), :] = value[:6]
                    else:
                        us[j, pl.ds(48 + q - 8, 6, stride=4), :] = value[:6]

        half80 = iota((80, 128), 1) < 64
        for j in range(TILES):
            both = us[j]
            swapped = pltpu.roll(both, 64, 1)
            for k in (2 * j, 2 * j + 1):
                nodes = jnp.where(half80, both, swapped) if k % 2 == 0 else jnp.where(half80, swapped, both)
                left = jnp.concatenate(split(nodes), axis=1)
                planes = bs[k]
                taken = lax.dot_general(
                    left, jnp.concatenate([planes, planes], axis=0),
                    (((1,), (0,)), ((), ())), preferred_element_type=jnp.float32,
                )
                for c in range(CHUNKS):
                    r = CHUNKS * k + c
                    part = taken[:, 128 * c : 128 * c + 128]
                    weights = [spread(wx, e * ROWS + r) for e in range(6)]
                    first = weights[0] * part[0:8]
                    for e in range(1, 6):
                        first = first + weights[e] * part[8 * e : 8 * e + 8]
                    second = jnp.where(sub < 4, weights[0], weights[1]) * part[48:56]
                    for e in (2, 4):
                        at = 48 + 4 * e
                        second = second + jnp.where(sub < 4, weights[e], weights[e + 1]) * part[at : at + 8]
                    gathered[pl.ds(16 * r, 8), :] = first
                    gathered[pl.ds(16 * r + 8, 8), :] = second

        def quantity(q):
            value = gathered[pl.ds(q, ROWS, stride=16), :]
            if q >= 8:
                value = value + gathered[pl.ds(q + 4, ROWS, stride=16), :]
            return value

        speed = [quantity(a) for a in range(3)]
        change = [None] * 9
        for a in range(3):
            for b in range(3):
                change[3 * a + b] = 4.0 * (quantity(3 + 3 * b + a) - speed[a] * centred[b])
        for a in range(3):
            off[a] = o[a] + time_step * speed[a]
            vel[a] = speed[a]
            for b in range(3):
                aff[3 * a + b] = change[3 * a + b]
                frame[3 * a + b] = f[3 * a + b] + time_step * (
                    change[3 * a] * f[b] + change[3 * a + 1] * f[3 + b] + change[3 * a + 2] * f[6 + b]
                )
        return carry

    lax.fori_loop(0, STEPS, one_step, 0)

    def finish(step, carry):
        for d, (dx, dy) in enumerate(DIRECTIONS):

            @pl.when(present(dx, dy))
            def _():
                copy_to(step, d).wait_send()

        return carry

    lax.fori_loop(0, STEPS, finish, 0)
    live = live_ref[...]
    for ref, count in ((off, 3), (vel, 3), (aff, 9), (frame, 9)):
        for i in range(count):
            ref[i] = ref[i] * live


def write_out(off, vel, aff, frame, off_out, vel_out, aff_out, frame_out, sem):
    copies = [
        pltpu.make_async_copy(source, target, sem.at[i])
        for i, (source, target) in enumerate(
            ((aff, aff_out), (frame, frame_out), (off, off_out), (vel, vel_out))
        )
    ]
    for copy in copies:
        copy.start()
    for copy in copies:
        copy.wait()


def per_device(offsets, velocity, affine, strain, particle_mass, plastic_ratio, block_counts):
    nx, ny = lax.axis_size("slope"), lax.axis_size("cross")
    f32 = jnp.float32
    vmem = pl.BlockSpec(memory_space=pltpu.VMEM)
    smem = pl.BlockSpec(memory_space=pltpu.SMEM)
    hbm = pl.BlockSpec(memory_space=pltpu.HBM)
    outs = pl.pallas_call(
        functools.partial(kernel, nx, ny),
        out_shape=[jax.ShapeDtypeStruct((n, ROWS, 128), f32) for n in (3, 3, 9, 9)],
        in_specs=[smem] + [hbm] * 6,
        out_specs=[vmem] * 4,
        scratch_shapes=[
            pltpu.VMEM((9, ROWS, 128), f32),
            pltpu.VMEM((ROWS, 128), f32),
            pltpu.VMEM((ROWS, 128), f32),
            pltpu.VMEM((ROWS, 128), f32),
            pltpu.VMEM((ROWS, 128), f32),
            pltpu.VMEM((ROWS, 128), f32),
            pltpu.VMEM((8 * ROWS, 128), f32),
            pltpu.VMEM((6 * ROWS, 128), f32),
            pltpu.VMEM((12 * ROWS, 128), f32),
            pltpu.VMEM((13 * ROWS, 128), f32),
            pltpu.VMEM((BLOCKS, 128, 512), jnp.bfloat16),
            pltpu.VMEM((TILES, 80, 128), f32),
            pltpu.VMEM((16 * ROWS, 128), f32),
            pltpu.VMEM((STEPS, 8, 8, 128), f32),
            pltpu.VMEM((STEPS, 2, 8, 128), f32),
            pltpu.VMEM((STEPS, 2, 8, 128), f32),
            pltpu.VMEM((STEPS, 8, 8, 128), f32),
            pltpu.VMEM((STEPS, 2, 8, 128), f32),
            pltpu.VMEM((STEPS, 2, 8, 128), f32),
            pltpu.VMEM((STEPS, 2, 8, 128), f32),
            pltpu.VMEM((STEPS, 2, 8, 128), f32),
            pltpu.SemaphoreType.DMA((6,)),
            pltpu.SemaphoreType.DMA((STEPS, 8)),
            pltpu.SemaphoreType.DMA((STEPS, 8)),
        ],
        compiler_params=pltpu.CompilerParams(
            collective_id=0, has_side_effects=True, vmem_limit_bytes=VMEM_BYTES
        ),
    )(
        block_counts.reshape(BLOCKS),
        offsets.reshape(3, ROWS, 128),
        velocity.reshape(3, ROWS, 128),
        affine.reshape(9, ROWS, 128),
        strain.reshape(9, ROWS, 128),
        particle_mass.reshape(ROWS, 128),
        plastic_ratio.reshape(ROWS, 128),
    )
    outs = pl.pallas_call(
        write_out,
        out_shape=[jax.ShapeDtypeStruct(out.shape, f32) for out in outs],
        in_specs=[hbm] * 4,
        out_specs=[hbm] * 4,
        scratch_shapes=[pltpu.SemaphoreType.DMA((4,))],
        compiler_params=pltpu.CompilerParams(vmem_limit_bytes=VMEM_BYTES),
    )(*outs)
    return tuple(out.reshape(out.shape[0], 1, 1, ROWS * 128) for out in outs)


def solution(mesh):
    wide = P(None, "slope", "cross", None)
    flat = P("slope", "cross", None)
    return jax.shard_map(
        per_device,
        mesh=mesh,
        in_specs=(wide, wide, wide, wide, flat, flat, flat),
        out_specs=(wide, wide, wide, wide),
        check_vma=False,
    )
```

```python
import functools

import jax
import jax.numpy as jnp
from jax import lax
from jax.experimental import pallas as pl
from jax.experimental.pallas import tpu as pltpu
from jax.sharding import PartitionSpec as P

STEPS = 5
BLOCKS = 8
ROWS = 32
CHUNKS = 4
TILES = 4
VMEM_BYTES = 40 * 1024 * 1024
MESH = pl.DeviceIdType.MESH

time_step = 0.02
shear_modulus = 4.0
lame_lambda = 4.0
hardening = 10.0
mass_floor = 0.25
gravity_slope = 1.5
gravity_vertical = -2.5
CENTRE = 2.5

DIRECTIONS = [(0, -1), (0, 1), (-1, -1), (-1, 1), (1, -1), (1, 1), (-1, 0), (1, 0)]


def iota(shape, dim):
    return lax.broadcasted_iota(jnp.int32, shape, dim)


def axis_weights(position):
    base = jnp.floor(position + 0.5)
    dist = position - base
    lower = 0.5 * (0.5 - dist) * (0.5 - dist)
    middle = 0.75 - dist * dist
    upper = 0.5 * (0.5 + dist) * (0.5 + dist)
    at = {e: base == float(e) for e in range(-1, 7)}
    return [
        jnp.where(at[e], middle, jnp.where(at[e + 1], lower, jnp.where(at[e - 1], upper, 0.0)))
        for e in range(6)
    ]


def split(values):
    high = values.astype(jnp.bfloat16)
    low = (values - high.astype(jnp.float32)).astype(jnp.bfloat16)
    return high, low


def kernel(
    nx, ny,
    counts_hbm, off_hbm, vel_hbm, aff_hbm, strain_hbm, mass_hbm, plastic_hbm,
    off, vel, aff, frame,
    counts, strain_in, mass_in, plastic_in, live_ref, mw_ref, hard_ref, wx, wy, wz, feats, bs, us, gathered,
    send_x, send_low, send_high, recv_x, recv_low, recv_high, diag_low, diag_high,
    load_sem, send_sem, recv_sem,
):
    ix = lax.axis_index("slope")
    iy = lax.axis_index("cross")

    def present(dx, dy):
        ok = None
        for d, i, n in ((dx, ix, nx), (dy, iy, ny)):
            if d == 0:
                continue
            here = (i + d >= 0) & (i + d < n)
            ok = here if ok is None else ok & here
        return ok

    loads = [
        pltpu.make_async_copy(source, target, load_sem.at[i])
        for i, (source, target) in enumerate((
            (counts_hbm, counts), (mass_hbm, mass_in), (plastic_hbm, plastic_in), (off_hbm, off), (vel_hbm, vel),
            (aff_hbm, aff), (strain_hbm, strain_in),
        ))
    ]
    for load in loads:
        load.start()

    for ref in (recv_x, recv_low, recv_high, diag_low, diag_high):
        ref[...] = jnp.zeros(ref.shape, ref.dtype)

    barrier = pltpu.get_barrier_semaphore()
    around = jnp.int32(0)
    for dx, dy in DIRECTIONS:
        ok = present(dx, dy)

        @pl.when(ok)
        def _():
            pl.semaphore_signal(barrier, inc=1, device_id=(ix + dx, iy + dy), device_id_type=MESH)

        around = around + jnp.where(ok, 1, 0).astype(jnp.int32)

    for ref in (wx, wz, us, bs):
        ref[...] = jnp.zeros(ref.shape, ref.dtype)
    for load in loads:
        load.wait()
    row = iota((ROWS, 128), 0)
    slot = (row % CHUNKS) * 128 + iota((ROWS, 128), 1)
    limit = jnp.zeros((ROWS, 128), jnp.int32)
    for k in range(BLOCKS):
        limit = jnp.where(row // CHUNKS == k, counts[k], limit)
    live = jnp.where(slot < limit, 1.0, 0.0).astype(jnp.float32)
    live_ref[...] = live
    mw_ref[...] = mass_in[...] * live
    hard_ref[...] = 4.0 * time_step * live * jnp.exp(hardening * (1.0 - plastic_in[...]))
    for i in range(9):
        frame[i] = strain_in[i] + (1.0 if i % 4 == 0 else 0.0)

    lane = iota((8, 128), 1)
    sub = iota((8, 128), 0)
    half = lane < 64
    r3 = lane % 8
    e2 = (lane % 64) // 8
    e3 = jnp.where(half, r3, (r3 + 4) % 8)
    ex = sub.astype(jnp.float32) - CENTRE
    ey = e2.astype(jnp.float32) - CENTRE
    ez = e3.astype(jnp.float32) - CENTRE
    own = half | (r3 >= 4)
    group = (lane % 64) // 16

    def copy_to(step, d):
        dx, dy = DIRECTIONS[d]
        back = DIRECTIONS.index((-dx, -dy))
        if dy == 0:
            source, target = send_x, recv_x
        elif dx == 0:
            source, target = (send_low, recv_high) if dy < 0 else (send_high, recv_low)
        else:
            source, target = (send_low, diag_high) if dy < 0 else (send_high, diag_low)
        source, target = source.at[step], target.at[step]
        if dx != 0:
            source = source.at[:, pl.ds(0 if dx < 0 else 4, 2), :]
            target = target.at[:, pl.ds(4 if dx < 0 else 0, 2), :]
        else:
            source = source.at[:, pl.ds(0, 6), :]
            target = target.at[:, pl.ds(0, 6), :]
        return pltpu.make_async_remote_copy(
            src_ref=source, dst_ref=target,
            send_sem=send_sem.at[step, d], recv_sem=recv_sem.at[step, back],
            device_id=(ix + dx, iy + dy), device_id_type=MESH,
        )

    def spread(ref, at):
        return jnp.broadcast_to(ref[pl.ds(at, 1), :], (8, 128))

    def one_step(step, carry):
        o = [off[i] for i in range(3)]
        f = [frame[i] for i in range(9)]
        det = (
            f[0] * (f[4] * f[8] - f[5] * f[7])
            - f[1] * (f[3] * f[8] - f[5] * f[6])
            + f[2] * (f[3] * f[7] - f[4] * f[6])
        )
        bulk = lame_lambda * (det - 1.0) * det
        mw = mw_ref[...]
        hard = hard_ref[...]
        centred = [v - CENTRE for v in o]
        terms = [[None] * 3 for _ in range(3)]
        for a in range(3):
            for b in range(a, 3):
                stretch = f[3 * a] * f[3 * b] + f[3 * a + 1] * f[3 * b + 1] + f[3 * a + 2] * f[3 * b + 2]
                if a == b:
                    tau = hard * (shear_modulus * (stretch - 1.0) + bulk)
                else:
                    tau = hard * (shear_modulus * stretch)
                terms[a][b] = mw * aff[3 * a + b] - tau
                if a != b:
                    terms[b][a] = mw * aff[3 * b + a] - tau
        feats[pl.ds(0, ROWS), :] = mw
        for a in range(3):
            moved = terms[a][0] * centred[0] + terms[a][1] * centred[1] + terms[a][2] * centred[2]
            feats[pl.ds((1 + a) * ROWS, ROWS), :] = mw * vel[a] - moved
            for b in range(3):
                feats[pl.ds((4 + 3 * b + a) * ROWS, ROWS), :] = terms[a][b]
        for e, w in enumerate(axis_weights(o[0])):
            wx[pl.ds(e * ROWS, ROWS), :] = w
        for e, w in enumerate(axis_weights(o[1])):
            wy[pl.ds(e * ROWS, ROWS), :] = w
        for e, w in enumerate(axis_weights(o[2])):
            wz[pl.ds((4 + e) * ROWS, ROWS), :] = w
            if e >= 4:
                wz[pl.ds((e - 4) * ROWS, ROWS), :] = w

        summed = []
        for k in range(BLOCKS):
            sides, planes = [], []
            for c in range(CHUNKS):
                r = CHUNKS * k + c
                wxs = wx[pl.ds(r, 8, stride=ROWS), :]
                wzs = wz[pl.ds(r + (4 * ROWS if k % 2 == 0 else 0), 8, stride=ROWS), :]
                planes.append(
                    jnp.concatenate([spread(wy, e * ROWS + r) * wzs for e in range(6)], axis=0)
                )
                part = [spread(feats, i * ROWS + r) for i in range(13)]
                side = [part[0] * wxs]
                side += [(part[1 + a] + part[4 + a] * ex) * wxs for a in range(3)]
                side += [part[7 + i] * wxs for i in range(6)]
                sides.append(jnp.concatenate(side, axis=0))
            plane_high, plane_low = split(jnp.concatenate(planes, axis=1))
            bs[k, 0:48, :] = plane_high
            bs[k, 64:112, :] = plane_low
            side_high, side_low = split(jnp.concatenate(sides, axis=1))
            dots = lax.dot_general(
                jnp.concatenate([side_high, side_low], axis=0), bs[k],
                (((1,), (1,)), ((), ())), preferred_element_type=jnp.float32,
            )
            total = dots[:80] + dots[80:]
            summed.append(total + pltpu.roll(total, 64, 1))

        fields = []
        for j in range(TILES):
            pair = [
                jnp.where(half, summed[2 * j][8 * i : 8 * i + 8], summed[2 * j + 1][8 * i : 8 * i + 8])
                for i in range(10)
            ]
            fields.append(
                [pair[0]] + [pair[1 + a] + ey * pair[4 + a] + ez * pair[7 + a] for a in range(3)]
            )
        zero = jnp.zeros((8, 128), jnp.float32)
        shifted = [
            [jnp.where(own, fields[j][i], fields[j - 1][i] if j else zero) for i in range(4)]
            for j in range(TILES)
        ]
        mine = {}
        for p in range(2):
            for i in range(4):
                first, second = shifted[2 * p][i], shifted[2 * p + 1][i]
                mine[i, p] = jnp.where(half, first, second) + pltpu.roll(
                    jnp.where(half, second, first), 64, 1
                )
                send_x[step, 2 * i + p] = mine[i, p]
            low, high = zero, zero
            for i in range(4):
                to_low = mine[i, p] if i == 0 else pltpu.roll(mine[i, p], 16 * i, 1)
                shift = (16 * i - 32) % 128
                to_high = mine[i, p] if shift == 0 else pltpu.roll(mine[i, p], shift, 1)
                low = jnp.where(group == i, to_low, low)
                high = jnp.where(group == i, to_high, high)
            send_low[step, p] = low
            send_high[step, p] = high

        @pl.when(step == 0)
        def _():
            pl.semaphore_wait(barrier, around)

        for d, (dx, dy) in enumerate(DIRECTIONS):

            @pl.when(present(dx, dy))
            def _():
                copy_to(step, d).start()

        for d, (dx, dy) in enumerate(DIRECTIONS):

            @pl.when(present(dx, dy))
            def _():
                copy_to(step, DIRECTIONS.index((-dx, -dy))).wait_recv()

        velocity = {}
        place_x = 4 * ix + sub
        place_y = 4 * iy + e2
        outside = (place_x >= 4 * nx) | (place_y >= 4 * ny)
        for p in range(2):
            below = recv_low[step, p] + diag_low[step, p]
            above = recv_high[step, p] + diag_high[step, p]
            total = []
            for i in range(4):
                from_low = below if i == 0 else pltpu.roll(below, 128 - 16 * i, 1)
                shift = (32 - 16 * i) % 128
                from_high = above if shift == 0 else pltpu.roll(above, shift, 1)
                extra = jnp.where(group == 0, from_low, jnp.where(group == 2, from_high, 0.0))
                total.append(mine[i, p] + recv_x[step, 2 * i + p] + extra)
            scale = 1.0 / jnp.maximum(total[0], mass_floor)
            speed_x = total[1] * scale + time_step * gravity_slope
            speed_y = total[2] * scale
            speed_z = total[3] * scale + time_step * gravity_vertical
            place_z = 16 * p + jnp.where(half, 0, 8) + r3
            speed_x = jnp.where(place_x < 2, jnp.maximum(speed_x, 0.0), speed_x)
            speed_x = jnp.where(place_x >= 4 * nx - 2, jnp.minimum(speed_x, 0.0), speed_x)
            speed_y = jnp.where(place_y < 2, jnp.maximum(speed_y, 0.0), speed_y)
            speed_y = jnp.where(place_y >= 4 * ny - 2, jnp.minimum(speed_y, 0.0), speed_y)
            speed_z = jnp.where(place_z >= 8 * TILES - 2, jnp.minimum(speed_z, 0.0), speed_z)
            still = outside | (place_z < 2)
            for a, speed in enumerate((speed_x, speed_y, speed_z)):
                velocity[a, p] = jnp.where(still, 0.0, speed)

        turned = {key: pltpu.roll(value, 64, 1) for key, value in velocity.items()}
        for a in range(3):
            turned[a, 2] = zero
        for j in range(TILES):
            p = j // 2
            for a in range(3):
                if j % 2 == 0:
                    window = jnp.where(half | (r3 < 4), velocity[a, p], turned[a, p])
                else:
                    window = jnp.where(
                        half, turned[a, p], jnp.where(r3 >= 4, velocity[a, p], turned[a, p + 1])
                    )
                for b, factor in enumerate((None, ex, ey, ez)):
                    q = 3 * b + a
                    value = window if factor is None else window * factor
                    if q < 8:
                        us[j, pl.ds(q, 6, stride=8), :] = value[:6]
                    else:
                        us[j, pl.ds(48 + q - 8, 6, stride=4), :] = value[:6]

        half80 = iota((80, 128), 1) < 64
        for j in range(TILES):
            both = us[j]
            swapped = pltpu.roll(both, 64, 1)
            for k in (2 * j, 2 * j + 1):
                nodes = jnp.where(half80, both, swapped) if k % 2 == 0 else jnp.where(half80, swapped, both)
                left = jnp.concatenate(split(nodes), axis=1)
                planes = bs[k]
                taken = lax.dot_general(
                    left, jnp.concatenate([planes, planes], axis=0),
                    (((1,), (0,)), ((), ())), preferred_element_type=jnp.float32,
                )
                for c in range(CHUNKS):
                    r = CHUNKS * k + c
                    part = taken[:, 128 * c : 128 * c + 128]
                    weights = [spread(wx, e * ROWS + r) for e in range(6)]
                    first = weights[0] * part[0:8]
                    for e in range(1, 6):
                        first = first + weights[e] * part[8 * e : 8 * e + 8]
                    second = jnp.where(sub < 4, weights[0], weights[1]) * part[48:56]
                    for e in (2, 4):
                        at = 48 + 4 * e
                        second = second + jnp.where(sub < 4, weights[e], weights[e + 1]) * part[at : at + 8]
                    gathered[pl.ds(16 * r, 8), :] = first
                    gathered[pl.ds(16 * r + 8, 8), :] = second

        def quantity(q):
            value = gathered[pl.ds(q, ROWS, stride=16), :]
            if q >= 8:
                value = value + gathered[pl.ds(q + 4, ROWS, stride=16), :]
            return value

        speed = [quantity(a) for a in range(3)]
        change = [None] * 9
        for a in range(3):
            for b in range(3):
                change[3 * a + b] = 4.0 * (quantity(3 + 3 * b + a) - speed[a] * centred[b])
        for a in range(3):
            off[a] = o[a] + time_step * speed[a]
            vel[a] = speed[a]
            for b in range(3):
                aff[3 * a + b] = change[3 * a + b]
                frame[3 * a + b] = f[3 * a + b] + time_step * (
                    change[3 * a] * f[b] + change[3 * a + 1] * f[3 + b] + change[3 * a + 2] * f[6 + b]
                )
        return carry

    lax.fori_loop(0, STEPS, one_step, 0)

    def finish(step, carry):
        for d, (dx, dy) in enumerate(DIRECTIONS):

            @pl.when(present(dx, dy))
            def _():
                copy_to(step, d).wait_send()

        return carry

    lax.fori_loop(0, STEPS, finish, 0)
    live = live_ref[...]
    for ref, count in ((off, 3), (vel, 3), (aff, 9), (frame, 9)):
        for i in range(count):
            ref[i] = ref[i] * live


def write_out(off, vel, aff, frame, off_out, vel_out, aff_out, frame_out, sem):
    copies = [
        pltpu.make_async_copy(source, target, sem.at[i])
        for i, (source, target) in enumerate(
            ((aff, aff_out), (frame, frame_out), (off, off_out), (vel, vel_out))
        )
    ]
    for copy in copies:
        copy.start()
    for copy in copies:
        copy.wait()


def per_device(offsets, velocity, affine, strain, particle_mass, plastic_ratio, block_counts):
    nx, ny = lax.axis_size("slope"), lax.axis_size("cross")
    f32 = jnp.float32
    vmem = pl.BlockSpec(memory_space=pltpu.VMEM)
    hbm = pl.BlockSpec(memory_space=pltpu.HBM)
    outs = pl.pallas_call(
        functools.partial(kernel, nx, ny),
        out_shape=[jax.ShapeDtypeStruct((n, ROWS, 128), f32) for n in (3, 3, 9, 9)],
        in_specs=[hbm] * 7,
        out_specs=[vmem] * 4,
        scratch_shapes=[
            pltpu.SMEM((BLOCKS,), jnp.int32),
            pltpu.VMEM((9, ROWS, 128), f32),
            pltpu.VMEM((ROWS, 128), f32),
            pltpu.VMEM((ROWS, 128), f32),
            pltpu.VMEM((ROWS, 128), f32),
            pltpu.VMEM((ROWS, 128), f32),
            pltpu.VMEM((ROWS, 128), f32),
            pltpu.VMEM((8 * ROWS, 128), f32),
            pltpu.VMEM((6 * ROWS, 128), f32),
            pltpu.VMEM((12 * ROWS, 128), f32),
            pltpu.VMEM((13 * ROWS, 128), f32),
            pltpu.VMEM((BLOCKS, 128, 512), jnp.bfloat16),
            pltpu.VMEM((TILES, 80, 128), f32),
            pltpu.VMEM((16 * ROWS, 128), f32),
            pltpu.VMEM((STEPS, 8, 8, 128), f32),
            pltpu.VMEM((STEPS, 2, 8, 128), f32),
            pltpu.VMEM((STEPS, 2, 8, 128), f32),
            pltpu.VMEM((STEPS, 8, 8, 128), f32),
            pltpu.VMEM((STEPS, 2, 8, 128), f32),
            pltpu.VMEM((STEPS, 2, 8, 128), f32),
            pltpu.VMEM((STEPS, 2, 8, 128), f32),
            pltpu.VMEM((STEPS, 2, 8, 128), f32),
            pltpu.SemaphoreType.DMA((7,)),
            pltpu.SemaphoreType.DMA((STEPS, 8)),
            pltpu.SemaphoreType.DMA((STEPS, 8)),
        ],
        compiler_params=pltpu.CompilerParams(
            collective_id=0, has_side_effects=True, vmem_limit_bytes=VMEM_BYTES
        ),
    )(
        *(
            pltpu.with_memory_space_constraint(value, pltpu.HBM)
            for value in (
                block_counts.reshape(BLOCKS),
                offsets.reshape(3, ROWS, 128),
                velocity.reshape(3, ROWS, 128),
                affine.reshape(9, ROWS, 128),
                strain.reshape(9, ROWS, 128),
                particle_mass.reshape(ROWS, 128),
                plastic_ratio.reshape(ROWS, 128),
            )
        ),
    )
    outs = pl.pallas_call(
        write_out,
        out_shape=[jax.ShapeDtypeStruct(out.shape, f32) for out in outs],
        in_specs=[vmem] * 4,
        out_specs=[hbm] * 4,
        scratch_shapes=[pltpu.SemaphoreType.DMA((4,))],
        compiler_params=pltpu.CompilerParams(vmem_limit_bytes=VMEM_BYTES),
    )(*outs)
    return tuple(out.reshape(out.shape[0], 1, 1, ROWS * 128) for out in outs)


def solution(mesh):
    wide = P(None, "slope", "cross", None)
    flat = P("slope", "cross", None)
    return jax.shard_map(
        per_device,
        mesh=mesh,
        in_specs=(wide, wide, wide, wide, flat, flat, flat),
        out_specs=(wide, wide, wide, wide),
        check_vma=False,
    )
```

```python
import functools

import jax
import jax.numpy as jnp
from jax import lax
from jax.experimental import pallas as pl
from jax.experimental.pallas import tpu as pltpu
from jax.sharding import PartitionSpec as P

STEPS = 5
BLOCKS = 8
ROWS = 32
CHUNKS = 4
TILES = 4
VMEM_BYTES = 40 * 1024 * 1024
MESH = pl.DeviceIdType.MESH

time_step = 0.02
shear_modulus = 4.0
lame_lambda = 4.0
hardening = 10.0
mass_floor = 0.25
gravity_slope = 1.5
gravity_vertical = -2.5
CENTRE = 2.5

DIRECTIONS = [(0, -1), (0, 1), (-1, -1), (-1, 1), (1, -1), (1, 1), (-1, 0), (1, 0)]


def iota(shape, dim):
    return lax.broadcasted_iota(jnp.int32, shape, dim)


def axis_weights(position):
    base = jnp.floor(position + 0.5)
    dist = position - base
    lower = 0.5 * (0.5 - dist) * (0.5 - dist)
    middle = 0.75 - dist * dist
    upper = 0.5 * (0.5 + dist) * (0.5 + dist)
    at = {e: base == float(e) for e in range(-1, 7)}
    return [
        jnp.where(at[e], middle, jnp.where(at[e + 1], lower, jnp.where(at[e - 1], upper, 0.0)))
        for e in range(6)
    ]


def split(values):
    high = values.astype(jnp.bfloat16)
    low = (values - high.astype(jnp.float32)).astype(jnp.bfloat16)
    return high, low


def kernel(
    nx, ny,
    counts_hbm, off_hbm, vel_hbm, aff_hbm, strain_hbm, mass_hbm, plastic_hbm,
    off, vel, aff, frame,
    counts, strain_in, mass_in, plastic_in, live_ref, mw_ref, hard_ref, wx, wy, wz, feats, bs, us,
    gathered, lower_speed, first_fields, spill_fields,
    send_x, send_low, send_high, recv_x, recv_low, recv_high, diag_low, diag_high,
    load_sem, send_sem, recv_sem,
):
    ix = lax.axis_index("slope")
    iy = lax.axis_index("cross")

    def neighbour(dx, dy):
        return (ix + dx + nx) % nx, (iy + dy + ny) % ny

    loads = [
        pltpu.make_async_copy(source, target, load_sem.at[i])
        for i, (source, target) in enumerate((
            (counts_hbm, counts), (mass_hbm, mass_in), (plastic_hbm, plastic_in), (off_hbm, off),
            (vel_hbm, vel), (aff_hbm, aff), (strain_hbm, strain_in),
        ))
    ]
    for load in loads:
        load.start()

    for ref in (recv_x, recv_low, recv_high, diag_low, diag_high):
        ref[...] = jnp.zeros(ref.shape, ref.dtype)
    barrier = pltpu.get_barrier_semaphore()
    for dx, dy in DIRECTIONS:
        pl.semaphore_signal(barrier, inc=1, device_id=neighbour(dx, dy), device_id_type=MESH)

    for ref in (wx, wz, us, bs, gathered):
        ref[...] = jnp.zeros(ref.shape, ref.dtype)
    for load in loads:
        load.wait()
    row = iota((ROWS, 128), 0)
    slot = (row % CHUNKS) * 128 + iota((ROWS, 128), 1)
    limit = jnp.zeros((ROWS, 128), jnp.int32)
    for k in range(BLOCKS):
        limit = jnp.where(row // CHUNKS == k, counts[k], limit)
    live = jnp.where(slot < limit, 1.0, 0.0).astype(jnp.float32)
    live_ref[...] = live
    mw_ref[...] = mass_in[...] * live
    hard_ref[...] = 4.0 * time_step * live * jnp.exp(hardening * (1.0 - plastic_in[...]))
    for i in range(9):
        frame[i] = strain_in[i] + (1.0 if i % 4 == 0 else 0.0)

    lane = iota((8, 128), 1)
    sub = iota((8, 128), 0)
    half = lane < 64
    r3 = lane % 8
    e2 = (lane % 64) // 8
    e3 = jnp.where(half, r3, (r3 + 4) % 8)
    ex = sub.astype(jnp.float32) - CENTRE
    ey = e2.astype(jnp.float32) - CENTRE
    ez = e3.astype(jnp.float32) - CENTRE
    own = half | (r3 >= 4)
    group = (lane % 64) // 16
    half80 = iota((80, 128), 1) < 64
    zero = jnp.zeros((8, 128), jnp.float32)
    place_x = 4 * ix + sub
    place_y = 4 * iy + e2
    inner_x = ((sub >= 2) | (ix > 0)) & ((sub < 4) | (ix < nx - 1))
    at_low = (group == 0) & (iy > 0)
    at_high = (group == 2) & (iy < ny - 1)
    outside = (place_x >= 4 * nx) | (place_y >= 4 * ny)

    def copy_to(step, p, d):
        dx, dy = DIRECTIONS[d]
        back = DIRECTIONS.index((-dx, -dy))
        if dy == 0:
            source, target = send_x.at[step, p], recv_x.at[step, p]
            source = source.at[:, pl.ds(0 if dx < 0 else 4, 2), :]
            target = target.at[:, pl.ds(4 if dx < 0 else 0, 2), :]
        else:
            if dx == 0:
                source, target = (send_low, recv_high) if dy < 0 else (send_high, recv_low)
                here, there = pl.ds(0, 6), pl.ds(0, 6)
            else:
                source, target = (send_low, diag_high) if dy < 0 else (send_high, diag_low)
                here, there = pl.ds(0 if dx < 0 else 4, 2), pl.ds(4 if dx < 0 else 0, 2)
            source, target = source.at[step, p, here, :], target.at[step, p, there, :]
        return pltpu.make_async_remote_copy(
            src_ref=source, dst_ref=target,
            send_sem=send_sem.at[step, p, d], recv_sem=recv_sem.at[step, p, back],
            device_id=neighbour(dx, dy), device_id_type=MESH,
        )

    def spread(ref, at):
        return jnp.broadcast_to(ref[pl.ds(at, 1), :], (8, 128))

    def terms(j, o, f, v, c):
        rows = pl.ds(8 * j, 8)
        det = (
            f[0] * (f[4] * f[8] - f[5] * f[7])
            - f[1] * (f[3] * f[8] - f[5] * f[6])
            + f[2] * (f[3] * f[7] - f[4] * f[6])
        )
        bulk = lame_lambda * (det - 1.0) * det
        mw = mw_ref[rows, :]
        hard = hard_ref[rows, :]
        terms_ = [[None] * 3 for _ in range(3)]
        for a in range(3):
            for b in range(a, 3):
                stretch = f[3 * a] * f[3 * b] + f[3 * a + 1] * f[3 * b + 1] + f[3 * a + 2] * f[3 * b + 2]
                if a == b:
                    tau = hard * (shear_modulus * (stretch - 1.0) + bulk)
                else:
                    tau = hard * (shear_modulus * stretch)
                terms_[a][b] = mw * c[3 * a + b] - tau
                if a != b:
                    terms_[b][a] = mw * c[3 * b + a] - tau
        feats[pl.ds(8 * j, 8), :] = mw
        for a in range(3):
            moved = (
                terms_[a][0] * (o[0] - CENTRE)
                + terms_[a][1] * (o[1] - CENTRE)
                + terms_[a][2] * (o[2] - CENTRE)
            )
            feats[pl.ds((1 + a) * ROWS + 8 * j, 8), :] = mw * v[a] - moved
            for b in range(3):
                feats[pl.ds((4 + 3 * b + a) * ROWS + 8 * j, 8), :] = terms_[a][b]
        for e, w in enumerate(axis_weights(o[0])):
            wx[pl.ds(e * ROWS + 8 * j, 8), :] = w
        for e, w in enumerate(axis_weights(o[1])):
            wy[pl.ds(e * ROWS + 8 * j, 8), :] = w
        for e, w in enumerate(axis_weights(o[2])):
            wz[pl.ds((4 + e) * ROWS + 8 * j, 8), :] = w
            if e >= 4:
                wz[pl.ds((e - 4) * ROWS + 8 * j, 8), :] = w

    def deposit(k):
        sides, planes = [], []
        for c in range(CHUNKS):
            r = CHUNKS * k + c
            wxs = wx[pl.ds(r, 8, stride=ROWS), :]
            wzs = wz[pl.ds(r + (4 * ROWS if k % 2 == 0 else 0), 8, stride=ROWS), :]
            planes.append(
                jnp.concatenate([spread(wy, e * ROWS + r) * wzs for e in range(6)], axis=0)
            )
            part = [spread(feats, i * ROWS + r) for i in range(13)]
            side = [part[0] * wxs]
            side += [(part[1 + a] + part[4 + a] * ex) * wxs for a in range(3)]
            side += [part[7 + i] * wxs for i in range(6)]
            sides.append(jnp.concatenate(side, axis=0))
        plane_high, plane_low = split(jnp.concatenate(planes, axis=1))
        bs[k, 0:48, :] = plane_high
        bs[k, 64:112, :] = plane_low
        side_high, side_low = split(jnp.concatenate(sides, axis=1))
        dots = lax.dot_general(
            jnp.concatenate([side_high, side_low], axis=0), bs[k],
            (((1,), (1,)), ((), ())), preferred_element_type=jnp.float32,
        )
        total = dots[:80] + dots[80:]
        return total + pltpu.roll(total, 64, 1)

    def deposit_tile(j):
        even, odd = deposit(2 * j), deposit(2 * j + 1)
        pair = [jnp.where(half, even[8 * i : 8 * i + 8], odd[8 * i : 8 * i + 8]) for i in range(10)]
        return [pair[0]] + [pair[1 + a] + ey * pair[4 + a] + ez * pair[7 + a] for a in range(3)]

    def send(step, p, before, first, second):
        low, high = zero, zero
        for i in range(4):
            one = jnp.where(own, first[i], before[i])
            two = jnp.where(own, second[i], first[i])
            mine = jnp.where(half, one, two) + pltpu.roll(jnp.where(half, two, one), 64, 1)
            send_x[step, p, i] = mine
            to_low = mine if i == 0 else pltpu.roll(mine, 16 * i, 1)
            shift = (16 * i - 32) % 128
            to_high = mine if shift == 0 else pltpu.roll(mine, shift, 1)
            low = jnp.where(group == i, to_low, low)
            high = jnp.where(group == i, to_high, high)
        send_low[step, p] = low
        send_high[step, p] = high

    def start(step, p):
        for d in range(8):
            copy_to(step, p, d).start()

    def arrive(step, p):
        for d in range(8):
            copy_to(step, p, d).wait_recv()

    def grid_speed(step, p):
        below = recv_low[step, p] + jnp.where(inner_x, diag_low[step, p], 0.0)
        above = recv_high[step, p] + jnp.where(inner_x, diag_high[step, p], 0.0)
        total = []
        for i in range(4):
            from_low = below if i == 0 else pltpu.roll(below, 128 - 16 * i, 1)
            shift = (32 - 16 * i) % 128
            from_high = above if shift == 0 else pltpu.roll(above, shift, 1)
            extra = jnp.where(at_low, from_low, jnp.where(at_high, from_high, 0.0))
            side = jnp.where(inner_x, recv_x[step, p, i], 0.0)
            total.append(send_x[step, p, i] + side + extra)
        scale = 1.0 / jnp.maximum(total[0], mass_floor)
        speed_x = total[1] * scale + time_step * gravity_slope
        speed_y = total[2] * scale
        speed_z = total[3] * scale + time_step * gravity_vertical
        place_z = 16 * p + jnp.where(half, 0, 8) + r3
        speed_x = jnp.where(place_x < 2, jnp.maximum(speed_x, 0.0), speed_x)
        speed_x = jnp.where(place_x >= 4 * nx - 2, jnp.minimum(speed_x, 0.0), speed_x)
        speed_y = jnp.where(place_y < 2, jnp.maximum(speed_y, 0.0), speed_y)
        speed_y = jnp.where(place_y >= 4 * ny - 2, jnp.minimum(speed_y, 0.0), speed_y)
        speed_z = jnp.where(place_z >= 8 * TILES - 2, jnp.minimum(speed_z, 0.0), speed_z)
        still = outside | (place_z < 2)
        return [jnp.where(still, 0.0, speed) for speed in (speed_x, speed_y, speed_z)]

    def windows(j, speed, turned, beyond):
        for a in range(3):
            if j % 2 == 0:
                window = jnp.where(half | (r3 < 4), speed[a], turned[a])
            else:
                window = jnp.where(half, turned[a], jnp.where(r3 >= 4, speed[a], beyond[a]))
            for b, factor in enumerate((None, ex, ey, ez)):
                q = 3 * b + a
                value = window if factor is None else window * factor
                if q < 8:
                    us[j, pl.ds(q, 6, stride=8), :] = value[:6]
                else:
                    us[j, pl.ds(48 + q - 8, 6, stride=4), :] = value[:6]

    def gather(k):
        both = us[k // 2]
        swapped = pltpu.roll(both, 64, 1)
        nodes = jnp.where(half80, both, swapped) if k % 2 == 0 else jnp.where(half80, swapped, both)
        left = jnp.concatenate(split(nodes), axis=1)
        planes = bs[k]
        taken = lax.dot_general(
            left, jnp.concatenate([planes, planes], axis=0),
            (((1,), (0,)), ((), ())), preferred_element_type=jnp.float32,
        )
        for c in range(CHUNKS):
            r = CHUNKS * k + c
            part = taken[:, 128 * c : 128 * c + 128]
            weights = [spread(wx, e * ROWS + r) for e in range(6)]
            first = weights[0] * part[0:8]
            for e in range(1, 6):
                first = first + weights[e] * part[8 * e : 8 * e + 8]
            second = jnp.where(sub < 4, weights[0], weights[1]) * part[48:56]
            for e in (2, 4):
                at = 48 + 4 * e
                second = second + jnp.where(sub < 4, weights[e], weights[e + 1]) * part[at : at + 8]
            gathered[pl.ds(16 * r, 8), :] = first
            gathered[pl.ds(16 * r + 8, 8), :] = second

    def advance(j):
        rows = pl.ds(8 * j, 8)

        def quantity(q):
            value = gathered[pl.ds(128 * j + q, 8, stride=16), :]
            if q >= 8:
                value = value + gathered[pl.ds(128 * j + q + 4, 8, stride=16), :]
            return value

        o = [off[i, rows, :] for i in range(3)]
        f = [frame[i, rows, :] for i in range(9)]
        v = [quantity(a) for a in range(3)]
        c = [None] * 9
        for a in range(3):
            for b in range(3):
                c[3 * a + b] = 4.0 * (quantity(3 + 3 * b + a) - v[a] * (o[b] - CENTRE))
        o = [o[a] + time_step * v[a] for a in range(3)]
        f = [
            f[3 * a + b]
            + time_step * (c[3 * a] * f[b] + c[3 * a + 1] * f[3 + b] + c[3 * a + 2] * f[6 + b])
            for a in range(3)
            for b in range(3)
        ]
        for ref, values in ((off, o), (vel, v), (aff, c), (frame, f)):
            for i, value in enumerate(values):
                ref[i, rows, :] = value
        return o, f, v, c

    def keep(ref, values):
        for i, value in enumerate(values):
            ref[i] = value

    def turn(values):
        return [pltpu.roll(value, 64, 1) for value in values]

    def phases(step, go_on):
        arrive(step, 0)
        speed = grid_speed(step, 0)
        turned = turn(speed)
        keep(lower_speed, speed)
        windows(0, speed, turned, None)
        windows(1, speed, turned, [zero] * 3)
        for k in range(3):
            gather(k)
        state = advance(0)
        if go_on:
            terms(0, *state)
            keep(first_fields, deposit_tile(0))

        arrive(step, 1)
        upper = grid_speed(step, 1)
        upper_turned = turn(upper)
        speed = [lower_speed[a] for a in range(3)]
        windows(1, speed, turn(speed), upper_turned)
        gather(3)
        state = advance(1)
        if go_on:
            terms(1, *state)
            fields = deposit_tile(1)
            keep(spill_fields, fields)
            send(step + 1, 0, [zero] * 4, [first_fields[i] for i in range(4)], fields)
            start(step + 1, 0)

        windows(2, upper, upper_turned, None)
        windows(3, upper, upper_turned, [zero] * 3)
        for k in range(4, 8):
            gather(k)
        states = [advance(2), advance(3)]
        if go_on:
            terms(2, *states[0])
            terms(3, *states[1])
            fields = [deposit_tile(2), deposit_tile(3)]
            send(step + 1, 1, [spill_fields[i] for i in range(4)], *fields)
            start(step + 1, 1)

    for j in range(TILES):
        rows = pl.ds(8 * j, 8)
        terms(j, *([ref[i, rows, :] for i in range(n)] for ref, n in ((off, 3), (frame, 9), (vel, 3), (aff, 9))))
    fields = [deposit_tile(0), deposit_tile(1)]
    send(0, 0, [zero] * 4, *fields)
    pl.semaphore_wait(barrier, 8)
    start(0, 0)
    before = fields[1]
    fields = [deposit_tile(2), deposit_tile(3)]
    send(0, 1, before, *fields)
    start(0, 1)

    def one_step(step, carry):
        phases(step, True)
        return carry

    lax.fori_loop(0, STEPS - 1, one_step, 0)
    phases(STEPS - 1, False)

    def finish(step, carry):
        for p in range(2):
            for d in range(8):
                copy_to(step, p, d).wait_send()
        return carry

    lax.fori_loop(0, STEPS, finish, 0)
    live = live_ref[...]
    for ref, count in ((off, 3), (vel, 3), (aff, 9), (frame, 9)):
        for i in range(count):
            ref[i] = ref[i] * live


def write_out(off, vel, aff, frame, off_out, vel_out, aff_out, frame_out, sem):
    copies = [
        pltpu.make_async_copy(source, target, sem.at[i])
        for i, (source, target) in enumerate(
            ((aff, aff_out), (frame, frame_out), (off, off_out), (vel, vel_out))
        )
    ]
    for copy in copies:
        copy.start()
    for copy in copies:
        copy.wait()


def per_device(offsets, velocity, affine, strain, particle_mass, plastic_ratio, block_counts):
    nx, ny = lax.axis_size("slope"), lax.axis_size("cross")
    f32 = jnp.float32
    vmem = pl.BlockSpec(memory_space=pltpu.VMEM)
    hbm = pl.BlockSpec(memory_space=pltpu.HBM)
    outs = pl.pallas_call(
        functools.partial(kernel, nx, ny),
        out_shape=[jax.ShapeDtypeStruct((n, ROWS, 128), f32) for n in (3, 3, 9, 9)],
        in_specs=[hbm] * 7,
        out_specs=[vmem] * 4,
        scratch_shapes=[
            pltpu.SMEM((BLOCKS,), jnp.int32),
            pltpu.VMEM((9, ROWS, 128), f32),
            pltpu.VMEM((ROWS, 128), f32),
            pltpu.VMEM((ROWS, 128), f32),
            pltpu.VMEM((ROWS, 128), f32),
            pltpu.VMEM((ROWS, 128), f32),
            pltpu.VMEM((ROWS, 128), f32),
            pltpu.VMEM((8 * ROWS, 128), f32),
            pltpu.VMEM((6 * ROWS, 128), f32),
            pltpu.VMEM((12 * ROWS, 128), f32),
            pltpu.VMEM((13 * ROWS, 128), f32),
            pltpu.VMEM((BLOCKS, 128, 512), jnp.bfloat16),
            pltpu.VMEM((TILES, 80, 128), f32),
            pltpu.VMEM((16 * ROWS, 128), f32),
            pltpu.VMEM((3, 8, 128), f32),
            pltpu.VMEM((4, 8, 128), f32),
            pltpu.VMEM((4, 8, 128), f32),
            pltpu.VMEM((STEPS, 2, 4, 8, 128), f32),
            pltpu.VMEM((STEPS, 2, 8, 128), f32),
            pltpu.VMEM((STEPS, 2, 8, 128), f32),
            pltpu.VMEM((STEPS, 2, 4, 8, 128), f32),
            pltpu.VMEM((STEPS, 2, 8, 128), f32),
            pltpu.VMEM((STEPS, 2, 8, 128), f32),
            pltpu.VMEM((STEPS, 2, 8, 128), f32),
            pltpu.VMEM((STEPS, 2, 8, 128), f32),
            pltpu.SemaphoreType.DMA((7,)),
            pltpu.SemaphoreType.DMA((STEPS, 2, 8)),
            pltpu.SemaphoreType.DMA((STEPS, 2, 8)),
        ],
        compiler_params=pltpu.CompilerParams(
            collective_id=0, has_side_effects=True, vmem_limit_bytes=VMEM_BYTES
        ),
    )(
        *(
            pltpu.with_memory_space_constraint(value, pltpu.HBM)
            for value in (
                block_counts.reshape(BLOCKS),
                offsets.reshape(3, ROWS, 128),
                velocity.reshape(3, ROWS, 128),
                affine.reshape(9, ROWS, 128),
                strain.reshape(9, ROWS, 128),
                particle_mass.reshape(ROWS, 128),
                plastic_ratio.reshape(ROWS, 128),
            )
        ),
    )
    outs = pl.pallas_call(
        write_out,
        out_shape=[jax.ShapeDtypeStruct(out.shape, f32) for out in outs],
        in_specs=[vmem] * 4,
        out_specs=[hbm] * 4,
        scratch_shapes=[pltpu.SemaphoreType.DMA((4,))],
        compiler_params=pltpu.CompilerParams(vmem_limit_bytes=VMEM_BYTES),
    )(*outs)
    return tuple(out.reshape(out.shape[0], 1, 1, ROWS * 128) for out in outs)


def solution(mesh):
    wide = P(None, "slope", "cross", None)
    flat = P("slope", "cross", None)
    return jax.shard_map(
        per_device,
        mesh=mesh,
        in_specs=(wide, wide, wide, wide, flat, flat, flat),
        out_specs=(wide, wide, wide, wide),
        check_vma=False,
    )
```

```python
import functools

import jax
import jax.numpy as jnp
from jax import lax
from jax.experimental import pallas as pl
from jax.experimental.pallas import tpu as pltpu
from jax.sharding import PartitionSpec as P

STEPS = 5
BLOCKS = 8
ROWS = 32
CHUNKS = 4
TILES = 4
VMEM_BYTES = 40 * 1024 * 1024
MESH = pl.DeviceIdType.MESH

time_step = 0.02
shear_modulus = 4.0
lame_lambda = 4.0
hardening = 10.0
mass_floor = 0.25
gravity_slope = 1.5
gravity_vertical = -2.5
CENTRE = 2.5

DIRECTIONS = [(0, -1), (0, 1), (-1, -1), (-1, 1), (1, -1), (1, 1), (-1, 0), (1, 0)]


def iota(shape, dim):
    return lax.broadcasted_iota(jnp.int32, shape, dim)


def axis_weights(position):
    base = jnp.floor(position + 0.5)
    dist = position - base
    lower = 0.5 * (0.5 - dist) * (0.5 - dist)
    middle = 0.75 - dist * dist
    upper = 0.5 * (0.5 + dist) * (0.5 + dist)
    at = {e: base == float(e) for e in range(-1, 7)}
    return [
        jnp.where(at[e], middle, jnp.where(at[e + 1], lower, jnp.where(at[e - 1], upper, 0.0)))
        for e in range(6)
    ]


def split(values):
    high = values.astype(jnp.bfloat16)
    low = (values - high.astype(jnp.float32)).astype(jnp.bfloat16)
    return high, low


def kernel(
    nx, ny,
    counts_hbm, off_hbm, vel_hbm, aff_hbm, strain_hbm, mass_hbm, plastic_hbm,
    off, vel, aff, frame,
    counts, strain_in, mass_in, plastic_in, live_ref, mw_ref, hard_ref, wx, wy, wz, feats, bs, sides, us,
    gathered,
    send_x, send_low, send_high, recv_x, recv_low, recv_high, diag_low, diag_high,
    load_sem, send_sem, recv_sem,
):
    ix = lax.axis_index("slope")
    iy = lax.axis_index("cross")

    def neighbour(dx, dy):
        return ix + dx, iy + dy

    def present(dx, dy):
        ok = None
        for d, i, n in ((dx, ix, nx), (dy, iy, ny)):
            if d != 0:
                here = (i + d >= 0) & (i + d < n)
                ok = here if ok is None else ok & here
        return ok

    inside = (ix > 0) & (ix < nx - 1) & (iy > 0) & (iy < ny - 1)

    def each_neighbour(act):
        @pl.when(inside)
        def _():
            for d in range(8):
                act(d)

        @pl.when(jnp.logical_not(inside))
        def _():
            for d, (dx, dy) in enumerate(DIRECTIONS):

                @pl.when(present(dx, dy))
                def _():
                    act(d)

    loads = [
        pltpu.make_async_copy(source, target, load_sem.at[i])
        for i, (source, target) in enumerate((
            (counts_hbm, counts), (mass_hbm, mass_in), (plastic_hbm, plastic_in), (off_hbm, off),
            (vel_hbm, vel), (aff_hbm, aff), (strain_hbm, strain_in),
        ))
    ]
    for load in loads:
        load.start()

    for ref in (recv_x, recv_low, recv_high, diag_low, diag_high):
        ref[...] = jnp.zeros(ref.shape, ref.dtype)
    barrier = pltpu.get_barrier_semaphore()
    around = jnp.int32(0)
    for dx, dy in DIRECTIONS:
        ok = present(dx, dy)
        around = around + jnp.where(ok, 1, 0).astype(jnp.int32)

        @pl.when(ok)
        def _():
            pl.semaphore_signal(barrier, inc=1, device_id=neighbour(dx, dy), device_id_type=MESH)

    for ref in (wx, wz, us, bs, gathered):
        ref[...] = jnp.zeros(ref.shape, ref.dtype)
    for load in loads:
        load.wait()
    row = iota((ROWS, 128), 0)
    slot = (row % CHUNKS) * 128 + iota((ROWS, 128), 1)
    limit = jnp.zeros((ROWS, 128), jnp.int32)
    for k in range(BLOCKS):
        limit = jnp.where(row // CHUNKS == k, counts[k], limit)
    live = jnp.where(slot < limit, 1.0, 0.0).astype(jnp.float32)
    live_ref[...] = live
    mw_ref[...] = mass_in[...] * live
    hard_ref[...] = 4.0 * time_step * live * jnp.exp(hardening * (1.0 - plastic_in[...]))
    for i in range(9):
        frame[i] = strain_in[i] + (1.0 if i % 4 == 0 else 0.0)

    lane = iota((8, 128), 1)
    sub = iota((8, 128), 0)
    half = lane < 64
    r3 = lane % 8
    e2 = (lane % 64) // 8
    e3 = jnp.where(half, r3, (r3 + 4) % 8)
    ex = sub.astype(jnp.float32) - CENTRE
    ey = e2.astype(jnp.float32) - CENTRE
    ez = e3.astype(jnp.float32) - CENTRE
    own = half | (r3 >= 4)
    group = (lane % 64) // 16
    own_tile = half == (r3 >= 4)
    ez_even = r3.astype(jnp.float32) - CENTRE
    ez_odd = ((r3 + 4) % 8).astype(jnp.float32) - CENTRE
    zero = jnp.zeros((8, 128), jnp.float32)
    place_x = 4 * ix + sub
    place_y = 4 * iy + e2
    outside = (place_x >= 4 * nx) | (place_y >= 4 * ny)

    def copy_to(step, d):
        dx, dy = DIRECTIONS[d]
        back = DIRECTIONS.index((-dx, -dy))
        if dy == 0:
            source, target = send_x, recv_x
        elif dx == 0:
            source, target = (send_low, recv_high) if dy < 0 else (send_high, recv_low)
        else:
            source, target = (send_low, diag_high) if dy < 0 else (send_high, diag_low)
        if dx == 0:
            here, there = pl.ds(0, 6), pl.ds(0, 6)
        else:
            here, there = pl.ds(0 if dx < 0 else 4, 2), pl.ds(4 if dx < 0 else 0, 2)
        return pltpu.make_async_remote_copy(
            src_ref=source.at[step, :, here, :], dst_ref=target.at[step, :, there, :],
            send_sem=send_sem.at[step, d], recv_sem=recv_sem.at[step, back],
            device_id=neighbour(dx, dy), device_id_type=MESH,
        )

    def spread(ref, at):
        return jnp.broadcast_to(ref[pl.ds(at, 1), :], (8, 128))

    def terms(j, o, f, v, c):
        rows = pl.ds(8 * j, 8)
        det = (
            f[0] * (f[4] * f[8] - f[5] * f[7])
            - f[1] * (f[3] * f[8] - f[5] * f[6])
            + f[2] * (f[3] * f[7] - f[4] * f[6])
        )
        bulk = lame_lambda * (det - 1.0) * det
        mw = mw_ref[rows, :]
        hard = hard_ref[rows, :]
        terms_ = [[None] * 3 for _ in range(3)]
        for a in range(3):
            for b in range(a, 3):
                stretch = f[3 * a] * f[3 * b] + f[3 * a + 1] * f[3 * b + 1] + f[3 * a + 2] * f[3 * b + 2]
                if a == b:
                    tau = hard * (shear_modulus * (stretch - 1.0) + bulk)
                else:
                    tau = hard * (shear_modulus * stretch)
                terms_[a][b] = mw * c[3 * a + b] - tau
                if a != b:
                    terms_[b][a] = mw * c[3 * b + a] - tau
        feats[pl.ds(8 * j, 8), :] = mw
        for a in range(3):
            moved = (
                terms_[a][0] * (o[0] - CENTRE)
                + terms_[a][1] * (o[1] - CENTRE)
                + terms_[a][2] * (o[2] - CENTRE)
            )
            feats[pl.ds((1 + a) * ROWS + 8 * j, 8), :] = mw * v[a] - moved
            for b in range(3):
                feats[pl.ds((4 + 3 * b + a) * ROWS + 8 * j, 8), :] = terms_[a][b]
        for e, w in enumerate(axis_weights(o[0])):
            wx[pl.ds(e * ROWS + 8 * j, 8), :] = w
        for e, w in enumerate(axis_weights(o[1])):
            wy[pl.ds(e * ROWS + 8 * j, 8), :] = w
        for e, w in enumerate(axis_weights(o[2])):
            wz[pl.ds((4 + e) * ROWS + 8 * j, 8), :] = w
            if e >= 4:
                wz[pl.ds((e - 4) * ROWS + 8 * j, 8), :] = w

    def deposit(k):
        for c in range(CHUNKS):
            r = CHUNKS * k + c
            lanes = pl.ds(128 * c, 128)
            wxs = wx[pl.ds(r, 8, stride=ROWS), :]
            wzs = wz[pl.ds(r + (4 * ROWS if k % 2 == 0 else 0), 8, stride=ROWS), :]
            for e in (0, 2, 4):
                high, low = split(jnp.concatenate(
                    [spread(wy, e * ROWS + r) * wzs, spread(wy, (e + 1) * ROWS + r) * wzs], axis=0
                ))
                bs[k, pl.ds(8 * e, 16), lanes] = high
                bs[k, pl.ds(64 + 8 * e, 16), lanes] = low
            part = [spread(feats, i * ROWS + r) for i in range(13)]
            side = [part[0] * wxs]
            side += [(part[1 + a] + part[4 + a] * ex) * wxs for a in range(3)]
            side += [part[7 + i] * wxs for i in range(6)]
            for i in range(0, 10, 2):
                high, low = split(jnp.concatenate(side[i : i + 2], axis=0))
                sides[k, pl.ds(8 * i, 16), lanes] = high
                sides[k, pl.ds(80 + 8 * i, 16), lanes] = low
        dots = lax.dot_general(
            sides[k], bs[k], (((1,), (1,)), ((), ())), preferred_element_type=jnp.float32
        )
        return dots[:80] + dots[80:]

    def deposit_tile(j):
        even, odd = deposit(2 * j), deposit(2 * j + 1)
        pair = []
        for i in range(10):
            one, two = even[8 * i : 8 * i + 8], odd[8 * i : 8 * i + 8]
            pair.append(jnp.where(half, one, two) + pltpu.roll(jnp.where(half, two, one), 64, 1))
        return [pair[0]] + [pair[1 + a] + ey * pair[4 + a] + ez * pair[7 + a] for a in range(3)]

    def send(step, p, before, first, second):
        low, high = zero, zero
        for i in range(4):
            one = jnp.where(own, first[i], before[i])
            two = jnp.where(own, second[i], first[i])
            mine = jnp.where(half, one, two) + pltpu.roll(jnp.where(half, two, one), 64, 1)
            send_x[step, 4 * p + i] = mine
            to_low = mine if i == 0 else pltpu.roll(mine, 16 * i, 1)
            shift = (16 * i - 32) % 128
            to_high = mine if shift == 0 else pltpu.roll(mine, shift, 1)
            low = jnp.where(group == i, to_low, low)
            high = jnp.where(group == i, to_high, high)
        send_low[step, p] = low
        send_high[step, p] = high

    def grid_speed(step, p):
        below = recv_low[step, p] + diag_low[step, p]
        above = recv_high[step, p] + diag_high[step, p]
        total = []
        for i in range(4):
            from_low = below if i == 0 else pltpu.roll(below, 128 - 16 * i, 1)
            shift = (32 - 16 * i) % 128
            from_high = above if shift == 0 else pltpu.roll(above, shift, 1)
            extra = jnp.where(group == 0, from_low, jnp.where(group == 2, from_high, 0.0))
            total.append(send_x[step, 4 * p + i] + recv_x[step, 4 * p + i] + extra)
        scale = 1.0 / jnp.maximum(total[0], mass_floor)
        speed_x = total[1] * scale + time_step * gravity_slope
        speed_y = total[2] * scale
        speed_z = total[3] * scale + time_step * gravity_vertical
        place_z = 16 * p + jnp.where(half, 0, 8) + r3
        speed_x = jnp.where(place_x < 2, jnp.maximum(speed_x, 0.0), speed_x)
        speed_x = jnp.where(place_x >= 4 * nx - 2, jnp.minimum(speed_x, 0.0), speed_x)
        speed_y = jnp.where(place_y < 2, jnp.maximum(speed_y, 0.0), speed_y)
        speed_y = jnp.where(place_y >= 4 * ny - 2, jnp.minimum(speed_y, 0.0), speed_y)
        speed_z = jnp.where(place_z >= 8 * TILES - 2, jnp.minimum(speed_z, 0.0), speed_z)
        still = outside | (place_z < 2)
        return [jnp.where(still, 0.0, speed) for speed in (speed_x, speed_y, speed_z)]

    def windows(k, speed, turned, beyond, beyond_turned):
        for a in range(3):
            first, second = (speed[a], turned[a]) if k % 4 < 2 else (turned[a], speed[a])
            if k % 2 == 0:
                window = jnp.where(half, first, second)
            elif k % 4 == 1:
                window = jnp.where(own_tile, first, second)
            else:
                window = jnp.where(
                    r3 >= 4,
                    jnp.where(half, first, second),
                    jnp.where(half, beyond[a], beyond_turned[a]),
                )
            for b, factor in enumerate((None, ex, ey, ez_odd if k % 2 else ez_even)):
                q = 3 * b + a
                value = window if factor is None else window * factor
                if q < 8:
                    us[k, pl.ds(q, 8, stride=8), :] = value
                else:
                    us[k, pl.ds(64 + q - 8, 8, stride=4), :] = value

    def gather(k):
        left = jnp.concatenate(
            split(jnp.concatenate([us[k, 0:48, :], us[k, 64:96, :]], axis=0)), axis=1
        )
        planes = bs[k]
        taken = lax.dot_general(
            left, jnp.concatenate([planes, planes], axis=0),
            (((1,), (0,)), ((), ())), preferred_element_type=jnp.float32,
        )
        for c in range(CHUNKS):
            r = CHUNKS * k + c
            part = taken[:, 128 * c : 128 * c + 128]
            weights = [spread(wx, e * ROWS + r) for e in range(6)]
            first = weights[0] * part[0:8]
            for e in range(1, 6):
                first = first + weights[e] * part[8 * e : 8 * e + 8]
            second = jnp.where(sub < 4, weights[0], weights[1]) * part[48:56]
            for e in (2, 4):
                at = 48 + 4 * e
                second = second + jnp.where(sub < 4, weights[e], weights[e + 1]) * part[at : at + 8]
            gathered[pl.ds(16 * r, 8), :] = first
            gathered[pl.ds(16 * r + 8, 8), :] = second

    def advance(j):
        rows = pl.ds(8 * j, 8)

        def quantity(q):
            value = gathered[pl.ds(128 * j + q, 8, stride=16), :]
            if q >= 8:
                value = value + gathered[pl.ds(128 * j + q + 4, 8, stride=16), :]
            return value

        o = [off[i, rows, :] for i in range(3)]
        f = [frame[i, rows, :] for i in range(9)]
        v = [quantity(a) for a in range(3)]
        c = [None] * 9
        for a in range(3):
            for b in range(3):
                c[3 * a + b] = 4.0 * (quantity(3 + 3 * b + a) - v[a] * (o[b] - CENTRE))
        o = [o[a] + time_step * v[a] for a in range(3)]
        f = [
            f[3 * a + b]
            + time_step * (c[3 * a] * f[b] + c[3 * a + 1] * f[3 + b] + c[3 * a + 2] * f[6 + b])
            for a in range(3)
            for b in range(3)
        ]
        for ref, values in ((off, o), (vel, v), (aff, c), (frame, f)):
            for i, value in enumerate(values):
                ref[i, rows, :] = value
        return o, f, v, c

    def turn(values):
        return [pltpu.roll(value, 64, 1) for value in values]

    def one_step(step, carry):
        fields = [deposit_tile(j) for j in range(TILES)]
        send(step, 0, [zero] * 4, fields[0], fields[1])
        send(step, 1, fields[1], fields[2], fields[3])

        @pl.when(step == 0)
        def _():
            pl.semaphore_wait(barrier, around)

        each_neighbour(lambda d: copy_to(step, d).start())

        def wait(d):
            dx, dy = DIRECTIONS[d]
            copy_to(step, DIRECTIONS.index((-dx, -dy))).wait_recv()

        each_neighbour(wait)
        speed = [grid_speed(step, p) for p in range(2)] + [[zero] * 3]
        turned = [turn(speed[0]), turn(speed[1]), [zero] * 3]
        for k in range(BLOCKS):
            p = k // 4
            windows(k, speed[p], turned[p], speed[p + 1], turned[p + 1])
        for k in range(BLOCKS):
            gather(k)
        for j in range(TILES):
            terms(j, *advance(j))
        return carry

    for j in range(TILES):
        rows = pl.ds(8 * j, 8)
        terms(j, *([ref[i, rows, :] for i in range(n)] for ref, n in ((off, 3), (frame, 9), (vel, 3), (aff, 9))))
    lax.fori_loop(0, STEPS, one_step, 0)

    def finish(step, carry):
        each_neighbour(lambda d: copy_to(step, d).wait_send())
        return carry

    lax.fori_loop(0, STEPS, finish, 0)
    live = live_ref[...]
    for ref, count in ((off, 3), (vel, 3), (aff, 9), (frame, 9)):
        for i in range(count):
            ref[i] = ref[i] * live


def write_out(off, vel, aff, frame, off_out, vel_out, aff_out, frame_out, sem):
    copies = [
        pltpu.make_async_copy(source, target, sem.at[i])
        for i, (source, target) in enumerate(
            ((aff, aff_out), (frame, frame_out), (off, off_out), (vel, vel_out))
        )
    ]
    for copy in copies:
        copy.start()
    for copy in copies:
        copy.wait()


def per_device(offsets, velocity, affine, strain, particle_mass, plastic_ratio, block_counts):
    nx, ny = lax.axis_size("slope"), lax.axis_size("cross")
    f32 = jnp.float32
    vmem = pl.BlockSpec(memory_space=pltpu.VMEM)
    hbm = pl.BlockSpec(memory_space=pltpu.HBM)
    outs = pl.pallas_call(
        functools.partial(kernel, nx, ny),
        out_shape=[jax.ShapeDtypeStruct((n, ROWS, 128), f32) for n in (3, 3, 9, 9)],
        in_specs=[hbm] * 7,
        out_specs=[vmem] * 4,
        scratch_shapes=[
            pltpu.SMEM((BLOCKS,), jnp.int32),
            pltpu.VMEM((9, ROWS, 128), f32),
            pltpu.VMEM((ROWS, 128), f32),
            pltpu.VMEM((ROWS, 128), f32),
            pltpu.VMEM((ROWS, 128), f32),
            pltpu.VMEM((ROWS, 128), f32),
            pltpu.VMEM((ROWS, 128), f32),
            pltpu.VMEM((8 * ROWS, 128), f32),
            pltpu.VMEM((6 * ROWS, 128), f32),
            pltpu.VMEM((12 * ROWS, 128), f32),
            pltpu.VMEM((13 * ROWS, 128), f32),
            pltpu.VMEM((BLOCKS, 128, 512), jnp.bfloat16),
            pltpu.VMEM((BLOCKS, 160, 512), jnp.bfloat16),
            pltpu.VMEM((BLOCKS, 96, 128), f32),
            pltpu.VMEM((16 * ROWS, 128), f32),
            pltpu.VMEM((STEPS, 8, 8, 128), f32),
            pltpu.VMEM((STEPS, 2, 8, 128), f32),
            pltpu.VMEM((STEPS, 2, 8, 128), f32),
            pltpu.VMEM((STEPS, 8, 8, 128), f32),
            pltpu.VMEM((STEPS, 2, 8, 128), f32),
            pltpu.VMEM((STEPS, 2, 8, 128), f32),
            pltpu.VMEM((STEPS, 2, 8, 128), f32),
            pltpu.VMEM((STEPS, 2, 8, 128), f32),
            pltpu.SemaphoreType.DMA((7,)),
            pltpu.SemaphoreType.DMA((STEPS, 8)),
            pltpu.SemaphoreType.DMA((STEPS, 8)),
        ],
        compiler_params=pltpu.CompilerParams(
            collective_id=0, has_side_effects=True, vmem_limit_bytes=VMEM_BYTES
        ),
    )(
        *(
            pltpu.with_memory_space_constraint(value, pltpu.HBM)
            for value in (
                block_counts.reshape(BLOCKS),
                offsets.reshape(3, ROWS, 128),
                velocity.reshape(3, ROWS, 128),
                affine.reshape(9, ROWS, 128),
                strain.reshape(9, ROWS, 128),
                particle_mass.reshape(ROWS, 128),
                plastic_ratio.reshape(ROWS, 128),
            )
        ),
    )
    outs = pl.pallas_call(
        write_out,
        out_shape=[jax.ShapeDtypeStruct(out.shape, f32) for out in outs],
        in_specs=[vmem] * 4,
        out_specs=[hbm] * 4,
        scratch_shapes=[pltpu.SemaphoreType.DMA((4,))],
        compiler_params=pltpu.CompilerParams(vmem_limit_bytes=VMEM_BYTES),
    )(*outs)
    return tuple(out.reshape(out.shape[0], 1, 1, ROWS * 128) for out in outs)


def solution(mesh):
    wide = P(None, "slope", "cross", None)
    flat = P("slope", "cross", None)
    return jax.shard_map(
        per_device,
        mesh=mesh,
        in_specs=(wide, wide, wide, wide, flat, flat, flat),
        out_specs=(wide, wide, wide, wide),
        check_vma=False,
    )
```

```python
import functools

import jax
import jax.numpy as jnp
from jax import lax
from jax.experimental import pallas as pl
from jax.experimental.pallas import tpu as pltpu
from jax.sharding import PartitionSpec as P

STEPS = 5
BLOCKS = 8
ROWS = 32
CHUNKS = 4
TILES = 4
VMEM_BYTES = 40 * 1024 * 1024
MESH = pl.DeviceIdType.MESH

time_step = 0.02
shear_modulus = 4.0
lame_lambda = 4.0
hardening = 10.0
mass_floor = 0.25
gravity_slope = 1.5
gravity_vertical = -2.5
CENTRE = 2.5

DIRECTIONS = [(0, -1), (0, 1), (-1, -1), (-1, 1), (1, -1), (1, 1), (-1, 0), (1, 0)]


def iota(shape, dim):
    return lax.broadcasted_iota(jnp.int32, shape, dim)


def axis_weights(position):
    base = jnp.floor(position + 0.5)
    dist = position - base
    lower = 0.5 * (0.5 - dist) * (0.5 - dist)
    middle = 0.75 - dist * dist
    upper = 0.5 * (0.5 + dist) * (0.5 + dist)
    at = {e: base == float(e) for e in range(-1, 7)}
    return [
        jnp.where(at[e], middle, jnp.where(at[e + 1], lower, jnp.where(at[e - 1], upper, 0.0)))
        for e in range(6)
    ]


def split(values):
    high = values.astype(jnp.bfloat16)
    low = (values - high.astype(jnp.float32)).astype(jnp.bfloat16)
    return high, low


def kernel(
    nx, ny,
    counts_hbm, off_hbm, vel_hbm, aff_hbm, strain_hbm, mass_hbm, plastic_hbm,
    off, vel, aff, frame,
    counts, strain_in, mass_in, plastic_in, live_ref, mw_ref, hard_ref, wx, wy, wz, feats, bs, sides, us,
    gathered,
    send_x, send_low, send_high, recv_x, recv_low, recv_high, diag_low, diag_high,
    load_sem, send_sem, recv_sem,
):
    ix = lax.axis_index("slope")
    iy = lax.axis_index("cross")

    def neighbour(dx, dy):
        return ix + dx, iy + dy

    def present(dx, dy):
        ok = None
        for d, i, n in ((dx, ix, nx), (dy, iy, ny)):
            if d != 0:
                here = (i + d >= 0) & (i + d < n)
                ok = here if ok is None else ok & here
        return ok

    inside = (ix > 0) & (ix < nx - 1) & (iy > 0) & (iy < ny - 1)

    def each_neighbour(act):
        @pl.when(inside)
        def _():
            for d in range(8):
                act(d)

        @pl.when(jnp.logical_not(inside))
        def _():
            for d, (dx, dy) in enumerate(DIRECTIONS):

                @pl.when(present(dx, dy))
                def _():
                    act(d)

    loads = [
        pltpu.make_async_copy(source, target, load_sem.at[i])
        for i, (source, target) in enumerate((
            (counts_hbm, counts), (mass_hbm, mass_in), (plastic_hbm, plastic_in), (off_hbm, off),
            (vel_hbm, vel), (aff_hbm, aff), (strain_hbm, strain_in),
        ))
    ]
    for load in loads:
        load.start()

    for ref in (recv_x, recv_low, recv_high, diag_low, diag_high):
        ref[...] = jnp.zeros(ref.shape, ref.dtype)
    barrier = pltpu.get_barrier_semaphore()
    around = jnp.int32(0)
    for dx, dy in DIRECTIONS:
        ok = present(dx, dy)
        around = around + jnp.where(ok, 1, 0).astype(jnp.int32)

        @pl.when(ok)
        def _():
            pl.semaphore_signal(barrier, inc=1, device_id=neighbour(dx, dy), device_id_type=MESH)

    for ref in (wx, wz, us, bs, gathered):
        ref[...] = jnp.zeros(ref.shape, ref.dtype)
    for load in loads:
        load.wait()
    row = iota((ROWS, 128), 0)
    slot = (row % CHUNKS) * 128 + iota((ROWS, 128), 1)
    limit = jnp.zeros((ROWS, 128), jnp.int32)
    for k in range(BLOCKS):
        limit = jnp.where(row // CHUNKS == k, counts[k], limit)
    live = jnp.where(slot < limit, 1.0, 0.0).astype(jnp.float32)
    live_ref[...] = live
    mw_ref[...] = mass_in[...] * live
    hard_ref[...] = 4.0 * time_step * live * jnp.exp(hardening * (1.0 - plastic_in[...]))
    for i in range(9):
        frame[i] = strain_in[i] + (1.0 if i % 4 == 0 else 0.0)

    lane = iota((8, 128), 1)
    sub = iota((8, 128), 0)
    half = lane < 64
    r3 = lane % 8
    e2 = (lane % 64) // 8
    e3 = jnp.where(half, r3, (r3 + 4) % 8)
    ex = sub.astype(jnp.float32) - CENTRE
    ey = e2.astype(jnp.float32) - CENTRE
    ez = e3.astype(jnp.float32) - CENTRE
    own = half | (r3 >= 4)
    group = (lane % 64) // 16
    own_tile = half == (r3 >= 4)
    ez_even = r3.astype(jnp.float32) - CENTRE
    ez_odd = ((r3 + 4) % 8).astype(jnp.float32) - CENTRE
    zero = jnp.zeros((8, 128), jnp.float32)
    place_x = 4 * ix + sub
    place_y = 4 * iy + e2
    outside = (place_x >= 4 * nx) | (place_y >= 4 * ny)

    def copy_to(step, d):
        dx, dy = DIRECTIONS[d]
        back = DIRECTIONS.index((-dx, -dy))
        if dy == 0:
            source, target = send_x, recv_x
        elif dx == 0:
            source, target = (send_low, recv_high) if dy < 0 else (send_high, recv_low)
        else:
            source, target = (send_low, diag_high) if dy < 0 else (send_high, diag_low)
        if dx == 0:
            here, there = pl.ds(0, 6), pl.ds(0, 6)
        else:
            here, there = pl.ds(0 if dx < 0 else 4, 2), pl.ds(4 if dx < 0 else 0, 2)
        return pltpu.make_async_remote_copy(
            src_ref=source.at[step, :, here, :], dst_ref=target.at[step, :, there, :],
            send_sem=send_sem.at[step, d], recv_sem=recv_sem.at[step, back],
            device_id=neighbour(dx, dy), device_id_type=MESH,
        )

    def spread(ref, at):
        return jnp.broadcast_to(ref[pl.ds(at, 1), :], (8, 128))

    def terms(j, o, f, v, c):
        rows = pl.ds(8 * j, 8)
        det = (
            f[0] * (f[4] * f[8] - f[5] * f[7])
            - f[1] * (f[3] * f[8] - f[5] * f[6])
            + f[2] * (f[3] * f[7] - f[4] * f[6])
        )
        bulk = lame_lambda * (det - 1.0) * det
        mw = mw_ref[rows, :]
        hard = hard_ref[rows, :]
        terms_ = [[None] * 3 for _ in range(3)]
        for a in range(3):
            for b in range(a, 3):
                stretch = f[3 * a] * f[3 * b] + f[3 * a + 1] * f[3 * b + 1] + f[3 * a + 2] * f[3 * b + 2]
                if a == b:
                    tau = hard * (shear_modulus * (stretch - 1.0) + bulk)
                else:
                    tau = hard * (shear_modulus * stretch)
                terms_[a][b] = mw * c[3 * a + b] - tau
                if a != b:
                    terms_[b][a] = mw * c[3 * b + a] - tau
        feats[pl.ds(8 * j, 8), :] = mw
        for a in range(3):
            moved = (
                terms_[a][0] * (o[0] - CENTRE)
                + terms_[a][1] * (o[1] - CENTRE)
                + terms_[a][2] * (o[2] - CENTRE)
            )
            feats[pl.ds((1 + a) * ROWS + 8 * j, 8), :] = mw * v[a] - moved
            for b in range(3):
                feats[pl.ds((4 + 3 * b + a) * ROWS + 8 * j, 8), :] = terms_[a][b]
        for e, w in enumerate(axis_weights(o[0])):
            wx[pl.ds(e * ROWS + 8 * j, 8), :] = w
        for e, w in enumerate(axis_weights(o[1])):
            wy[pl.ds(e * ROWS + 8 * j, 8), :] = w
        for e, w in enumerate(axis_weights(o[2])):
            wz[pl.ds((4 + e) * ROWS + 8 * j, 8), :] = w
            if e >= 4:
                wz[pl.ds((e - 4) * ROWS + 8 * j, 8), :] = w

    def deposit(k):
        for c in range(CHUNKS):
            r = CHUNKS * k + c
            lanes = pl.ds(128 * c, 128)
            wxs = wx[pl.ds(r, 8, stride=ROWS), :]
            wzs = wz[pl.ds(r + (4 * ROWS if k % 2 == 0 else 0), 8, stride=ROWS), :]
            for e in (0, 2, 4):
                high, low = split(jnp.concatenate(
                    [spread(wy, e * ROWS + r) * wzs, spread(wy, (e + 1) * ROWS + r) * wzs], axis=0
                ))
                bs[k, pl.ds(8 * e, 16), lanes] = high
                bs[k, pl.ds(64 + 8 * e, 16), lanes] = low
            part = [spread(feats, i * ROWS + r) for i in range(13)]
            side = [part[0] * wxs]
            side += [(part[1 + a] + part[4 + a] * ex) * wxs for a in range(3)]
            side += [part[7 + i] * wxs for i in range(6)]
            for i in range(0, 10, 2):
                high, low = split(jnp.concatenate(side[i : i + 2], axis=0))
                sides[k, pl.ds(8 * i, 16), lanes] = high
                sides[k, pl.ds(80 + 8 * i, 16), lanes] = low
        dots = lax.dot_general(
            sides[k], bs[k], (((1,), (1,)), ((), ())), preferred_element_type=jnp.float32
        )
        return dots[:80] + dots[80:]

    def deposit_tile(j):
        even, odd = deposit(2 * j), deposit(2 * j + 1)
        pair = []
        for i in range(10):
            one, two = even[8 * i : 8 * i + 8], odd[8 * i : 8 * i + 8]
            pair.append(jnp.where(half, one, two) + pltpu.roll(jnp.where(half, two, one), 64, 1))
        return [pair[0]] + [pair[1 + a] + ey * pair[4 + a] + ez * pair[7 + a] for a in range(3)]

    def send(step, p, before, first, second):
        low, high = zero, zero
        for i in range(4):
            one = jnp.where(own, first[i], before[i])
            two = jnp.where(own, second[i], first[i])
            mine = jnp.where(half, one, two) + pltpu.roll(jnp.where(half, two, one), 64, 1)
            send_x[step, 4 * p + i] = mine
            to_low = mine if i == 0 else pltpu.roll(mine, 16 * i, 1)
            shift = (16 * i - 32) % 128
            to_high = mine if shift == 0 else pltpu.roll(mine, shift, 1)
            low = jnp.where(group == i, to_low, low)
            high = jnp.where(group == i, to_high, high)
        send_low[step, p] = low
        send_high[step, p] = high

    def grid_speed(step, p):
        below = recv_low[step, p] + diag_low[step, p]
        above = recv_high[step, p] + diag_high[step, p]
        total = []
        for i in range(4):
            from_low = below if i == 0 else pltpu.roll(below, 128 - 16 * i, 1)
            shift = (32 - 16 * i) % 128
            from_high = above if shift == 0 else pltpu.roll(above, shift, 1)
            extra = jnp.where(group == 0, from_low, jnp.where(group == 2, from_high, 0.0))
            total.append(send_x[step, 4 * p + i] + recv_x[step, 4 * p + i] + extra)
        scale = 1.0 / jnp.maximum(total[0], mass_floor)
        speed_x = total[1] * scale + time_step * gravity_slope
        speed_y = total[2] * scale
        speed_z = total[3] * scale + time_step * gravity_vertical
        place_z = 16 * p + jnp.where(half, 0, 8) + r3
        speed_x = jnp.where(place_x < 2, jnp.maximum(speed_x, 0.0), speed_x)
        speed_x = jnp.where(place_x >= 4 * nx - 2, jnp.minimum(speed_x, 0.0), speed_x)
        speed_y = jnp.where(place_y < 2, jnp.maximum(speed_y, 0.0), speed_y)
        speed_y = jnp.where(place_y >= 4 * ny - 2, jnp.minimum(speed_y, 0.0), speed_y)
        speed_z = jnp.where(place_z >= 8 * TILES - 2, jnp.minimum(speed_z, 0.0), speed_z)
        still = outside | (place_z < 2)
        return [jnp.where(still, 0.0, speed) for speed in (speed_x, speed_y, speed_z)]

    def windows(k, speed, turned, beyond, beyond_turned):
        for a in range(3):
            first, second = (speed[a], turned[a]) if k % 4 < 2 else (turned[a], speed[a])
            if k % 2 == 0:
                window = jnp.where(half, first, second)
            elif k % 4 == 1:
                window = jnp.where(own_tile, first, second)
            else:
                window = jnp.where(
                    r3 >= 4,
                    jnp.where(half, first, second),
                    jnp.where(half, beyond[a], beyond_turned[a]),
                )
            for b, factor in enumerate((None, ex, ey, ez_odd if k % 2 else ez_even)):
                q = 3 * b + a
                value = window if factor is None else window * factor
                if q < 8:
                    us[k, pl.ds(q, 8, stride=8), :] = value
                else:
                    us[k, pl.ds(64 + q - 8, 8, stride=4), :] = value

    def gather(k):
        left = jnp.concatenate(
            split(jnp.concatenate([us[k, 0:48, :], us[k, 64:96, :]], axis=0)), axis=0
        )
        taken = lax.dot_general(
            left, bs[k], (((1,), (0,)), ((), ())), preferred_element_type=jnp.float32
        )
        taken = taken[:80] + taken[80:]
        for c in range(CHUNKS):
            r = CHUNKS * k + c
            part = taken[:, 128 * c : 128 * c + 128]
            weights = [spread(wx, e * ROWS + r) for e in range(6)]
            first = weights[0] * part[0:8]
            for e in range(1, 6):
                first = first + weights[e] * part[8 * e : 8 * e + 8]
            second = jnp.where(sub < 4, weights[0], weights[1]) * part[48:56]
            for e in (2, 4):
                at = 48 + 4 * e
                second = second + jnp.where(sub < 4, weights[e], weights[e + 1]) * part[at : at + 8]
            gathered[pl.ds(16 * r, 8), :] = first
            gathered[pl.ds(16 * r + 8, 8), :] = second

    def advance(j):
        rows = pl.ds(8 * j, 8)

        def quantity(q):
            value = gathered[pl.ds(128 * j + q, 8, stride=16), :]
            if q >= 8:
                value = value + gathered[pl.ds(128 * j + q + 4, 8, stride=16), :]
            return value

        o = [off[i, rows, :] for i in range(3)]
        f = [frame[i, rows, :] for i in range(9)]
        v = [quantity(a) for a in range(3)]
        c = [None] * 9
        for a in range(3):
            for b in range(3):
                c[3 * a + b] = 4.0 * (quantity(3 + 3 * b + a) - v[a] * (o[b] - CENTRE))
        o = [o[a] + time_step * v[a] for a in range(3)]
        f = [
            f[3 * a + b]
            + time_step * (c[3 * a] * f[b] + c[3 * a + 1] * f[3 + b] + c[3 * a + 2] * f[6 + b])
            for a in range(3)
            for b in range(3)
        ]
        for ref, values in ((off, o), (vel, v), (aff, c), (frame, f)):
            for i, value in enumerate(values):
                ref[i, rows, :] = value
        return o, f, v, c

    def turn(values):
        return [pltpu.roll(value, 64, 1) for value in values]

    def one_step(step, carry):
        for j in range(TILES):
            rows = pl.ds(8 * j, 8)
            terms(j, *([ref[i, rows, :] for i in range(n)] for ref, n in ((off, 3), (frame, 9), (vel, 3), (aff, 9))))
        fields = [deposit_tile(j) for j in range(TILES)]
        send(step, 0, [zero] * 4, fields[0], fields[1])
        send(step, 1, fields[1], fields[2], fields[3])

        @pl.when(step == 0)
        def _():
            pl.semaphore_wait(barrier, around)

        each_neighbour(lambda d: copy_to(step, d).start())

        def wait(d):
            dx, dy = DIRECTIONS[d]
            copy_to(step, DIRECTIONS.index((-dx, -dy))).wait_recv()

        each_neighbour(wait)
        speed = [grid_speed(step, p) for p in range(2)] + [[zero] * 3]
        turned = [turn(speed[0]), turn(speed[1]), [zero] * 3]
        for k in range(BLOCKS):
            p = k // 4
            windows(k, speed[p], turned[p], speed[p + 1], turned[p + 1])
        for k in range(BLOCKS):
            gather(k)
        for j in range(TILES):
            advance(j)
        return carry

    lax.fori_loop(0, STEPS, one_step, 0)

    def finish(step, carry):
        each_neighbour(lambda d: copy_to(step, d).wait_send())
        return carry

    lax.fori_loop(0, STEPS, finish, 0)
    live = live_ref[...]
    for ref, count in ((off, 3), (vel, 3), (aff, 9), (frame, 9)):
        for i in range(count):
            ref[i] = ref[i] * live


def write_out(off, vel, aff, frame, off_out, vel_out, aff_out, frame_out, sem):
    copies = [
        pltpu.make_async_copy(source, target, sem.at[i])
        for i, (source, target) in enumerate(
            ((aff, aff_out), (frame, frame_out), (off, off_out), (vel, vel_out))
        )
    ]
    for copy in copies:
        copy.start()
    for copy in copies:
        copy.wait()


def per_device(offsets, velocity, affine, strain, particle_mass, plastic_ratio, block_counts):
    nx, ny = lax.axis_size("slope"), lax.axis_size("cross")
    f32 = jnp.float32
    vmem = pl.BlockSpec(memory_space=pltpu.VMEM)
    hbm = pl.BlockSpec(memory_space=pltpu.HBM)
    outs = pl.pallas_call(
        functools.partial(kernel, nx, ny),
        out_shape=[jax.ShapeDtypeStruct((n, ROWS, 128), f32) for n in (3, 3, 9, 9)],
        in_specs=[hbm] * 7,
        out_specs=[vmem] * 4,
        scratch_shapes=[
            pltpu.SMEM((BLOCKS,), jnp.int32),
            pltpu.VMEM((9, ROWS, 128), f32),
            pltpu.VMEM((ROWS, 128), f32),
            pltpu.VMEM((ROWS, 128), f32),
            pltpu.VMEM((ROWS, 128), f32),
            pltpu.VMEM((ROWS, 128), f32),
            pltpu.VMEM((ROWS, 128), f32),
            pltpu.VMEM((8 * ROWS, 128), f32),
            pltpu.VMEM((6 * ROWS, 128), f32),
            pltpu.VMEM((12 * ROWS, 128), f32),
            pltpu.VMEM((13 * ROWS, 128), f32),
            pltpu.VMEM((BLOCKS, 128, 512), jnp.bfloat16),
            pltpu.VMEM((BLOCKS, 160, 512), jnp.bfloat16),
            pltpu.VMEM((BLOCKS, 96, 128), f32),
            pltpu.VMEM((16 * ROWS, 128), f32),
            pltpu.VMEM((STEPS, 8, 8, 128), f32),
            pltpu.VMEM((STEPS, 2, 8, 128), f32),
            pltpu.VMEM((STEPS, 2, 8, 128), f32),
            pltpu.VMEM((STEPS, 8, 8, 128), f32),
            pltpu.VMEM((STEPS, 2, 8, 128), f32),
            pltpu.VMEM((STEPS, 2, 8, 128), f32),
            pltpu.VMEM((STEPS, 2, 8, 128), f32),
            pltpu.VMEM((STEPS, 2, 8, 128), f32),
            pltpu.SemaphoreType.DMA((7,)),
            pltpu.SemaphoreType.DMA((STEPS, 8)),
            pltpu.SemaphoreType.DMA((STEPS, 8)),
        ],
        compiler_params=pltpu.CompilerParams(
            collective_id=0, has_side_effects=True, vmem_limit_bytes=VMEM_BYTES
        ),
    )(
        *(
            pltpu.with_memory_space_constraint(value, pltpu.HBM)
            for value in (
                block_counts.reshape(BLOCKS),
                offsets.reshape(3, ROWS, 128),
                velocity.reshape(3, ROWS, 128),
                affine.reshape(9, ROWS, 128),
                strain.reshape(9, ROWS, 128),
                particle_mass.reshape(ROWS, 128),
                plastic_ratio.reshape(ROWS, 128),
            )
        ),
    )
    outs = pl.pallas_call(
        write_out,
        out_shape=[jax.ShapeDtypeStruct(out.shape, f32) for out in outs],
        in_specs=[vmem] * 4,
        out_specs=[hbm] * 4,
        scratch_shapes=[pltpu.SemaphoreType.DMA((4,))],
        compiler_params=pltpu.CompilerParams(vmem_limit_bytes=VMEM_BYTES),
    )(*outs)
    return tuple(out.reshape(out.shape[0], 1, 1, ROWS * 128) for out in outs)


def solution(mesh):
    wide = P(None, "slope", "cross", None)
    flat = P("slope", "cross", None)
    return jax.shard_map(
        per_device,
        mesh=mesh,
        in_specs=(wide, wide, wide, wide, flat, flat, flat),
        out_specs=(wide, wide, wide, wide),
        check_vma=False,
    )
```

```python
import functools

import jax
import jax.numpy as jnp
from jax import lax
from jax.experimental import pallas as pl
from jax.experimental.pallas import tpu as pltpu
from jax.sharding import PartitionSpec as P

STEPS = 5
BLOCKS = 8
ROWS = 32
CHUNKS = 4
TILES = 4
VMEM_BYTES = 40 * 1024 * 1024
MESH = pl.DeviceIdType.MESH

time_step = 0.02
shear_modulus = 4.0
lame_lambda = 4.0
hardening = 10.0
mass_floor = 0.25
gravity_slope = 1.5
gravity_vertical = -2.5
CENTRE = 2.5

DIRECTIONS = [(0, -1), (0, 1), (-1, -1), (-1, 1), (1, -1), (1, 1), (-1, 0), (1, 0)]


def iota(shape, dim):
    return lax.broadcasted_iota(jnp.int32, shape, dim)


def axis_weights(position):
    base = jnp.floor(position + 0.5)
    dist = position - base
    lower = 0.5 * (0.5 - dist) * (0.5 - dist)
    middle = 0.75 - dist * dist
    upper = 0.5 * (0.5 + dist) * (0.5 + dist)
    at = {e: base == float(e) for e in range(-1, 7)}
    return [
        jnp.where(at[e], middle, jnp.where(at[e + 1], lower, jnp.where(at[e - 1], upper, 0.0)))
        for e in range(6)
    ]


def split(values):
    high = values.astype(jnp.bfloat16)
    low = (values - high.astype(jnp.float32)).astype(jnp.bfloat16)
    return high, low


def kernel(
    nx, ny,
    counts_hbm, off_hbm, vel_hbm, aff_hbm, strain_hbm, mass_hbm, plastic_hbm,
    off, vel, aff, frame,
    counts, strain_in, mass_in, plastic_in, live_ref, mw_ref, hard_ref, wx, wy, wz, feats, bs, sides, us,
    gathered,
    send_x, send_low, send_high, recv_x, recv_low, recv_high, diag_low, diag_high,
    load_sem, send_sem, recv_sem,
):
    ix = lax.axis_index("slope")
    iy = lax.axis_index("cross")

    def neighbour(dx, dy):
        return ix + dx, iy + dy

    def present(dx, dy):
        ok = None
        for d, i, n in ((dx, ix, nx), (dy, iy, ny)):
            if d != 0:
                here = (i + d >= 0) & (i + d < n)
                ok = here if ok is None else ok & here
        return ok

    inside = (ix > 0) & (ix < nx - 1) & (iy > 0) & (iy < ny - 1)

    def each_neighbour(act):
        @pl.when(inside)
        def _():
            for d in range(8):
                act(d)

        @pl.when(jnp.logical_not(inside))
        def _():
            for d, (dx, dy) in enumerate(DIRECTIONS):

                @pl.when(present(dx, dy))
                def _():
                    act(d)

    loads = [
        pltpu.make_async_copy(source, target, load_sem.at[i])
        for i, (source, target) in enumerate((
            (counts_hbm, counts), (mass_hbm, mass_in), (plastic_hbm, plastic_in), (off_hbm, off),
            (vel_hbm, vel), (aff_hbm, aff), (strain_hbm, strain_in),
        ))
    ]
    for load in loads:
        load.start()

    for ref in (recv_x, recv_low, recv_high, diag_low, diag_high):
        ref[...] = jnp.zeros(ref.shape, ref.dtype)
    barrier = pltpu.get_barrier_semaphore()
    around = jnp.int32(0)
    for dx, dy in DIRECTIONS:
        ok = present(dx, dy)
        around = around + jnp.where(ok, 1, 0).astype(jnp.int32)

        @pl.when(ok)
        def _():
            pl.semaphore_signal(barrier, inc=1, device_id=neighbour(dx, dy), device_id_type=MESH)

    for ref in (wx, wz, us, bs, gathered):
        ref[...] = jnp.zeros(ref.shape, ref.dtype)
    for load in loads:
        load.wait()
    row = iota((ROWS, 128), 0)
    slot = (row % CHUNKS) * 128 + iota((ROWS, 128), 1)
    limit = jnp.zeros((ROWS, 128), jnp.int32)
    for k in range(BLOCKS):
        limit = jnp.where(row // CHUNKS == k, counts[k], limit)
    live = jnp.where(slot < limit, 1.0, 0.0).astype(jnp.float32)
    live_ref[...] = live
    mw_ref[...] = mass_in[...] * live
    hard_ref[...] = 4.0 * time_step * live * jnp.exp(hardening * (1.0 - plastic_in[...]))
    for i in range(9):
        frame[i] = strain_in[i] + (1.0 if i % 4 == 0 else 0.0)

    lane = iota((8, 128), 1)
    sub = iota((8, 128), 0)
    half = lane < 64
    r3 = lane % 8
    e2 = (lane % 64) // 8
    e3 = jnp.where(half, r3, (r3 + 4) % 8)
    ex = sub.astype(jnp.float32) - CENTRE
    ey = e2.astype(jnp.float32) - CENTRE
    ez = e3.astype(jnp.float32) - CENTRE
    own = half | (r3 >= 4)
    group = (lane % 64) // 16
    own_tile = half == (r3 >= 4)
    ez_even = r3.astype(jnp.float32) - CENTRE
    ez_odd = ((r3 + 4) % 8).astype(jnp.float32) - CENTRE
    zero = jnp.zeros((8, 128), jnp.float32)
    place_x = 4 * ix + sub
    place_y = 4 * iy + e2
    outside = (place_x >= 4 * nx) | (place_y >= 4 * ny)

    def copy_to(step, p, d):
        dx, dy = DIRECTIONS[d]
        back = DIRECTIONS.index((-dx, -dy))
        if dy == 0:
            source, target = send_x, recv_x
        elif dx == 0:
            source, target = (send_low, recv_high) if dy < 0 else (send_high, recv_low)
        else:
            source, target = (send_low, diag_high) if dy < 0 else (send_high, diag_low)
        if dx == 0:
            here, there = pl.ds(0, 6), pl.ds(0, 6)
        else:
            here, there = pl.ds(0 if dx < 0 else 4, 2), pl.ds(4 if dx < 0 else 0, 2)
        return pltpu.make_async_remote_copy(
            src_ref=source.at[step, p, :, here, :], dst_ref=target.at[step, p, :, there, :],
            send_sem=send_sem.at[step, p, d], recv_sem=recv_sem.at[step, p, back],
            device_id=neighbour(dx, dy), device_id_type=MESH,
        )

    def spread(ref, at):
        return jnp.broadcast_to(ref[pl.ds(at, 1), :], (8, 128))

    def terms(j, o, f, v, c):
        rows = pl.ds(8 * j, 8)
        det = (
            f[0] * (f[4] * f[8] - f[5] * f[7])
            - f[1] * (f[3] * f[8] - f[5] * f[6])
            + f[2] * (f[3] * f[7] - f[4] * f[6])
        )
        bulk = lame_lambda * (det - 1.0) * det
        mw = mw_ref[rows, :]
        hard = hard_ref[rows, :]
        terms_ = [[None] * 3 for _ in range(3)]
        for a in range(3):
            for b in range(a, 3):
                stretch = f[3 * a] * f[3 * b] + f[3 * a + 1] * f[3 * b + 1] + f[3 * a + 2] * f[3 * b + 2]
                if a == b:
                    tau = hard * (shear_modulus * (stretch - 1.0) + bulk)
                else:
                    tau = hard * (shear_modulus * stretch)
                terms_[a][b] = mw * c[3 * a + b] - tau
                if a != b:
                    terms_[b][a] = mw * c[3 * b + a] - tau
        feats[pl.ds(8 * j, 8), :] = mw
        for a in range(3):
            moved = (
                terms_[a][0] * (o[0] - CENTRE)
                + terms_[a][1] * (o[1] - CENTRE)
                + terms_[a][2] * (o[2] - CENTRE)
            )
            feats[pl.ds((1 + a) * ROWS + 8 * j, 8), :] = mw * v[a] - moved
            for b in range(3):
                feats[pl.ds((4 + 3 * b + a) * ROWS + 8 * j, 8), :] = terms_[a][b]
        for e, w in enumerate(axis_weights(o[0])):
            wx[pl.ds(e * ROWS + 8 * j, 8), :] = w
        for e, w in enumerate(axis_weights(o[1])):
            wy[pl.ds(e * ROWS + 8 * j, 8), :] = w
        for e, w in enumerate(axis_weights(o[2])):
            wz[pl.ds((4 + e) * ROWS + 8 * j, 8), :] = w
            if e >= 4:
                wz[pl.ds((e - 4) * ROWS + 8 * j, 8), :] = w

    def deposit(k):
        for c in range(CHUNKS):
            r = CHUNKS * k + c
            lanes = pl.ds(128 * c, 128)
            wxs = wx[pl.ds(r, 8, stride=ROWS), :]
            wzs = wz[pl.ds(r + (4 * ROWS if k % 2 == 0 else 0), 8, stride=ROWS), :]
            for e in (0, 2, 4):
                high, low = split(jnp.concatenate(
                    [spread(wy, e * ROWS + r) * wzs, spread(wy, (e + 1) * ROWS + r) * wzs], axis=0
                ))
                bs[k, pl.ds(8 * e, 16), lanes] = high
                bs[k, pl.ds(64 + 8 * e, 16), lanes] = low
            part = [spread(feats, i * ROWS + r) for i in range(13)]
            side = [part[0] * wxs]
            side += [(part[1 + a] + part[4 + a] * ex) * wxs for a in range(3)]
            side += [part[7 + i] * wxs for i in range(6)]
            for i in range(0, 10, 2):
                high, low = split(jnp.concatenate(side[i : i + 2], axis=0))
                sides[k, pl.ds(8 * i, 16), lanes] = high
                sides[k, pl.ds(80 + 8 * i, 16), lanes] = low
        dots = lax.dot_general(
            sides[k], bs[k], (((1,), (1,)), ((), ())), preferred_element_type=jnp.float32
        )
        return dots[:80] + dots[80:]

    def deposit_tile(j):
        even, odd = deposit(2 * j), deposit(2 * j + 1)
        pair = []
        for i in range(10):
            one, two = even[8 * i : 8 * i + 8], odd[8 * i : 8 * i + 8]
            pair.append(jnp.where(half, one, two) + pltpu.roll(jnp.where(half, two, one), 64, 1))
        return [pair[0]] + [pair[1 + a] + ey * pair[4 + a] + ez * pair[7 + a] for a in range(3)]

    def send(step, p, before, first, second):
        low, high = zero, zero
        for i in range(4):
            one = jnp.where(own, first[i], before[i])
            two = jnp.where(own, second[i], first[i])
            mine = jnp.where(half, one, two) + pltpu.roll(jnp.where(half, two, one), 64, 1)
            send_x[step, p, i] = mine
            to_low = mine if i == 0 else pltpu.roll(mine, 16 * i, 1)
            shift = (16 * i - 32) % 128
            to_high = mine if shift == 0 else pltpu.roll(mine, shift, 1)
            low = jnp.where(group == i, to_low, low)
            high = jnp.where(group == i, to_high, high)
        send_low[step, p, 0] = low
        send_high[step, p, 0] = high

    def grid_speed(step, p):
        below = recv_low[step, p, 0] + diag_low[step, p, 0]
        above = recv_high[step, p, 0] + diag_high[step, p, 0]
        total = []
        for i in range(4):
            from_low = below if i == 0 else pltpu.roll(below, 128 - 16 * i, 1)
            shift = (32 - 16 * i) % 128
            from_high = above if shift == 0 else pltpu.roll(above, shift, 1)
            extra = jnp.where(group == 0, from_low, jnp.where(group == 2, from_high, 0.0))
            total.append(send_x[step, p, i] + recv_x[step, p, i] + extra)
        scale = 1.0 / jnp.maximum(total[0], mass_floor)
        speed_x = total[1] * scale + time_step * gravity_slope
        speed_y = total[2] * scale
        speed_z = total[3] * scale + time_step * gravity_vertical
        place_z = 16 * p + jnp.where(half, 0, 8) + r3
        speed_x = jnp.where(place_x < 2, jnp.maximum(speed_x, 0.0), speed_x)
        speed_x = jnp.where(place_x >= 4 * nx - 2, jnp.minimum(speed_x, 0.0), speed_x)
        speed_y = jnp.where(place_y < 2, jnp.maximum(speed_y, 0.0), speed_y)
        speed_y = jnp.where(place_y >= 4 * ny - 2, jnp.minimum(speed_y, 0.0), speed_y)
        speed_z = jnp.where(place_z >= 8 * TILES - 2, jnp.minimum(speed_z, 0.0), speed_z)
        still = outside | (place_z < 2)
        return [jnp.where(still, 0.0, speed) for speed in (speed_x, speed_y, speed_z)]

    def windows(k, speed, turned, beyond, beyond_turned):
        for a in range(3):
            first, second = (speed[a], turned[a]) if k % 4 < 2 else (turned[a], speed[a])
            if k % 2 == 0:
                window = jnp.where(half, first, second)
            elif k % 4 == 1:
                window = jnp.where(own_tile, first, second)
            else:
                window = jnp.where(
                    r3 >= 4,
                    jnp.where(half, first, second),
                    jnp.where(half, beyond[a], beyond_turned[a]),
                )
            for b, factor in enumerate((None, ex, ey, ez_odd if k % 2 else ez_even)):
                q = 3 * b + a
                value = window if factor is None else window * factor
                if q < 8:
                    us[k, pl.ds(q, 8, stride=8), :] = value
                else:
                    us[k, pl.ds(64 + q - 8, 8, stride=4), :] = value

    def gather(k):
        left = jnp.concatenate(
            split(jnp.concatenate([us[k, 0:48, :], us[k, 64:96, :]], axis=0)), axis=0
        )
        taken = lax.dot_general(
            left, bs[k], (((1,), (0,)), ((), ())), preferred_element_type=jnp.float32
        )
        taken = taken[:80] + taken[80:]
        for c in range(CHUNKS):
            r = CHUNKS * k + c
            part = taken[:, 128 * c : 128 * c + 128]
            weights = [spread(wx, e * ROWS + r) for e in range(6)]
            first = weights[0] * part[0:8]
            for e in range(1, 6):
                first = first + weights[e] * part[8 * e : 8 * e + 8]
            second = jnp.where(sub < 4, weights[0], weights[1]) * part[48:56]
            for e in (2, 4):
                at = 48 + 4 * e
                second = second + jnp.where(sub < 4, weights[e], weights[e + 1]) * part[at : at + 8]
            gathered[pl.ds(16 * r, 8), :] = first
            gathered[pl.ds(16 * r + 8, 8), :] = second

    def advance(j):
        rows = pl.ds(8 * j, 8)

        def quantity(q):
            value = gathered[pl.ds(128 * j + q, 8, stride=16), :]
            if q >= 8:
                value = value + gathered[pl.ds(128 * j + q + 4, 8, stride=16), :]
            return value

        o = [off[i, rows, :] for i in range(3)]
        f = [frame[i, rows, :] for i in range(9)]
        v = [quantity(a) for a in range(3)]
        c = [None] * 9
        for a in range(3):
            for b in range(3):
                c[3 * a + b] = 4.0 * (quantity(3 + 3 * b + a) - v[a] * (o[b] - CENTRE))
        o = [o[a] + time_step * v[a] for a in range(3)]
        f = [
            f[3 * a + b]
            + time_step * (c[3 * a] * f[b] + c[3 * a + 1] * f[3 + b] + c[3 * a + 2] * f[6 + b])
            for a in range(3)
            for b in range(3)
        ]
        for ref, values in ((off, o), (vel, v), (aff, c), (frame, f)):
            for i, value in enumerate(values):
                ref[i, rows, :] = value
        return o, f, v, c

    def turn(values):
        return [pltpu.roll(value, 64, 1) for value in values]

    def one_step(step, carry):
        for j in range(TILES):
            rows = pl.ds(8 * j, 8)
            terms(j, *([ref[i, rows, :] for i in range(n)] for ref, n in ((off, 3), (frame, 9), (vel, 3), (aff, 9))))
        fields = [deposit_tile(0), deposit_tile(1)]
        send(step, 0, [zero] * 4, fields[0], fields[1])

        @pl.when(step == 0)
        def _():
            pl.semaphore_wait(barrier, around)

        each_neighbour(lambda d: copy_to(step, 0, d).start())
        fields += [deposit_tile(2), deposit_tile(3)]
        send(step, 1, fields[1], fields[2], fields[3])
        each_neighbour(lambda d: copy_to(step, 1, d).start())

        def wait(d):
            dx, dy = DIRECTIONS[d]
            for p in range(2):
                copy_to(step, p, DIRECTIONS.index((-dx, -dy))).wait_recv()

        each_neighbour(wait)
        speed = [grid_speed(step, p) for p in range(2)] + [[zero] * 3]
        turned = [turn(speed[0]), turn(speed[1]), [zero] * 3]
        for k in range(BLOCKS):
            p = k // 4
            windows(k, speed[p], turned[p], speed[p + 1], turned[p + 1])
        for k in range(BLOCKS):
            gather(k)
        for j in range(TILES):
            advance(j)
        return carry

    lax.fori_loop(0, STEPS, one_step, 0)

    def finish(step, carry):
        for p in range(2):
            each_neighbour(lambda d: copy_to(step, p, d).wait_send())
        return carry

    lax.fori_loop(0, STEPS, finish, 0)
    live = live_ref[...]
    for ref, count in ((off, 3), (vel, 3), (aff, 9), (frame, 9)):
        for i in range(count):
            ref[i] = ref[i] * live


def write_out(off, vel, aff, frame, off_out, vel_out, aff_out, frame_out, sem):
    copies = [
        pltpu.make_async_copy(source, target, sem.at[i])
        for i, (source, target) in enumerate(
            ((aff, aff_out), (frame, frame_out), (off, off_out), (vel, vel_out))
        )
    ]
    for copy in copies:
        copy.start()
    for copy in copies:
        copy.wait()


def per_device(offsets, velocity, affine, strain, particle_mass, plastic_ratio, block_counts):
    nx, ny = lax.axis_size("slope"), lax.axis_size("cross")
    f32 = jnp.float32
    vmem = pl.BlockSpec(memory_space=pltpu.VMEM)
    hbm = pl.BlockSpec(memory_space=pltpu.HBM)
    outs = pl.pallas_call(
        functools.partial(kernel, nx, ny),
        out_shape=[jax.ShapeDtypeStruct((n, ROWS, 128), f32) for n in (3, 3, 9, 9)],
        in_specs=[hbm] * 7,
        out_specs=[vmem] * 4,
        scratch_shapes=[
            pltpu.SMEM((BLOCKS,), jnp.int32),
            pltpu.VMEM((9, ROWS, 128), f32),
            pltpu.VMEM((ROWS, 128), f32),
            pltpu.VMEM((ROWS, 128), f32),
            pltpu.VMEM((ROWS, 128), f32),
            pltpu.VMEM((ROWS, 128), f32),
            pltpu.VMEM((ROWS, 128), f32),
            pltpu.VMEM((8 * ROWS, 128), f32),
            pltpu.VMEM((6 * ROWS, 128), f32),
            pltpu.VMEM((12 * ROWS, 128), f32),
            pltpu.VMEM((13 * ROWS, 128), f32),
            pltpu.VMEM((BLOCKS, 128, 512), jnp.bfloat16),
            pltpu.VMEM((BLOCKS, 160, 512), jnp.bfloat16),
            pltpu.VMEM((BLOCKS, 96, 128), f32),
            pltpu.VMEM((16 * ROWS, 128), f32),
            pltpu.VMEM((STEPS, 2, 4, 8, 128), f32),
            pltpu.VMEM((STEPS, 2, 1, 8, 128), f32),
            pltpu.VMEM((STEPS, 2, 1, 8, 128), f32),
            pltpu.VMEM((STEPS, 2, 4, 8, 128), f32),
            pltpu.VMEM((STEPS, 2, 1, 8, 128), f32),
            pltpu.VMEM((STEPS, 2, 1, 8, 128), f32),
            pltpu.VMEM((STEPS, 2, 1, 8, 128), f32),
            pltpu.VMEM((STEPS, 2, 1, 8, 128), f32),
            pltpu.SemaphoreType.DMA((7,)),
            pltpu.SemaphoreType.DMA((STEPS, 2, 8)),
            pltpu.SemaphoreType.DMA((STEPS, 2, 8)),
        ],
        compiler_params=pltpu.CompilerParams(
            collective_id=0, has_side_effects=True, vmem_limit_bytes=VMEM_BYTES
        ),
    )(
        *(
            pltpu.with_memory_space_constraint(value, pltpu.HBM)
            for value in (
                block_counts.reshape(BLOCKS),
                offsets.reshape(3, ROWS, 128),
                velocity.reshape(3, ROWS, 128),
                affine.reshape(9, ROWS, 128),
                strain.reshape(9, ROWS, 128),
                particle_mass.reshape(ROWS, 128),
                plastic_ratio.reshape(ROWS, 128),
            )
        ),
    )
    outs = pl.pallas_call(
        write_out,
        out_shape=[jax.ShapeDtypeStruct(out.shape, f32) for out in outs],
        in_specs=[vmem] * 4,
        out_specs=[hbm] * 4,
        scratch_shapes=[pltpu.SemaphoreType.DMA((4,))],
        compiler_params=pltpu.CompilerParams(vmem_limit_bytes=VMEM_BYTES),
    )(*outs)
    return tuple(out.reshape(out.shape[0], 1, 1, ROWS * 128) for out in outs)


def solution(mesh):
    wide = P(None, "slope", "cross", None)
    flat = P("slope", "cross", None)
    return jax.shard_map(
        per_device,
        mesh=mesh,
        in_specs=(wide, wide, wide, wide, flat, flat, flat),
        out_specs=(wide, wide, wide, wide),
        check_vma=False,
    )
```

```python
import functools

import jax
import jax.numpy as jnp
from jax import lax
from jax.experimental import pallas as pl
from jax.experimental.pallas import tpu as pltpu
from jax.sharding import PartitionSpec as P

STEPS = 5
BLOCKS = 8
ROWS = 32
CHUNKS = 4
TILES = 4
VMEM_BYTES = 40 * 1024 * 1024
MESH = pl.DeviceIdType.MESH

time_step = 0.02
shear_modulus = 4.0
lame_lambda = 4.0
hardening = 10.0
mass_floor = 0.25
gravity_slope = 1.5
gravity_vertical = -2.5
CENTRE = 2.5

DIRECTIONS = [(0, -1), (0, 1), (-1, -1), (-1, 1), (1, -1), (1, 1), (-1, 0), (1, 0)]


def iota(shape, dim):
    return lax.broadcasted_iota(jnp.int32, shape, dim)


def axis_weights(position):
    base = jnp.floor(position + 0.5)
    dist = position - base
    lower = 0.5 * (0.5 - dist) * (0.5 - dist)
    middle = 0.75 - dist * dist
    upper = 0.5 * (0.5 + dist) * (0.5 + dist)
    at = {e: base == float(e) for e in range(-1, 7)}
    return [
        jnp.where(at[e], middle, jnp.where(at[e + 1], lower, jnp.where(at[e - 1], upper, 0.0)))
        for e in range(6)
    ]


def split(values):
    high = values.astype(jnp.bfloat16)
    low = (values - high.astype(jnp.float32)).astype(jnp.bfloat16)
    return high, low


def kernel(
    nx, ny,
    counts_hbm, off_hbm, vel_hbm, aff_hbm, strain_hbm, mass_hbm, plastic_hbm,
    off, vel, aff, frame,
    counts, strain_in, mass_in, plastic_in, live_ref, mw_ref, hard_ref, wx, wy, wz, feats, bs, sides, us,
    gathered, counted,
    send_x, send_low, send_high, recv_x, recv_low, recv_high, diag_low, diag_high,
    load_sem, send_sem, recv_sem,
):
    ix = lax.axis_index("slope")
    iy = lax.axis_index("cross")

    def neighbour(dx, dy):
        return ix + dx, iy + dy

    def present(dx, dy):
        ok = None
        for d, i, n in ((dx, ix, nx), (dy, iy, ny)):
            if d != 0:
                here = (i + d >= 0) & (i + d < n)
                ok = here if ok is None else ok & here
        return ok

    inside = (ix > 0) & (ix < nx - 1) & (iy > 0) & (iy < ny - 1)

    def each_neighbour(act):
        @pl.when(inside)
        def _():
            for d in range(8):
                act(d)

        @pl.when(jnp.logical_not(inside))
        def _():
            for d, (dx, dy) in enumerate(DIRECTIONS):

                @pl.when(present(dx, dy))
                def _():
                    act(d)

    loads = [
        pltpu.make_async_copy(source, target, load_sem.at[i])
        for i, (source, target) in enumerate((
            (counts_hbm, counts), (mass_hbm, mass_in), (plastic_hbm, plastic_in), (off_hbm, off),
            (vel_hbm, vel), (aff_hbm, aff), (strain_hbm, strain_in),
        ))
    ]
    for load in loads:
        load.start()

    for ref in (recv_x, recv_low, recv_high, diag_low, diag_high):
        ref[...] = jnp.zeros(ref.shape, ref.dtype)
    barrier = pltpu.get_barrier_semaphore()
    around = jnp.int32(0)
    for dx, dy in DIRECTIONS:
        ok = present(dx, dy)
        around = around + jnp.where(ok, 1, 0).astype(jnp.int32)

        @pl.when(ok)
        def _():
            pl.semaphore_signal(barrier, inc=1, device_id=neighbour(dx, dy), device_id_type=MESH)

    for ref in (wx, wz, us, bs, gathered):
        ref[...] = jnp.zeros(ref.shape, ref.dtype)
    for load in loads:
        load.wait()
    row = iota((ROWS, 128), 0)
    slot = (row % CHUNKS) * 128 + iota((ROWS, 128), 1)
    limit = jnp.zeros((ROWS, 128), jnp.int32)
    for k in range(BLOCKS):
        limit = jnp.where(row // CHUNKS == k, counts[k], limit)
    live = jnp.where(slot < limit, 1.0, 0.0).astype(jnp.float32)
    live_ref[...] = live
    mw_ref[...] = mass_in[...] * live
    hard_ref[...] = 4.0 * time_step * live * jnp.exp(hardening * (1.0 - plastic_in[...]))
    for i in range(9):
        frame[i] = strain_in[i] + (1.0 if i % 4 == 0 else 0.0)

    lane = iota((8, 128), 1)
    sub = iota((8, 128), 0)
    half = lane < 64
    r3 = lane % 8
    e2 = (lane % 64) // 8
    e3 = jnp.where(half, r3, (r3 + 4) % 8)
    ex = sub.astype(jnp.float32) - CENTRE
    ey = e2.astype(jnp.float32) - CENTRE
    ez = e3.astype(jnp.float32) - CENTRE
    own = half | (r3 >= 4)
    group = (lane % 64) // 16
    own_tile = half == (r3 >= 4)
    ez_even = r3.astype(jnp.float32) - CENTRE
    ez_odd = ((r3 + 4) % 8).astype(jnp.float32) - CENTRE
    zero = jnp.zeros((8, 128), jnp.float32)
    place_x = 4 * ix + sub
    place_y = 4 * iy + e2
    outside = (place_x >= 4 * nx) | (place_y >= 4 * ny)

    def copy_to(step, d):
        dx, dy = DIRECTIONS[d]
        if dy == 0:
            source, target = send_x, recv_x
        elif dx == 0:
            source, target = (send_low, recv_high) if dy < 0 else (send_high, recv_low)
        else:
            source, target = (send_low, diag_high) if dy < 0 else (send_high, diag_low)
        if dx == 0:
            here, there = pl.ds(0, 6), pl.ds(0, 6)
        else:
            here, there = pl.ds(0 if dx < 0 else 4, 2), pl.ds(4 if dx < 0 else 0, 2)
        return pltpu.make_async_remote_copy(
            src_ref=source.at[step, :, here, :], dst_ref=target.at[step, :, there, :],
            send_sem=send_sem, recv_sem=recv_sem.at[step],
            device_id=neighbour(dx, dy), device_id_type=MESH,
        )

    def passed(sem, rows):
        pltpu.make_async_copy(counted.at[pl.ds(0, rows), :], counted.at[pl.ds(0, rows), :], sem).wait()

    def each_edge(act):
        side_x = (ix == 0) | (ix == nx - 1)
        side_y = (iy == 0) | (iy == ny - 1)
        for at_x, at_y, rows in ((0, 0, 72), (1, 0, 48), (0, 1, 52), (1, 1, 32)):

            @pl.when((side_x == bool(at_x)) & (side_y == bool(at_y)))
            def _():
                act(rows)

    def spread(ref, at):
        return jnp.broadcast_to(ref[pl.ds(at, 1), :], (8, 128))

    def terms(j, o, f, v, c):
        rows = pl.ds(8 * j, 8)
        det = (
            f[0] * (f[4] * f[8] - f[5] * f[7])
            - f[1] * (f[3] * f[8] - f[5] * f[6])
            + f[2] * (f[3] * f[7] - f[4] * f[6])
        )
        bulk = lame_lambda * (det - 1.0) * det
        mw = mw_ref[rows, :]
        hard = hard_ref[rows, :]
        terms_ = [[None] * 3 for _ in range(3)]
        for a in range(3):
            for b in range(a, 3):
                stretch = f[3 * a] * f[3 * b] + f[3 * a + 1] * f[3 * b + 1] + f[3 * a + 2] * f[3 * b + 2]
                if a == b:
                    tau = hard * (shear_modulus * (stretch - 1.0) + bulk)
                else:
                    tau = hard * (shear_modulus * stretch)
                terms_[a][b] = mw * c[3 * a + b] - tau
                if a != b:
                    terms_[b][a] = mw * c[3 * b + a] - tau
        feats[pl.ds(8 * j, 8), :] = mw
        for a in range(3):
            moved = (
                terms_[a][0] * (o[0] - CENTRE)
                + terms_[a][1] * (o[1] - CENTRE)
                + terms_[a][2] * (o[2] - CENTRE)
            )
            feats[pl.ds((1 + a) * ROWS + 8 * j, 8), :] = mw * v[a] - moved
            for b in range(3):
                feats[pl.ds((4 + 3 * b + a) * ROWS + 8 * j, 8), :] = terms_[a][b]
        for e, w in enumerate(axis_weights(o[0])):
            wx[pl.ds(e * ROWS + 8 * j, 8), :] = w
        for e, w in enumerate(axis_weights(o[1])):
            wy[pl.ds(e * ROWS + 8 * j, 8), :] = w
        for e, w in enumerate(axis_weights(o[2])):
            wz[pl.ds((4 + e) * ROWS + 8 * j, 8), :] = w
            if e >= 4:
                wz[pl.ds((e - 4) * ROWS + 8 * j, 8), :] = w

    def deposit(k):
        for c in range(CHUNKS):
            r = CHUNKS * k + c
            lanes = pl.ds(128 * c, 128)
            wxs = wx[pl.ds(r, 8, stride=ROWS), :]
            wzs = wz[pl.ds(r + (4 * ROWS if k % 2 == 0 else 0), 8, stride=ROWS), :]
            for e in (0, 2, 4):
                high, low = split(jnp.concatenate(
                    [spread(wy, e * ROWS + r) * wzs, spread(wy, (e + 1) * ROWS + r) * wzs], axis=0
                ))
                bs[k, pl.ds(8 * e, 16), lanes] = high
                bs[k, pl.ds(64 + 8 * e, 16), lanes] = low
            part = [spread(feats, i * ROWS + r) for i in range(13)]
            side = [part[0] * wxs]
            side += [(part[1 + a] + part[4 + a] * ex) * wxs for a in range(3)]
            side += [part[7 + i] * wxs for i in range(6)]
            for i in range(0, 10, 2):
                high, low = split(jnp.concatenate(side[i : i + 2], axis=0))
                sides[k, pl.ds(8 * i, 16), lanes] = high
                sides[k, pl.ds(80 + 8 * i, 16), lanes] = low
        dots = lax.dot_general(
            sides[k], bs[k], (((1,), (1,)), ((), ())), preferred_element_type=jnp.float32
        )
        return dots[:80] + dots[80:]

    def deposit_tile(j):
        even, odd = deposit(2 * j), deposit(2 * j + 1)
        pair = []
        for i in range(10):
            one, two = even[8 * i : 8 * i + 8], odd[8 * i : 8 * i + 8]
            pair.append(jnp.where(half, one, two) + pltpu.roll(jnp.where(half, two, one), 64, 1))
        return [pair[0]] + [pair[1 + a] + ey * pair[4 + a] + ez * pair[7 + a] for a in range(3)]

    def send(step, p, before, first, second):
        low, high = zero, zero
        for i in range(4):
            one = jnp.where(own, first[i], before[i])
            two = jnp.where(own, second[i], first[i])
            mine = jnp.where(half, one, two) + pltpu.roll(jnp.where(half, two, one), 64, 1)
            send_x[step, 4 * p + i] = mine
            to_low = mine if i == 0 else pltpu.roll(mine, 16 * i, 1)
            shift = (16 * i - 32) % 128
            to_high = mine if shift == 0 else pltpu.roll(mine, shift, 1)
            low = jnp.where(group == i, to_low, low)
            high = jnp.where(group == i, to_high, high)
        send_low[step, p] = low
        send_high[step, p] = high

    def grid_speed(step, p):
        below = recv_low[step, p] + diag_low[step, p]
        above = recv_high[step, p] + diag_high[step, p]
        total = []
        for i in range(4):
            from_low = below if i == 0 else pltpu.roll(below, 128 - 16 * i, 1)
            shift = (32 - 16 * i) % 128
            from_high = above if shift == 0 else pltpu.roll(above, shift, 1)
            extra = jnp.where(group == 0, from_low, jnp.where(group == 2, from_high, 0.0))
            total.append(send_x[step, 4 * p + i] + recv_x[step, 4 * p + i] + extra)
        scale = 1.0 / jnp.maximum(total[0], mass_floor)
        speed_x = total[1] * scale + time_step * gravity_slope
        speed_y = total[2] * scale
        speed_z = total[3] * scale + time_step * gravity_vertical
        place_z = 16 * p + jnp.where(half, 0, 8) + r3
        speed_x = jnp.where(place_x < 2, jnp.maximum(speed_x, 0.0), speed_x)
        speed_x = jnp.where(place_x >= 4 * nx - 2, jnp.minimum(speed_x, 0.0), speed_x)
        speed_y = jnp.where(place_y < 2, jnp.maximum(speed_y, 0.0), speed_y)
        speed_y = jnp.where(place_y >= 4 * ny - 2, jnp.minimum(speed_y, 0.0), speed_y)
        speed_z = jnp.where(place_z >= 8 * TILES - 2, jnp.minimum(speed_z, 0.0), speed_z)
        still = outside | (place_z < 2)
        return [jnp.where(still, 0.0, speed) for speed in (speed_x, speed_y, speed_z)]

    def windows(k, speed, turned, beyond, beyond_turned):
        for a in range(3):
            first, second = (speed[a], turned[a]) if k % 4 < 2 else (turned[a], speed[a])
            if k % 2 == 0:
                window = jnp.where(half, first, second)
            elif k % 4 == 1:
                window = jnp.where(own_tile, first, second)
            else:
                window = jnp.where(
                    r3 >= 4,
                    jnp.where(half, first, second),
                    jnp.where(half, beyond[a], beyond_turned[a]),
                )
            for b, factor in enumerate((None, ex, ey, ez_odd if k % 2 else ez_even)):
                q = 3 * b + a
                value = window if factor is None else window * factor
                if q < 8:
                    us[k, pl.ds(q, 8, stride=8), :] = value
                else:
                    us[k, pl.ds(64 + q - 8, 8, stride=4), :] = value

    def gather(k):
        left = jnp.concatenate(
            split(jnp.concatenate([us[k, 0:48, :], us[k, 64:96, :]], axis=0)), axis=0
        )
        taken = lax.dot_general(
            left, bs[k], (((1,), (0,)), ((), ())), preferred_element_type=jnp.float32
        )
        taken = taken[:80] + taken[80:]
        for c in range(CHUNKS):
            r = CHUNKS * k + c
            part = taken[:, 128 * c : 128 * c + 128]
            weights = [spread(wx, e * ROWS + r) for e in range(6)]
            first = weights[0] * part[0:8]
            for e in range(1, 6):
                first = first + weights[e] * part[8 * e : 8 * e + 8]
            second = jnp.where(sub < 4, weights[0], weights[1]) * part[48:56]
            for e in (2, 4):
                at = 48 + 4 * e
                second = second + jnp.where(sub < 4, weights[e], weights[e + 1]) * part[at : at + 8]
            gathered[pl.ds(16 * r, 8), :] = first
            gathered[pl.ds(16 * r + 8, 8), :] = second

    def advance(j):
        rows = pl.ds(8 * j, 8)

        def quantity(q):
            value = gathered[pl.ds(128 * j + q, 8, stride=16), :]
            if q >= 8:
                value = value + gathered[pl.ds(128 * j + q + 4, 8, stride=16), :]
            return value

        o = [off[i, rows, :] for i in range(3)]
        f = [frame[i, rows, :] for i in range(9)]
        v = [quantity(a) for a in range(3)]
        c = [None] * 9
        for a in range(3):
            for b in range(3):
                c[3 * a + b] = 4.0 * (quantity(3 + 3 * b + a) - v[a] * (o[b] - CENTRE))
        o = [o[a] + time_step * v[a] for a in range(3)]
        f = [
            f[3 * a + b]
            + time_step * (c[3 * a] * f[b] + c[3 * a + 1] * f[3 + b] + c[3 * a + 2] * f[6 + b])
            for a in range(3)
            for b in range(3)
        ]
        for ref, values in ((off, o), (vel, v), (aff, c), (frame, f)):
            for i, value in enumerate(values):
                ref[i, rows, :] = value
        return o, f, v, c

    def turn(values):
        return [pltpu.roll(value, 64, 1) for value in values]

    def one_step(step, carry):
        for j in range(TILES):
            rows = pl.ds(8 * j, 8)
            terms(j, *([ref[i, rows, :] for i in range(n)] for ref, n in ((off, 3), (frame, 9), (vel, 3), (aff, 9))))
        fields = [deposit_tile(j) for j in range(TILES)]
        send(step, 0, [zero] * 4, fields[0], fields[1])
        send(step, 1, fields[1], fields[2], fields[3])

        @pl.when(step == 0)
        def _():
            pl.semaphore_wait(barrier, around)

        each_neighbour(lambda d: copy_to(step, d).start())

        each_edge(lambda rows: passed(recv_sem.at[step], rows))
        speed = [grid_speed(step, p) for p in range(2)] + [[zero] * 3]
        turned = [turn(speed[0]), turn(speed[1]), [zero] * 3]
        for k in range(BLOCKS):
            p = k // 4
            windows(k, speed[p], turned[p], speed[p + 1], turned[p + 1])
        for k in range(BLOCKS):
            gather(k)
        for j in range(TILES):
            advance(j)
        return carry

    lax.fori_loop(0, STEPS, one_step, 0)

    each_edge(lambda rows: passed(send_sem, STEPS * rows))
    live = live_ref[...]
    for ref, count in ((off, 3), (vel, 3), (aff, 9), (frame, 9)):
        for i in range(count):
            ref[i] = ref[i] * live


def write_out(off, vel, aff, frame, off_out, vel_out, aff_out, frame_out, sem):
    copies = [
        pltpu.make_async_copy(source, target, sem.at[i])
        for i, (source, target) in enumerate(
            ((aff, aff_out), (frame, frame_out), (off, off_out), (vel, vel_out))
        )
    ]
    for copy in copies:
        copy.start()
    for copy in copies:
        copy.wait()


def per_device(offsets, velocity, affine, strain, particle_mass, plastic_ratio, block_counts):
    nx, ny = lax.axis_size("slope"), lax.axis_size("cross")
    f32 = jnp.float32
    vmem = pl.BlockSpec(memory_space=pltpu.VMEM)
    hbm = pl.BlockSpec(memory_space=pltpu.HBM)
    outs = pl.pallas_call(
        functools.partial(kernel, nx, ny),
        out_shape=[jax.ShapeDtypeStruct((n, ROWS, 128), f32) for n in (3, 3, 9, 9)],
        in_specs=[hbm] * 7,
        out_specs=[vmem] * 4,
        scratch_shapes=[
            pltpu.SMEM((BLOCKS,), jnp.int32),
            pltpu.VMEM((9, ROWS, 128), f32),
            pltpu.VMEM((ROWS, 128), f32),
            pltpu.VMEM((ROWS, 128), f32),
            pltpu.VMEM((ROWS, 128), f32),
            pltpu.VMEM((ROWS, 128), f32),
            pltpu.VMEM((ROWS, 128), f32),
            pltpu.VMEM((8 * ROWS, 128), f32),
            pltpu.VMEM((6 * ROWS, 128), f32),
            pltpu.VMEM((12 * ROWS, 128), f32),
            pltpu.VMEM((13 * ROWS, 128), f32),
            pltpu.VMEM((BLOCKS, 128, 512), jnp.bfloat16),
            pltpu.VMEM((BLOCKS, 160, 512), jnp.bfloat16),
            pltpu.VMEM((BLOCKS, 96, 128), f32),
            pltpu.VMEM((16 * ROWS, 128), f32),
            pltpu.VMEM((STEPS * 72, 128), f32),
            pltpu.VMEM((STEPS, 8, 8, 128), f32),
            pltpu.VMEM((STEPS, 2, 8, 128), f32),
            pltpu.VMEM((STEPS, 2, 8, 128), f32),
            pltpu.VMEM((STEPS, 8, 8, 128), f32),
            pltpu.VMEM((STEPS, 2, 8, 128), f32),
            pltpu.VMEM((STEPS, 2, 8, 128), f32),
            pltpu.VMEM((STEPS, 2, 8, 128), f32),
            pltpu.VMEM((STEPS, 2, 8, 128), f32),
            pltpu.SemaphoreType.DMA((7,)),
            pltpu.SemaphoreType.DMA,
            pltpu.SemaphoreType.DMA((STEPS,)),
        ],
        compiler_params=pltpu.CompilerParams(
            collective_id=0, has_side_effects=True, vmem_limit_bytes=VMEM_BYTES
        ),
    )(
        *(
            pltpu.with_memory_space_constraint(value, pltpu.HBM)
            for value in (
                block_counts.reshape(BLOCKS),
                offsets.reshape(3, ROWS, 128),
                velocity.reshape(3, ROWS, 128),
                affine.reshape(9, ROWS, 128),
                strain.reshape(9, ROWS, 128),
                particle_mass.reshape(ROWS, 128),
                plastic_ratio.reshape(ROWS, 128),
            )
        ),
    )
    outs = pl.pallas_call(
        write_out,
        out_shape=[jax.ShapeDtypeStruct(out.shape, f32) for out in outs],
        in_specs=[vmem] * 4,
        out_specs=[hbm] * 4,
        scratch_shapes=[pltpu.SemaphoreType.DMA((4,))],
        compiler_params=pltpu.CompilerParams(vmem_limit_bytes=VMEM_BYTES),
    )(*outs)
    return tuple(out.reshape(out.shape[0], 1, 1, ROWS * 128) for out in outs)


def solution(mesh):
    wide = P(None, "slope", "cross", None)
    flat = P("slope", "cross", None)
    return jax.shard_map(
        per_device,
        mesh=mesh,
        in_specs=(wide, wide, wide, wide, flat, flat, flat),
        out_specs=(wide, wide, wide, wide),
        check_vma=False,
    )
```

```python
import functools

import jax
import jax.numpy as jnp
from jax import lax
from jax.experimental import pallas as pl
from jax.experimental.pallas import tpu as pltpu
from jax.sharding import PartitionSpec as P

STEPS = 5
BLOCKS = 8
ROWS = 32
CHUNKS = 4
TILES = 4
VMEM_BYTES = 40 * 1024 * 1024
MESH = pl.DeviceIdType.MESH

time_step = 0.02
shear_modulus = 4.0
lame_lambda = 4.0
hardening = 10.0
mass_floor = 0.25
gravity_slope = 1.5
gravity_vertical = -2.5
CENTRE = 2.5

DIRECTIONS = [(0, -1), (0, 1), (-1, -1), (-1, 1), (1, -1), (1, 1), (-1, 0), (1, 0)]


def iota(shape, dim):
    return lax.broadcasted_iota(jnp.int32, shape, dim)


def axis_weights(position):
    base = jnp.floor(position + 0.5)
    dist = position - base
    lower = 0.5 * (0.5 - dist) * (0.5 - dist)
    middle = 0.75 - dist * dist
    upper = 0.5 * (0.5 + dist) * (0.5 + dist)
    at = {e: base == float(e) for e in range(-1, 7)}
    return [
        jnp.where(at[e], middle, jnp.where(at[e + 1], lower, jnp.where(at[e - 1], upper, 0.0)))
        for e in range(6)
    ]


def split(values):
    high = values.astype(jnp.bfloat16)
    low = (values - high.astype(jnp.float32)).astype(jnp.bfloat16)
    return high, low


def kernel(
    nx, ny,
    counts_hbm, off_hbm, vel_hbm, aff_hbm, strain_hbm, mass_hbm, plastic_hbm,
    off, vel, aff, frame,
    counts, strain_in, mass_in, plastic_in, live_ref, mw_ref, hard_ref, wx, side_rows, plane_rows, pairs, bs, sides, us,
    gathered, counted,
    send_x, send_low, send_high, recv_x, recv_low, recv_high, diag_low, diag_high,
    load_sem, send_sem, recv_sem,
):
    ix = lax.axis_index("slope")
    iy = lax.axis_index("cross")

    def neighbour(dx, dy):
        return ix + dx, iy + dy

    def present(dx, dy):
        ok = None
        for d, i, n in ((dx, ix, nx), (dy, iy, ny)):
            if d != 0:
                here = (i + d >= 0) & (i + d < n)
                ok = here if ok is None else ok & here
        return ok

    inside = (ix > 0) & (ix < nx - 1) & (iy > 0) & (iy < ny - 1)

    def each_neighbour(act):
        @pl.when(inside)
        def _():
            for d in range(8):
                act(d)

        @pl.when(jnp.logical_not(inside))
        def _():
            for d, (dx, dy) in enumerate(DIRECTIONS):

                @pl.when(present(dx, dy))
                def _():
                    act(d)

    loads = [
        pltpu.make_async_copy(source, target, load_sem.at[i])
        for i, (source, target) in enumerate((
            (counts_hbm, counts), (mass_hbm, mass_in), (plastic_hbm, plastic_in), (off_hbm, off),
            (vel_hbm, vel), (aff_hbm, aff), (strain_hbm, strain_in),
        ))
    ]
    for load in loads:
        load.start()

    for ref in (recv_x, recv_low, recv_high, diag_low, diag_high):
        ref[...] = jnp.zeros(ref.shape, ref.dtype)
    barrier = pltpu.get_barrier_semaphore()
    around = jnp.int32(0)
    for dx, dy in DIRECTIONS:
        ok = present(dx, dy)
        around = around + jnp.where(ok, 1, 0).astype(jnp.int32)

        @pl.when(ok)
        def _():
            pl.semaphore_signal(barrier, inc=1, device_id=neighbour(dx, dy), device_id_type=MESH)

    for ref in (side_rows, plane_rows, us, bs):
        ref[...] = jnp.zeros(ref.shape, ref.dtype)
    for load in loads:
        load.wait()
    row = iota((ROWS, 128), 0)
    slot = (row % CHUNKS) * 128 + iota((ROWS, 128), 1)
    limit = jnp.zeros((ROWS, 128), jnp.int32)
    for k in range(BLOCKS):
        limit = jnp.where(row // CHUNKS == k, counts[k], limit)
    live = jnp.where(slot < limit, 1.0, 0.0).astype(jnp.float32)
    live_ref[...] = live
    mw_ref[...] = mass_in[...] * live
    hard_ref[...] = 4.0 * time_step * live * jnp.exp(hardening * (1.0 - plastic_in[...]))
    for i in range(9):
        frame[i] = strain_in[i] + (1.0 if i % 4 == 0 else 0.0)

    lane = iota((8, 128), 1)
    sub = iota((8, 128), 0)
    half = lane < 64
    r3 = lane % 8
    e2 = (lane % 64) // 8
    e3 = jnp.where(half, r3, (r3 + 4) % 8)
    ex = sub.astype(jnp.float32) - CENTRE
    ey = e2.astype(jnp.float32) - CENTRE
    ez = e3.astype(jnp.float32) - CENTRE
    own = half | (r3 >= 4)
    group = (lane % 64) // 16
    own_tile = half == (r3 >= 4)
    ez_even = r3.astype(jnp.float32) - CENTRE
    ez_odd = ((r3 + 4) % 8).astype(jnp.float32) - CENTRE
    zero = jnp.zeros((8, 128), jnp.float32)
    place_x = 4 * ix + sub
    place_y = 4 * iy + e2
    outside = (place_x >= 4 * nx) | (place_y >= 4 * ny)

    def copy_to(step, d):
        dx, dy = DIRECTIONS[d]
        if dy == 0:
            source, target = send_x, recv_x
        elif dx == 0:
            source, target = (send_low, recv_high) if dy < 0 else (send_high, recv_low)
        else:
            source, target = (send_low, diag_high) if dy < 0 else (send_high, diag_low)
        if dx == 0:
            here, there = pl.ds(0, 6), pl.ds(0, 6)
        else:
            here, there = pl.ds(0 if dx < 0 else 4, 2), pl.ds(4 if dx < 0 else 0, 2)
        return pltpu.make_async_remote_copy(
            src_ref=source.at[step, :, here, :], dst_ref=target.at[step, :, there, :],
            send_sem=send_sem, recv_sem=recv_sem.at[step],
            device_id=neighbour(dx, dy), device_id_type=MESH,
        )

    def passed(sem, rows):
        pltpu.make_async_copy(counted.at[pl.ds(0, rows), :], counted.at[pl.ds(0, rows), :], sem).wait()

    def each_edge(act):
        side_x = (ix == 0) | (ix == nx - 1)
        side_y = (iy == 0) | (iy == ny - 1)
        for at_x, at_y, rows in ((0, 0, 72), (1, 0, 48), (0, 1, 52), (1, 1, 32)):

            @pl.when((side_x == bool(at_x)) & (side_y == bool(at_y)))
            def _():
                act(rows)

    def terms(j):
        rows = pl.ds(8 * j, 8)
        o, f, v, c = (
            [ref[i, rows, :] for i in range(n)] for ref, n in ((off, 3), (frame, 9), (vel, 3), (aff, 9))
        )
        det = (
            f[0] * (f[4] * f[8] - f[5] * f[7])
            - f[1] * (f[3] * f[8] - f[5] * f[6])
            + f[2] * (f[3] * f[7] - f[4] * f[6])
        )
        bulk = lame_lambda * (det - 1.0) * det
        mw = mw_ref[rows, :]
        hard = hard_ref[rows, :]
        pull = [[None] * 3 for _ in range(3)]
        for a in range(3):
            for b in range(a, 3):
                stretch = f[3 * a] * f[3 * b] + f[3 * a + 1] * f[3 * b + 1] + f[3 * a + 2] * f[3 * b + 2]
                if a == b:
                    tau = hard * (shear_modulus * (stretch - 1.0) + bulk)
                else:
                    tau = hard * (shear_modulus * stretch)
                pull[a][b] = mw * c[3 * a + b] - tau
                if a != b:
                    pull[b][a] = mw * c[3 * b + a] - tau
        push = []
        for a in range(3):
            moved = (
                pull[a][0] * (o[0] - CENTRE) + pull[a][1] * (o[1] - CENTRE) + pull[a][2] * (o[2] - CENTRE)
            )
            push.append(mw * v[a] - moved)
        return mw, push, pull, [axis_weights(o[i]) for i in range(3)]

    def deposit_tile(j):
        mw, push, pull, weights = terms(j)
        for e in range(6):
            at = weights[0][e]
            wx[j, e] = at
            side = [mw]
            side += [push[a] + (e - CENTRE) * pull[a][0] for a in range(3)]
            side += [pull[a][b] for b in (1, 2) for a in range(3)]
            for i, value in enumerate(side):
                side_rows[j, pl.ds(8 * (6 * i + e), 8), :] = value * at
        for e in range(6):
            for z in range(6):
                value = weights[1][e] * weights[2][z]
                plane_rows[j, 0, pl.ds(8 * (8 * e + z), 8), :] = value
                plane_rows[j, 1, pl.ds(8 * (8 * e + (z + 4) % 8), 8), :] = value
        totals = []
        for odd in range(2):
            k = 2 * j + odd
            for c in range(CHUNKS):
                s = CHUNKS * odd + c
                lanes = pl.ds(128 * c, 128)
                high, low = split(plane_rows[j, odd, pl.ds(s, 48, stride=8), :])
                bs[k, 0:48, lanes] = high
                bs[k, 64:112, lanes] = low
                high, low = split(side_rows[j, pl.ds(s, 64, stride=8), :])
                sides[k, 0:64, lanes] = high
                sides[k, 64:128, lanes] = low
            dots = lax.dot_general(
                sides[k], bs[k], (((1,), (1,)), ((), ())), preferred_element_type=jnp.float32
            )
            totals.append(dots[:64] + dots[64:])
        for i in range(8):
            one, two = totals[0][8 * i : 8 * i + 8], totals[1][8 * i : 8 * i + 8]
            pairs[j, pl.ds(8 * i, 8), :] = jnp.where(half, one, two) + pltpu.roll(
                jnp.where(half, two, one), 64, 1
            )
        pair = [pairs[j, pl.ds(6 * i, 8), :] for i in range(10)]
        return [pair[0]] + [pair[1 + a] + ey * pair[4 + a] + ez * pair[7 + a] for a in range(3)]

    def send(step, p, before, first, second):
        low, high = zero, zero
        for i in range(4):
            one = jnp.where(own, first[i], before[i])
            two = jnp.where(own, second[i], first[i])
            mine = jnp.where(half, one, two) + pltpu.roll(jnp.where(half, two, one), 64, 1)
            send_x[step, 4 * p + i] = mine
            to_low = mine if i == 0 else pltpu.roll(mine, 16 * i, 1)
            shift = (16 * i - 32) % 128
            to_high = mine if shift == 0 else pltpu.roll(mine, shift, 1)
            low = jnp.where(group == i, to_low, low)
            high = jnp.where(group == i, to_high, high)
        send_low[step, p] = low
        send_high[step, p] = high

    def grid_speed(step, p):
        below = recv_low[step, p] + diag_low[step, p]
        above = recv_high[step, p] + diag_high[step, p]
        total = []
        for i in range(4):
            from_low = below if i == 0 else pltpu.roll(below, 128 - 16 * i, 1)
            shift = (32 - 16 * i) % 128
            from_high = above if shift == 0 else pltpu.roll(above, shift, 1)
            extra = jnp.where(group == 0, from_low, jnp.where(group == 2, from_high, 0.0))
            total.append(send_x[step, 4 * p + i] + recv_x[step, 4 * p + i] + extra)
        scale = 1.0 / jnp.maximum(total[0], mass_floor)
        speed_x = total[1] * scale + time_step * gravity_slope
        speed_y = total[2] * scale
        speed_z = total[3] * scale + time_step * gravity_vertical
        place_z = 16 * p + jnp.where(half, 0, 8) + r3
        speed_x = jnp.where(place_x < 2, jnp.maximum(speed_x, 0.0), speed_x)
        speed_x = jnp.where(place_x >= 4 * nx - 2, jnp.minimum(speed_x, 0.0), speed_x)
        speed_y = jnp.where(place_y < 2, jnp.maximum(speed_y, 0.0), speed_y)
        speed_y = jnp.where(place_y >= 4 * ny - 2, jnp.minimum(speed_y, 0.0), speed_y)
        speed_z = jnp.where(place_z >= 8 * TILES - 2, jnp.minimum(speed_z, 0.0), speed_z)
        still = outside | (place_z < 2)
        return [jnp.where(still, 0.0, speed) for speed in (speed_x, speed_y, speed_z)]

    def windows(k, speed, turned, beyond, beyond_turned):
        for a in range(3):
            first, second = (speed[a], turned[a]) if k % 4 < 2 else (turned[a], speed[a])
            if k % 2 == 0:
                window = jnp.where(half, first, second)
            elif k % 4 == 1:
                window = jnp.where(own_tile, first, second)
            else:
                window = jnp.where(
                    r3 >= 4,
                    jnp.where(half, first, second),
                    jnp.where(half, beyond[a], beyond_turned[a]),
                )
            for b, factor in enumerate((None, ex, ey, ez_odd if k % 2 else ez_even)):
                q = 3 * b + a
                value = window if factor is None else window * factor
                us[k, pl.ds(q, 8, stride=12), :] = value

    def gather(k):
        left = jnp.concatenate(split(us[k, 0:80, :]), axis=1)
        planes = bs[k]
        taken = lax.dot_general(
            left, jnp.concatenate([planes, planes], axis=0),
            (((1,), (0,)), ((), ())), preferred_element_type=jnp.float32,
        )
        for c in range(CHUNKS):
            s = CHUNKS * (k % 2) + c
            gathered[k // 2, pl.ds(s, 72, stride=8), :] = taken[:72, 128 * c : 128 * c + 128]

    def advance(j):
        rows = pl.ds(8 * j, 8)
        weights = [wx[j, e] for e in range(6)]

        def quantity(q):
            value = weights[0] * gathered[j, pl.ds(8 * q, 8), :]
            for e in range(1, 6):
                value = value + weights[e] * gathered[j, pl.ds(8 * (12 * e + q), 8), :]
            return value

        o = [off[i, rows, :] for i in range(3)]
        f = [frame[i, rows, :] for i in range(9)]
        v = [quantity(a) for a in range(3)]
        c = [None] * 9
        for a in range(3):
            for b in range(3):
                c[3 * a + b] = 4.0 * (quantity(3 + 3 * b + a) - v[a] * (o[b] - CENTRE))
        o = [o[a] + time_step * v[a] for a in range(3)]
        f = [
            f[3 * a + b]
            + time_step * (c[3 * a] * f[b] + c[3 * a + 1] * f[3 + b] + c[3 * a + 2] * f[6 + b])
            for a in range(3)
            for b in range(3)
        ]
        for ref, values in ((off, o), (vel, v), (aff, c), (frame, f)):
            for i, value in enumerate(values):
                ref[i, rows, :] = value
        return o, f, v, c

    def turn(values):
        return [pltpu.roll(value, 64, 1) for value in values]

    def one_step(step, carry):
        fields = [deposit_tile(j) for j in range(TILES)]
        send(step, 0, [zero] * 4, fields[0], fields[1])
        send(step, 1, fields[1], fields[2], fields[3])

        @pl.when(step == 0)
        def _():
            pl.semaphore_wait(barrier, around)

        each_neighbour(lambda d: copy_to(step, d).start())

        each_edge(lambda rows: passed(recv_sem.at[step], rows))
        speed = [grid_speed(step, p) for p in range(2)] + [[zero] * 3]
        turned = [turn(speed[0]), turn(speed[1]), [zero] * 3]
        for k in range(BLOCKS):
            p = k // 4
            windows(k, speed[p], turned[p], speed[p + 1], turned[p + 1])
        for k in range(BLOCKS):
            gather(k)
        for j in range(TILES):
            advance(j)
        return carry

    lax.fori_loop(0, STEPS, one_step, 0)

    each_edge(lambda rows: passed(send_sem, STEPS * rows))
    live = live_ref[...]
    for ref, count in ((off, 3), (vel, 3), (aff, 9), (frame, 9)):
        for i in range(count):
            ref[i] = ref[i] * live


def write_out(off, vel, aff, frame, off_out, vel_out, aff_out, frame_out, sem):
    copies = [
        pltpu.make_async_copy(source, target, sem.at[i])
        for i, (source, target) in enumerate(
            ((aff, aff_out), (frame, frame_out), (off, off_out), (vel, vel_out))
        )
    ]
    for copy in copies:
        copy.start()
    for copy in copies:
        copy.wait()


def per_device(offsets, velocity, affine, strain, particle_mass, plastic_ratio, block_counts):
    nx, ny = lax.axis_size("slope"), lax.axis_size("cross")
    f32 = jnp.float32
    vmem = pl.BlockSpec(memory_space=pltpu.VMEM)
    hbm = pl.BlockSpec(memory_space=pltpu.HBM)
    outs = pl.pallas_call(
        functools.partial(kernel, nx, ny),
        out_shape=[jax.ShapeDtypeStruct((n, ROWS, 128), f32) for n in (3, 3, 9, 9)],
        in_specs=[hbm] * 7,
        out_specs=[vmem] * 4,
        scratch_shapes=[
            pltpu.SMEM((BLOCKS,), jnp.int32),
            pltpu.VMEM((9, ROWS, 128), f32),
            pltpu.VMEM((ROWS, 128), f32),
            pltpu.VMEM((ROWS, 128), f32),
            pltpu.VMEM((ROWS, 128), f32),
            pltpu.VMEM((ROWS, 128), f32),
            pltpu.VMEM((ROWS, 128), f32),
            pltpu.VMEM((TILES, 6, 8, 128), f32),
            pltpu.VMEM((TILES, 512, 128), f32),
            pltpu.VMEM((TILES, 2, 384, 128), f32),
            pltpu.VMEM((TILES, 64, 128), f32),
            pltpu.VMEM((BLOCKS, 128, 512), jnp.bfloat16),
            pltpu.VMEM((BLOCKS, 128, 512), jnp.bfloat16),
            pltpu.VMEM((BLOCKS, 96, 128), f32),
            pltpu.VMEM((TILES, 576, 128), f32),
            pltpu.VMEM((STEPS * 72, 128), f32),
            pltpu.VMEM((STEPS, 8, 8, 128), f32),
            pltpu.VMEM((STEPS, 2, 8, 128), f32),
            pltpu.VMEM((STEPS, 2, 8, 128), f32),
            pltpu.VMEM((STEPS, 8, 8, 128), f32),
            pltpu.VMEM((STEPS, 2, 8, 128), f32),
            pltpu.VMEM((STEPS, 2, 8, 128), f32),
            pltpu.VMEM((STEPS, 2, 8, 128), f32),
            pltpu.VMEM((STEPS, 2, 8, 128), f32),
            pltpu.SemaphoreType.DMA((7,)),
            pltpu.SemaphoreType.DMA,
            pltpu.SemaphoreType.DMA((STEPS,)),
        ],
        compiler_params=pltpu.CompilerParams(
            collective_id=0, has_side_effects=True, vmem_limit_bytes=VMEM_BYTES
        ),
    )(
        *(
            pltpu.with_memory_space_constraint(value, pltpu.HBM)
            for value in (
                block_counts.reshape(BLOCKS),
                offsets.reshape(3, ROWS, 128),
                velocity.reshape(3, ROWS, 128),
                affine.reshape(9, ROWS, 128),
                strain.reshape(9, ROWS, 128),
                particle_mass.reshape(ROWS, 128),
                plastic_ratio.reshape(ROWS, 128),
            )
        ),
    )
    outs = pl.pallas_call(
        write_out,
        out_shape=[jax.ShapeDtypeStruct(out.shape, f32) for out in outs],
        in_specs=[vmem] * 4,
        out_specs=[hbm] * 4,
        scratch_shapes=[pltpu.SemaphoreType.DMA((4,))],
        compiler_params=pltpu.CompilerParams(vmem_limit_bytes=VMEM_BYTES),
    )(*outs)
    return tuple(out.reshape(out.shape[0], 1, 1, ROWS * 128) for out in outs)


def solution(mesh):
    wide = P(None, "slope", "cross", None)
    flat = P("slope", "cross", None)
    return jax.shard_map(
        per_device,
        mesh=mesh,
        in_specs=(wide, wide, wide, wide, flat, flat, flat),
        out_specs=(wide, wide, wide, wide),
        check_vma=False,
    )
```

```python
import functools

import jax
import jax.numpy as jnp
from jax import lax
from jax.experimental import pallas as pl
from jax.experimental.pallas import tpu as pltpu
from jax.sharding import PartitionSpec as P

STEPS = 5
BLOCKS = 8
ROWS = 32
CHUNKS = 4
TILES = 4
VMEM_BYTES = 40 * 1024 * 1024
MESH = pl.DeviceIdType.MESH

time_step = 0.02
shear_modulus = 4.0
lame_lambda = 4.0
hardening = 10.0
mass_floor = 0.25
gravity_slope = 1.5
gravity_vertical = -2.5
CENTRE = 2.5

DIRECTIONS = [(-1, -1), (1, 1), (-1, 1), (1, -1), (0, -1), (0, 1), (-1, 0), (1, 0)]


def iota(shape, dim):
    return lax.broadcasted_iota(jnp.int32, shape, dim)


def axis_weights(position):
    base = jnp.floor(position + 0.5)
    dist = position - base
    lower = 0.5 * (0.5 - dist) * (0.5 - dist)
    middle = 0.75 - dist * dist
    upper = 0.5 * (0.5 + dist) * (0.5 + dist)
    at = {e: base == float(e) for e in range(-1, 7)}
    return [
        jnp.where(at[e], middle, jnp.where(at[e + 1], lower, jnp.where(at[e - 1], upper, 0.0)))
        for e in range(6)
    ]


def split(values):
    high = values.astype(jnp.bfloat16)
    low = (values - high.astype(jnp.float32)).astype(jnp.bfloat16)
    return high, low


def kernel(
    nx, ny,
    counts_hbm, off_hbm, vel_hbm, aff_hbm, strain_hbm, mass_hbm, plastic_hbm,
    off, vel, aff, frame,
    counts, strain_in, mass_in, plastic_in, live_ref, mw_ref, hard_ref, wx, side_rows, plane_rows, pairs, bs, sides, us,
    gathered, counted,
    send_x, send_low, send_high, recv_x, recv_low, recv_high, diag_low, diag_high,
    load_sem, send_sem, recv_sem,
):
    ix = lax.axis_index("slope")
    iy = lax.axis_index("cross")

    def neighbour(dx, dy):
        return ix + dx, iy + dy

    def present(dx, dy):
        ok = None
        for d, i, n in ((dx, ix, nx), (dy, iy, ny)):
            if d != 0:
                here = (i + d >= 0) & (i + d < n)
                ok = here if ok is None else ok & here
        return ok

    inside = (ix > 0) & (ix < nx - 1) & (iy > 0) & (iy < ny - 1)

    def each_neighbour(act):
        @pl.when(inside)
        def _():
            for d in range(8):
                act(d)

        @pl.when(jnp.logical_not(inside))
        def _():
            for d, (dx, dy) in enumerate(DIRECTIONS):

                @pl.when(present(dx, dy))
                def _():
                    act(d)

    loads = [
        pltpu.make_async_copy(source, target, load_sem.at[i])
        for i, (source, target) in enumerate((
            (counts_hbm, counts), (mass_hbm, mass_in), (plastic_hbm, plastic_in), (off_hbm, off),
            (vel_hbm, vel), (aff_hbm, aff), (strain_hbm, strain_in),
        ))
    ]
    for ref in (recv_x, recv_low, recv_high, diag_low, diag_high):
        ref[...] = jnp.zeros(ref.shape, ref.dtype)
    barrier = pltpu.get_barrier_semaphore()
    around = jnp.int32(0)
    for dx, dy in DIRECTIONS:
        ok = present(dx, dy)
        around = around + jnp.where(ok, 1, 0).astype(jnp.int32)

        @pl.when(ok)
        def _():
            pl.semaphore_signal(barrier, inc=1, device_id=neighbour(dx, dy), device_id_type=MESH)

    for load in loads:
        load.start()
    for ref in (side_rows, plane_rows, us, bs):
        ref[...] = jnp.zeros(ref.shape, ref.dtype)
    for load in loads:
        load.wait()
    row = iota((ROWS, 128), 0)
    slot = (row % CHUNKS) * 128 + iota((ROWS, 128), 1)
    limit = jnp.zeros((ROWS, 128), jnp.int32)
    for k in range(BLOCKS):
        limit = jnp.where(row // CHUNKS == k, counts[k], limit)
    live = jnp.where(slot < limit, 1.0, 0.0).astype(jnp.float32)
    live_ref[...] = live
    mw_ref[...] = mass_in[...] * live
    hard_ref[...] = 4.0 * time_step * live * jnp.exp(hardening * (1.0 - plastic_in[...]))
    for i in range(9):
        frame[i] = strain_in[i] + (1.0 if i % 4 == 0 else 0.0)

    lane = iota((8, 128), 1)
    sub = iota((8, 128), 0)
    half = lane < 64
    r3 = lane % 8
    e2 = (lane % 64) // 8
    e3 = jnp.where(half, r3, (r3 + 4) % 8)
    ex = sub.astype(jnp.float32) - CENTRE
    ey = e2.astype(jnp.float32) - CENTRE
    ez = e3.astype(jnp.float32) - CENTRE
    own = half | (r3 >= 4)
    group = (lane % 64) // 16
    own_tile = half == (r3 >= 4)
    ez_even = r3.astype(jnp.float32) - CENTRE
    ez_odd = ((r3 + 4) % 8).astype(jnp.float32) - CENTRE
    zero = jnp.zeros((8, 128), jnp.float32)
    place_x = 4 * ix + sub
    place_y = 4 * iy + e2
    outside = (place_x >= 4 * nx) | (place_y >= 4 * ny)

    def copy_to(step, d):
        dx, dy = DIRECTIONS[d]
        if dy == 0:
            source, target = send_x, recv_x
        elif dx == 0:
            source, target = (send_low, recv_high) if dy < 0 else (send_high, recv_low)
        else:
            source, target = (send_low, diag_high) if dy < 0 else (send_high, diag_low)
        if dx == 0:
            here, there = pl.ds(0, 6), pl.ds(0, 6)
        else:
            here, there = pl.ds(0 if dx < 0 else 4, 2), pl.ds(4 if dx < 0 else 0, 2)
        return pltpu.make_async_remote_copy(
            src_ref=source.at[step, :, here, :], dst_ref=target.at[step, :, there, :],
            send_sem=send_sem, recv_sem=recv_sem.at[step],
            device_id=neighbour(dx, dy), device_id_type=MESH,
        )

    def passed(sem, rows):
        pltpu.make_async_copy(counted.at[pl.ds(0, rows), :], counted.at[pl.ds(0, rows), :], sem).wait()

    def each_edge(act):
        side_x = (ix == 0) | (ix == nx - 1)
        side_y = (iy == 0) | (iy == ny - 1)
        for at_x, at_y, rows in ((0, 0, 72), (1, 0, 48), (0, 1, 52), (1, 1, 32)):

            @pl.when((side_x == bool(at_x)) & (side_y == bool(at_y)))
            def _():
                act(rows)

    def terms(j):
        rows = pl.ds(8 * j, 8)
        o, f, v, c = (
            [ref[i, rows, :] for i in range(n)] for ref, n in ((off, 3), (frame, 9), (vel, 3), (aff, 9))
        )
        det = (
            f[0] * (f[4] * f[8] - f[5] * f[7])
            - f[1] * (f[3] * f[8] - f[5] * f[6])
            + f[2] * (f[3] * f[7] - f[4] * f[6])
        )
        bulk = lame_lambda * (det - 1.0) * det
        mw = mw_ref[rows, :]
        hard = hard_ref[rows, :]
        pull = [[None] * 3 for _ in range(3)]
        for a in range(3):
            for b in range(a, 3):
                stretch = f[3 * a] * f[3 * b] + f[3 * a + 1] * f[3 * b + 1] + f[3 * a + 2] * f[3 * b + 2]
                if a == b:
                    tau = hard * (shear_modulus * (stretch - 1.0) + bulk)
                else:
                    tau = hard * (shear_modulus * stretch)
                pull[a][b] = mw * c[3 * a + b] - tau
                if a != b:
                    pull[b][a] = mw * c[3 * b + a] - tau
        push = []
        for a in range(3):
            moved = (
                pull[a][0] * (o[0] - CENTRE) + pull[a][1] * (o[1] - CENTRE) + pull[a][2] * (o[2] - CENTRE)
            )
            push.append(mw * v[a] - moved)
        return mw, push, pull, [axis_weights(o[i]) for i in range(3)]

    def deposit_tile(j):
        mw, push, pull, weights = terms(j)
        for e in range(6):
            at = weights[0][e]
            wx[j, e] = at
            side = [mw]
            side += [push[a] + (e - CENTRE) * pull[a][0] for a in range(3)]
            side += [pull[a][b] for b in (1, 2) for a in range(3)]
            for i, value in enumerate(side):
                side_rows[j, pl.ds(8 * (6 * i + e), 8), :] = value * at
        for e in range(6):
            for z in range(6):
                value = weights[1][e] * weights[2][z]
                plane_rows[j, 0, pl.ds(8 * (8 * e + z), 8), :] = value
                plane_rows[j, 1, pl.ds(8 * (8 * e + (z + 4) % 8), 8), :] = value
        totals = []
        for odd in range(2):
            k = 2 * j + odd
            for c in range(CHUNKS):
                s = CHUNKS * odd + c
                lanes = pl.ds(128 * c, 128)
                high, low = split(plane_rows[j, odd, pl.ds(s, 48, stride=8), :])
                bs[k, 0:48, lanes] = high
                bs[k, 64:112, lanes] = low
                high, low = split(side_rows[j, pl.ds(s, 64, stride=8), :])
                sides[k, 0:64, lanes] = high
                sides[k, 64:128, lanes] = low
            dots = lax.dot_general(
                sides[k], bs[k], (((1,), (1,)), ((), ())), preferred_element_type=jnp.float32
            )
            totals.append(dots[:64] + dots[64:])
        for i in range(8):
            one, two = totals[0][8 * i : 8 * i + 8], totals[1][8 * i : 8 * i + 8]
            pairs[j, pl.ds(8 * i, 8), :] = jnp.where(half, one, two) + pltpu.roll(
                jnp.where(half, two, one), 64, 1
            )
        pair = [pairs[j, pl.ds(6 * i, 8), :] for i in range(10)]
        return [pair[0]] + [pair[1 + a] + ey * pair[4 + a] + ez * pair[7 + a] for a in range(3)]

    def turned_sum(near, far, shift):
        kept = near if shift == 0 else pltpu.roll(near, shift % 128, 1)
        return kept + pltpu.roll(far, (shift + 64) % 128, 1)

    def send(step, p, before, first, second):
        low, high = zero, zero
        for i in range(4):
            one = jnp.where(own, first[i], before[i])
            two = jnp.where(own, second[i], first[i])
            near, far = jnp.where(half, one, two), jnp.where(half, two, one)
            send_x[step, 4 * p + i] = turned_sum(near, far, 0)
            to_low = turned_sum(near, far, 16 * i)
            to_high = turned_sum(near, far, 16 * i - 32)
            low = jnp.where(group == i, to_low, low)
            high = jnp.where(group == i, to_high, high)
        send_low[step, p] = low
        send_high[step, p] = high

    def grid_speed(step, p):
        below = recv_low[step, p] + diag_low[step, p]
        above = recv_high[step, p] + diag_high[step, p]
        total = []
        for i in range(4):
            from_low = below if i == 0 else pltpu.roll(below, 128 - 16 * i, 1)
            shift = (32 - 16 * i) % 128
            from_high = above if shift == 0 else pltpu.roll(above, shift, 1)
            extra = jnp.where(group == 0, from_low, jnp.where(group == 2, from_high, 0.0))
            total.append(send_x[step, 4 * p + i] + recv_x[step, 4 * p + i] + extra)
        scale = 1.0 / jnp.maximum(total[0], mass_floor)
        speed_x = total[1] * scale + time_step * gravity_slope
        speed_y = total[2] * scale
        speed_z = total[3] * scale + time_step * gravity_vertical
        place_z = 16 * p + jnp.where(half, 0, 8) + r3
        speed_x = jnp.where(place_x < 2, jnp.maximum(speed_x, 0.0), speed_x)
        speed_x = jnp.where(place_x >= 4 * nx - 2, jnp.minimum(speed_x, 0.0), speed_x)
        speed_y = jnp.where(place_y < 2, jnp.maximum(speed_y, 0.0), speed_y)
        speed_y = jnp.where(place_y >= 4 * ny - 2, jnp.minimum(speed_y, 0.0), speed_y)
        speed_z = jnp.where(place_z >= 8 * TILES - 2, jnp.minimum(speed_z, 0.0), speed_z)
        still = outside | (place_z < 2)
        return [jnp.where(still, 0.0, speed) for speed in (speed_x, speed_y, speed_z)]

    def windows(k, speed, turned, beyond, beyond_turned):
        for a in range(3):
            first, second = (speed[a], turned[a]) if k % 4 < 2 else (turned[a], speed[a])
            if k % 2 == 0:
                window = jnp.where(half, first, second)
            elif k % 4 == 1:
                window = jnp.where(own_tile, first, second)
            else:
                window = jnp.where(
                    r3 >= 4,
                    jnp.where(half, first, second),
                    jnp.where(half, beyond[a], beyond_turned[a]),
                )
            for b, factor in enumerate((None, ex, ey, ez_odd if k % 2 else ez_even)):
                q = 3 * b + a
                value = window if factor is None else window * factor
                us[k, pl.ds(q, 8, stride=12), :] = value

    def gather(k):
        left = jnp.concatenate(split(us[k, 0:80, :]), axis=1)
        planes = bs[k]
        taken = lax.dot_general(
            left, jnp.concatenate([planes, planes], axis=0),
            (((1,), (0,)), ((), ())), preferred_element_type=jnp.float32,
        )
        for c in range(CHUNKS):
            s = CHUNKS * (k % 2) + c
            gathered[k // 2, pl.ds(s, 72, stride=8), :] = taken[:72, 128 * c : 128 * c + 128]

    def advance(j, last):
        rows = pl.ds(8 * j, 8)
        weights = [wx[j, e] for e in range(6)]

        def quantity(q):
            value = weights[0] * gathered[j, pl.ds(8 * q, 8), :]
            for e in range(1, 6):
                value = value + weights[e] * gathered[j, pl.ds(8 * (12 * e + q), 8), :]
            return value

        o = [off[i, rows, :] for i in range(3)]
        f = [frame[i, rows, :] for i in range(9)]
        v = [quantity(a) for a in range(3)]
        c = [None] * 9
        for a in range(3):
            for b in range(3):
                c[3 * a + b] = 4.0 * (quantity(3 + 3 * b + a) - v[a] * (o[b] - CENTRE))
        o = [o[a] + time_step * v[a] for a in range(3)]
        f = [
            f[3 * a + b]
            + time_step * (c[3 * a] * f[b] + c[3 * a + 1] * f[3 + b] + c[3 * a + 2] * f[6 + b])
            for a in range(3)
            for b in range(3)
        ]
        live_now = live_ref[rows, :]
        for ref, values in ((off, o), (vel, v), (aff, c), (frame, f)):
            for i, value in enumerate(values):
                ref[i, rows, :] = value * live_now if last else value

    def turn(values):
        return [pltpu.roll(value, 64, 1) for value in values]

    def send_all(step, fields):
        send(step, 0, [zero] * 4, fields[0], fields[1])
        send(step, 1, fields[1], fields[2], fields[3])

    def start_all(step):
        each_neighbour(lambda d: copy_to(step, d).start())

    def take(step, last):
        each_edge(lambda rows: passed(recv_sem.at[step], rows))
        speed = [grid_speed(step, p) for p in range(2)] + [[zero] * 3]
        turned = [turn(speed[0]), turn(speed[1]), [zero] * 3]
        fields = []
        for j in range(TILES):
            p = j // 2
            for k in (2 * j, 2 * j + 1):
                windows(k, speed[p], turned[p], speed[p + 1], turned[p + 1])
                gather(k)
            advance(j, last)
            if not last:
                fields.append(deposit_tile(j))
        return fields

    def one_step(step, carry):
        send_all(step + 1, take(step, False))
        start_all(step + 1)
        return carry

    send_all(0, [deposit_tile(j) for j in range(TILES)])
    pl.semaphore_wait(barrier, around)
    start_all(0)
    lax.fori_loop(0, STEPS - 1, one_step, 0)
    take(STEPS - 1, True)

    each_edge(lambda rows: passed(send_sem, STEPS * rows))


def write_out(off, vel, aff, frame, off_out, vel_out, aff_out, frame_out, sem):
    copies = [
        pltpu.make_async_copy(source, target, sem.at[i])
        for i, (source, target) in enumerate(
            ((aff, aff_out), (frame, frame_out), (off, off_out), (vel, vel_out))
        )
    ]
    for copy in copies:
        copy.start()
    for copy in copies:
        copy.wait()


def per_device(offsets, velocity, affine, strain, particle_mass, plastic_ratio, block_counts):
    nx, ny = lax.axis_size("slope"), lax.axis_size("cross")
    f32 = jnp.float32
    vmem = pl.BlockSpec(memory_space=pltpu.VMEM)
    hbm = pl.BlockSpec(memory_space=pltpu.HBM)
    outs = pl.pallas_call(
        functools.partial(kernel, nx, ny),
        out_shape=[jax.ShapeDtypeStruct((n, ROWS, 128), f32) for n in (3, 3, 9, 9)],
        in_specs=[hbm] * 7,
        out_specs=[vmem] * 4,
        scratch_shapes=[
            pltpu.SMEM((BLOCKS,), jnp.int32),
            pltpu.VMEM((9, ROWS, 128), f32),
            pltpu.VMEM((ROWS, 128), f32),
            pltpu.VMEM((ROWS, 128), f32),
            pltpu.VMEM((ROWS, 128), f32),
            pltpu.VMEM((ROWS, 128), f32),
            pltpu.VMEM((ROWS, 128), f32),
            pltpu.VMEM((TILES, 6, 8, 128), f32),
            pltpu.VMEM((TILES, 512, 128), f32),
            pltpu.VMEM((TILES, 2, 384, 128), f32),
            pltpu.VMEM((TILES, 64, 128), f32),
            pltpu.VMEM((BLOCKS, 128, 512), jnp.bfloat16),
            pltpu.VMEM((BLOCKS, 128, 512), jnp.bfloat16),
            pltpu.VMEM((BLOCKS, 96, 128), f32),
            pltpu.VMEM((TILES, 576, 128), f32),
            pltpu.VMEM((STEPS * 72, 128), f32),
            pltpu.VMEM((STEPS, 8, 8, 128), f32),
            pltpu.VMEM((STEPS, 2, 8, 128), f32),
            pltpu.VMEM((STEPS, 2, 8, 128), f32),
            pltpu.VMEM((STEPS, 8, 8, 128), f32),
            pltpu.VMEM((STEPS, 2, 8, 128), f32),
            pltpu.VMEM((STEPS, 2, 8, 128), f32),
            pltpu.VMEM((STEPS, 2, 8, 128), f32),
            pltpu.VMEM((STEPS, 2, 8, 128), f32),
            pltpu.SemaphoreType.DMA((7,)),
            pltpu.SemaphoreType.DMA,
            pltpu.SemaphoreType.DMA((STEPS,)),
        ],
        compiler_params=pltpu.CompilerParams(
            collective_id=0, has_side_effects=True, vmem_limit_bytes=VMEM_BYTES
        ),
    )(
        *(
            pltpu.with_memory_space_constraint(value, pltpu.HBM)
            for value in (
                block_counts.reshape(BLOCKS),
                offsets.reshape(3, ROWS, 128),
                velocity.reshape(3, ROWS, 128),
                affine.reshape(9, ROWS, 128),
                strain.reshape(9, ROWS, 128),
                particle_mass.reshape(ROWS, 128),
                plastic_ratio.reshape(ROWS, 128),
            )
        ),
    )
    outs = pl.pallas_call(
        write_out,
        out_shape=[jax.ShapeDtypeStruct(out.shape, f32) for out in outs],
        in_specs=[vmem] * 4,
        out_specs=[hbm] * 4,
        scratch_shapes=[pltpu.SemaphoreType.DMA((4,))],
        compiler_params=pltpu.CompilerParams(vmem_limit_bytes=VMEM_BYTES),
    )(*outs)
    return tuple(out.reshape(out.shape[0], 1, 1, ROWS * 128) for out in outs)


def solution(mesh):
    wide = P(None, "slope", "cross", None)
    flat = P("slope", "cross", None)
    return jax.shard_map(
        per_device,
        mesh=mesh,
        in_specs=(wide, wide, wide, wide, flat, flat, flat),
        out_specs=(wide, wide, wide, wide),
        check_vma=False,
    )
```

```python
import functools

import jax
import jax.numpy as jnp
from jax import lax
from jax.experimental import pallas as pl
from jax.experimental.pallas import tpu as pltpu
from jax.sharding import PartitionSpec as P

STEPS = 5
BLOCKS = 8
ROWS = 32
CHUNKS = 4
TILES = 4
VMEM_BYTES = 40 * 1024 * 1024
MESH = pl.DeviceIdType.MESH

time_step = 0.02
shear_modulus = 4.0
lame_lambda = 4.0
hardening = 10.0
mass_floor = 0.25
gravity_slope = 1.5
gravity_vertical = -2.5
CENTRE = 2.5

DIRECTIONS = [(0, -1), (0, 1), (-1, -1), (-1, 1), (1, -1), (1, 1), (-1, 0), (1, 0)]


def iota(shape, dim):
    return lax.broadcasted_iota(jnp.int32, shape, dim)


def axis_weights(position):
    base = jnp.floor(position + 0.5)
    dist = position - base
    lower = 0.5 * (0.5 - dist) * (0.5 - dist)
    middle = 0.75 - dist * dist
    upper = 0.5 * (0.5 + dist) * (0.5 + dist)
    at = {e: base == float(e) for e in range(-1, 7)}
    return [
        jnp.where(at[e], middle, jnp.where(at[e + 1], lower, jnp.where(at[e - 1], upper, 0.0)))
        for e in range(6)
    ]


def split(values):
    high = values.astype(jnp.bfloat16)
    low = (values - high.astype(jnp.float32)).astype(jnp.bfloat16)
    return high, low


def kernel(
    nx, ny,
    counts_hbm, off_hbm, vel_hbm, aff_hbm, strain_hbm, mass_hbm, plastic_hbm,
    off, vel, aff, frame,
    counts, strain_in, mass_in, plastic_in, live_ref, mw_ref, hard_ref, wx, side_rows, plane_rows, pairs, bs, sides, us,
    gathered, counted,
    send_x, send_low, send_high, recv_x, recv_low, recv_high, diag_low, diag_high,
    load_sem, send_sem, recv_sem,
):
    ix = lax.axis_index("slope")
    iy = lax.axis_index("cross")

    def neighbour(dx, dy):
        return ix + dx, iy + dy

    def present(dx, dy):
        ok = None
        for d, i, n in ((dx, ix, nx), (dy, iy, ny)):
            if d != 0:
                here = (i + d >= 0) & (i + d < n)
                ok = here if ok is None else ok & here
        return ok

    inside = (ix > 0) & (ix < nx - 1) & (iy > 0) & (iy < ny - 1)

    def each_neighbour(act):
        @pl.when(inside)
        def _():
            for d in range(8):
                act(d)

        @pl.when(jnp.logical_not(inside))
        def _():
            for d, (dx, dy) in enumerate(DIRECTIONS):

                @pl.when(present(dx, dy))
                def _():
                    act(d)

    loads = [
        pltpu.make_async_copy(source, target, load_sem.at[i])
        for i, (source, target) in enumerate((
            (counts_hbm, counts), (mass_hbm, mass_in), (plastic_hbm, plastic_in), (off_hbm, off),
            (vel_hbm, vel), (aff_hbm, aff), (strain_hbm, strain_in),
        ))
    ]
    def clear_step(step, carry):
        for ref in (recv_x, recv_low, recv_high, diag_low, diag_high):
            ref[step] = jnp.zeros(ref.shape[1:], ref.dtype)
        return carry

    lax.fori_loop(0, STEPS, clear_step, 0)
    barrier = pltpu.get_barrier_semaphore()
    around = jnp.int32(0)
    for dx, dy in DIRECTIONS:
        ok = present(dx, dy)
        around = around + jnp.where(ok, 1, 0).astype(jnp.int32)

        @pl.when(ok)
        def _():
            pl.semaphore_signal(barrier, inc=1, device_id=neighbour(dx, dy), device_id_type=MESH)

    for load in loads:
        load.start()
    blank = jnp.zeros((8, 128), jnp.float32)

    def clear_tile(j, carry):
        side_rows[j, 480:512, :] = jnp.zeros((32, 128), jnp.float32)
        for odd in range(2):
            for e in range(6):
                for z in (6, 7):
                    plane_rows[j, odd, pl.ds(8 * (8 * e + (z + 4 * odd) % 8), 8), :] = blank
            for at in (48, 112):
                bs[2 * j + odd, at : at + 16, :] = jnp.zeros((16, 512), jnp.bfloat16)
        return carry

    lax.fori_loop(0, TILES, clear_tile, 0)
    for load in loads:
        load.wait()
    row = iota((ROWS, 128), 0)
    slot = (row % CHUNKS) * 128 + iota((ROWS, 128), 1)
    limit = jnp.zeros((ROWS, 128), jnp.int32)
    for k in range(BLOCKS):
        limit = jnp.where(row // CHUNKS == k, counts[k], limit)
    live = jnp.where(slot < limit, 1.0, 0.0).astype(jnp.float32)
    live_ref[...] = live
    mw_ref[...] = mass_in[...] * live
    hard_ref[...] = 4.0 * time_step * live * jnp.exp(hardening * (1.0 - plastic_in[...]))
    for i in range(9):
        frame[i] = strain_in[i] + (1.0 if i % 4 == 0 else 0.0)

    lane = iota((8, 128), 1)
    sub = iota((8, 128), 0)
    half = lane < 64
    r3 = lane % 8
    e2 = (lane % 64) // 8
    e3 = jnp.where(half, r3, (r3 + 4) % 8)
    ex = sub.astype(jnp.float32) - CENTRE
    ey = e2.astype(jnp.float32) - CENTRE
    ez = e3.astype(jnp.float32) - CENTRE
    own = half | (r3 >= 4)
    group = (lane % 64) // 16
    own_tile = half == (r3 >= 4)
    ez_even = r3.astype(jnp.float32) - CENTRE
    ez_odd = ((r3 + 4) % 8).astype(jnp.float32) - CENTRE
    zero = jnp.zeros((8, 128), jnp.float32)
    place_x = 4 * ix + sub
    place_y = 4 * iy + e2
    outside = (place_x >= 4 * nx) | (place_y >= 4 * ny)

    def copy_to(step, d):
        dx, dy = DIRECTIONS[d]
        if dy == 0:
            source, target = send_x, recv_x
        elif dx == 0:
            source, target = (send_low, recv_high) if dy < 0 else (send_high, recv_low)
        else:
            source, target = (send_low, diag_high) if dy < 0 else (send_high, diag_low)
        if dx == 0:
            here, there = pl.ds(0, 6), pl.ds(0, 6)
        else:
            here, there = pl.ds(0 if dx < 0 else 4, 2), pl.ds(4 if dx < 0 else 0, 2)
        return pltpu.make_async_remote_copy(
            src_ref=source.at[step, :, here, :], dst_ref=target.at[step, :, there, :],
            send_sem=send_sem, recv_sem=recv_sem.at[step],
            device_id=neighbour(dx, dy), device_id_type=MESH,
        )

    def passed(sem, rows):
        pltpu.make_async_copy(counted.at[pl.ds(0, rows), :], counted.at[pl.ds(0, rows), :], sem).wait()

    def each_edge(act):
        side_x = (ix == 0) | (ix == nx - 1)
        side_y = (iy == 0) | (iy == ny - 1)
        for at_x, at_y, rows in ((0, 0, 72), (1, 0, 48), (0, 1, 52), (1, 1, 32)):

            @pl.when((side_x == bool(at_x)) & (side_y == bool(at_y)))
            def _():
                act(rows)

    def terms(j):
        rows = pl.ds(8 * j, 8)
        o, f, v, c = (
            [ref[i, rows, :] for i in range(n)] for ref, n in ((off, 3), (frame, 9), (vel, 3), (aff, 9))
        )
        det = (
            f[0] * (f[4] * f[8] - f[5] * f[7])
            - f[1] * (f[3] * f[8] - f[5] * f[6])
            + f[2] * (f[3] * f[7] - f[4] * f[6])
        )
        bulk = lame_lambda * (det - 1.0) * det
        mw = mw_ref[rows, :]
        hard = hard_ref[rows, :]
        pull = [[None] * 3 for _ in range(3)]
        for a in range(3):
            for b in range(a, 3):
                stretch = f[3 * a] * f[3 * b] + f[3 * a + 1] * f[3 * b + 1] + f[3 * a + 2] * f[3 * b + 2]
                if a == b:
                    tau = hard * (shear_modulus * (stretch - 1.0) + bulk)
                else:
                    tau = hard * (shear_modulus * stretch)
                pull[a][b] = mw * c[3 * a + b] - tau
                if a != b:
                    pull[b][a] = mw * c[3 * b + a] - tau
        push = []
        for a in range(3):
            moved = (
                pull[a][0] * (o[0] - CENTRE) + pull[a][1] * (o[1] - CENTRE) + pull[a][2] * (o[2] - CENTRE)
            )
            push.append(mw * v[a] - moved)
        return mw, push, pull, [axis_weights(o[i]) for i in range(3)]

    def deposit_tile(j):
        mw, push, pull, weights = terms(j)
        for e in range(6):
            at = weights[0][e]
            wx[j, e] = at
            side = [mw]
            side += [push[a] + (e - CENTRE) * pull[a][0] for a in range(3)]
            side += [pull[a][b] for b in (1, 2) for a in range(3)]
            for i, value in enumerate(side):
                side_rows[j, pl.ds(8 * (6 * i + e), 8), :] = value * at
        for e in range(6):
            for z in range(6):
                value = weights[1][e] * weights[2][z]
                plane_rows[j, 0, pl.ds(8 * (8 * e + z), 8), :] = value
                plane_rows[j, 1, pl.ds(8 * (8 * e + (z + 4) % 8), 8), :] = value
        totals = []
        for odd in range(2):
            k = 2 * j + odd
            for c in range(CHUNKS):
                s = CHUNKS * odd + c
                lanes = pl.ds(128 * c, 128)
                high, low = split(plane_rows[j, odd, pl.ds(s, 48, stride=8), :])
                bs[k, 0:48, lanes] = high
                bs[k, 64:112, lanes] = low
                high, low = split(side_rows[j, pl.ds(s, 64, stride=8), :])
                sides[k, 0:64, lanes] = high
                sides[k, 64:128, lanes] = low
            dots = lax.dot_general(
                sides[k], bs[k], (((1,), (1,)), ((), ())), preferred_element_type=jnp.float32
            )
            totals.append(dots[:64] + dots[64:])
        for i in range(8):
            one, two = totals[0][8 * i : 8 * i + 8], totals[1][8 * i : 8 * i + 8]
            pairs[j, pl.ds(8 * i, 8), :] = jnp.where(half, one, two) + pltpu.roll(
                jnp.where(half, two, one), 64, 1
            )
        pair = [pairs[j, pl.ds(6 * i, 8), :] for i in range(10)]
        return [pair[0]] + [pair[1 + a] + ey * pair[4 + a] + ez * pair[7 + a] for a in range(3)]

    def send(step, p, before, first, second):
        low, high = zero, zero
        for i in range(4):
            one = jnp.where(own, first[i], before[i])
            two = jnp.where(own, second[i], first[i])
            mine = jnp.where(half, one, two) + pltpu.roll(jnp.where(half, two, one), 64, 1)
            send_x[step, 4 * p + i] = mine
            to_low = mine if i == 0 else pltpu.roll(mine, 16 * i, 1)
            shift = (16 * i - 32) % 128
            to_high = mine if shift == 0 else pltpu.roll(mine, shift, 1)
            low = jnp.where(group == i, to_low, low)
            high = jnp.where(group == i, to_high, high)
        send_low[step, p] = low
        send_high[step, p] = high

    def grid_speed(step, p):
        below = recv_low[step, p] + diag_low[step, p]
        above = recv_high[step, p] + diag_high[step, p]
        total = []
        for i in range(4):
            from_low = below if i == 0 else pltpu.roll(below, 128 - 16 * i, 1)
            shift = (32 - 16 * i) % 128
            from_high = above if shift == 0 else pltpu.roll(above, shift, 1)
            extra = jnp.where(group == 0, from_low, jnp.where(group == 2, from_high, 0.0))
            total.append(send_x[step, 4 * p + i] + recv_x[step, 4 * p + i] + extra)
        scale = 1.0 / jnp.maximum(total[0], mass_floor)
        speed_x = total[1] * scale + time_step * gravity_slope
        speed_y = total[2] * scale
        speed_z = total[3] * scale + time_step * gravity_vertical
        place_z = 16 * p + jnp.where(half, 0, 8) + r3
        speed_x = jnp.where(place_x < 2, jnp.maximum(speed_x, 0.0), speed_x)
        speed_x = jnp.where(place_x >= 4 * nx - 2, jnp.minimum(speed_x, 0.0), speed_x)
        speed_y = jnp.where(place_y < 2, jnp.maximum(speed_y, 0.0), speed_y)
        speed_y = jnp.where(place_y >= 4 * ny - 2, jnp.minimum(speed_y, 0.0), speed_y)
        speed_z = jnp.where(place_z >= 8 * TILES - 2, jnp.minimum(speed_z, 0.0), speed_z)
        still = outside | (place_z < 2)
        return [jnp.where(still, 0.0, speed) for speed in (speed_x, speed_y, speed_z)]

    def windows(k, speed, turned, beyond, beyond_turned):
        for a in range(3):
            first, second = (speed[a], turned[a]) if k % 4 < 2 else (turned[a], speed[a])
            if k % 2 == 0:
                window = jnp.where(half, first, second)
            elif k % 4 == 1:
                window = jnp.where(own_tile, first, second)
            else:
                window = jnp.where(
                    r3 >= 4,
                    jnp.where(half, first, second),
                    jnp.where(half, beyond[a], beyond_turned[a]),
                )
            for b, factor in enumerate((None, ex, ey, ez_odd if k % 2 else ez_even)):
                q = 3 * b + a
                value = window if factor is None else window * factor
                us[k, pl.ds(q, 8, stride=12), :] = value

    def gather(k):
        left = jnp.concatenate(split(us[k, 0:80, :]), axis=1)
        planes = bs[k]
        taken = lax.dot_general(
            left, jnp.concatenate([planes, planes], axis=0),
            (((1,), (0,)), ((), ())), preferred_element_type=jnp.float32,
        )
        for c in range(CHUNKS):
            s = CHUNKS * (k % 2) + c
            gathered[k // 2, pl.ds(s, 72, stride=8), :] = taken[:72, 128 * c : 128 * c + 128]

    def advance(j, step):
        rows = pl.ds(8 * j, 8)
        weights = [wx[j, e] for e in range(6)]

        def quantity(q):
            value = weights[0] * gathered[j, pl.ds(8 * q, 8), :]
            for e in range(1, 6):
                value = value + weights[e] * gathered[j, pl.ds(8 * (12 * e + q), 8), :]
            return value

        o = [off[i, rows, :] for i in range(3)]
        f = [frame[i, rows, :] for i in range(9)]
        v = [quantity(a) for a in range(3)]
        c = [None] * 9
        for a in range(3):
            for b in range(3):
                c[3 * a + b] = 4.0 * (quantity(3 + 3 * b + a) - v[a] * (o[b] - CENTRE))
        o = [o[a] + time_step * v[a] for a in range(3)]
        f = [
            f[3 * a + b]
            + time_step * (c[3 * a] * f[b] + c[3 * a + 1] * f[3 + b] + c[3 * a + 2] * f[6 + b])
            for a in range(3)
            for b in range(3)
        ]
        scale = jnp.where(step == STEPS - 1, live_ref[rows, :], 1.0)
        for ref, values in ((off, o), (vel, v), (aff, c), (frame, f)):
            for i, value in enumerate(values):
                ref[i, rows, :] = value * scale

    def turn(values):
        return [pltpu.roll(value, 64, 1) for value in values]

    def one_step(step, carry):
        fields = [deposit_tile(j) for j in range(TILES)]
        send(step, 0, [zero] * 4, fields[0], fields[1])
        send(step, 1, fields[1], fields[2], fields[3])

        @pl.when(step == 0)
        def _():
            pl.semaphore_wait(barrier, around)

        each_neighbour(lambda d: copy_to(step, d).start())

        each_edge(lambda rows: passed(recv_sem.at[step], rows))
        speed = [grid_speed(step, p) for p in range(2)] + [[zero] * 3]
        turned = [turn(speed[0]), turn(speed[1]), [zero] * 3]
        for k in range(BLOCKS):
            p = k // 4
            windows(k, speed[p], turned[p], speed[p + 1], turned[p + 1])
        for k in range(BLOCKS):
            gather(k)
        for j in range(TILES):
            advance(j, step)
        return carry

    lax.fori_loop(0, STEPS, one_step, 0)

    each_edge(lambda rows: passed(send_sem, STEPS * rows))


def write_out(off, vel, aff, frame, off_out, vel_out, aff_out, frame_out, sem):
    copies = [
        pltpu.make_async_copy(source, target, sem.at[i])
        for i, (source, target) in enumerate(
            ((aff, aff_out), (frame, frame_out), (off, off_out), (vel, vel_out))
        )
    ]
    for copy in copies:
        copy.start()
    for copy in copies:
        copy.wait()


def per_device(offsets, velocity, affine, strain, particle_mass, plastic_ratio, block_counts):
    nx, ny = lax.axis_size("slope"), lax.axis_size("cross")
    f32 = jnp.float32
    vmem = pl.BlockSpec(memory_space=pltpu.VMEM)
    hbm = pl.BlockSpec(memory_space=pltpu.HBM)
    outs = pl.pallas_call(
        functools.partial(kernel, nx, ny),
        out_shape=[jax.ShapeDtypeStruct((n, ROWS, 128), f32) for n in (3, 3, 9, 9)],
        in_specs=[hbm] * 7,
        out_specs=[vmem] * 4,
        scratch_shapes=[
            pltpu.SMEM((BLOCKS,), jnp.int32),
            pltpu.VMEM((9, ROWS, 128), f32),
            pltpu.VMEM((ROWS, 128), f32),
            pltpu.VMEM((ROWS, 128), f32),
            pltpu.VMEM((ROWS, 128), f32),
            pltpu.VMEM((ROWS, 128), f32),
            pltpu.VMEM((ROWS, 128), f32),
            pltpu.VMEM((TILES, 6, 8, 128), f32),
            pltpu.VMEM((TILES, 512, 128), f32),
            pltpu.VMEM((TILES, 2, 384, 128), f32),
            pltpu.VMEM((TILES, 64, 128), f32),
            pltpu.VMEM((BLOCKS, 128, 512), jnp.bfloat16),
            pltpu.VMEM((BLOCKS, 128, 512), jnp.bfloat16),
            pltpu.VMEM((BLOCKS, 96, 128), f32),
            pltpu.VMEM((TILES, 576, 128), f32),
            pltpu.VMEM((STEPS * 72, 128), f32),
            pltpu.VMEM((STEPS, 8, 8, 128), f32),
            pltpu.VMEM((STEPS, 2, 8, 128), f32),
            pltpu.VMEM((STEPS, 2, 8, 128), f32),
            pltpu.VMEM((STEPS, 8, 8, 128), f32),
            pltpu.VMEM((STEPS, 2, 8, 128), f32),
            pltpu.VMEM((STEPS, 2, 8, 128), f32),
            pltpu.VMEM((STEPS, 2, 8, 128), f32),
            pltpu.VMEM((STEPS, 2, 8, 128), f32),
            pltpu.SemaphoreType.DMA((7,)),
            pltpu.SemaphoreType.DMA,
            pltpu.SemaphoreType.DMA((STEPS,)),
        ],
        compiler_params=pltpu.CompilerParams(
            collective_id=0, has_side_effects=True, vmem_limit_bytes=VMEM_BYTES
        ),
    )(
        *(
            pltpu.with_memory_space_constraint(value, pltpu.HBM)
            for value in (
                block_counts.reshape(BLOCKS),
                offsets.reshape(3, ROWS, 128),
                velocity.reshape(3, ROWS, 128),
                affine.reshape(9, ROWS, 128),
                strain.reshape(9, ROWS, 128),
                particle_mass.reshape(ROWS, 128),
                plastic_ratio.reshape(ROWS, 128),
            )
        ),
    )
    outs = pl.pallas_call(
        write_out,
        out_shape=[jax.ShapeDtypeStruct(out.shape, f32) for out in outs],
        in_specs=[vmem] * 4,
        out_specs=[hbm] * 4,
        scratch_shapes=[pltpu.SemaphoreType.DMA((4,))],
        compiler_params=pltpu.CompilerParams(vmem_limit_bytes=VMEM_BYTES),
    )(*outs)
    return tuple(out.reshape(out.shape[0], 1, 1, ROWS * 128) for out in outs)


def solution(mesh):
    wide = P(None, "slope", "cross", None)
    flat = P("slope", "cross", None)
    return jax.shard_map(
        per_device,
        mesh=mesh,
        in_specs=(wide, wide, wide, wide, flat, flat, flat),
        out_specs=(wide, wide, wide, wide),
        check_vma=False,
    )
```

```python
import functools

import jax
import jax.numpy as jnp
from jax import lax
from jax.experimental import pallas as pl
from jax.experimental.pallas import tpu as pltpu
from jax.sharding import PartitionSpec as P

STEPS = 5
BLOCKS = 8
ROWS = 32
CHUNKS = 4
TILES = 4
VMEM_BYTES = 40 * 1024 * 1024
MESH = pl.DeviceIdType.MESH

time_step = 0.02
shear_modulus = 4.0
lame_lambda = 4.0
hardening = 10.0
mass_floor = 0.25
gravity_slope = 1.5
gravity_vertical = -2.5
CENTRE = 2.5

DIRECTIONS = [(0, -1), (0, 1), (-1, -1), (-1, 1), (1, -1), (1, 1), (-1, 0), (1, 0)]


def iota(shape, dim):
    return lax.broadcasted_iota(jnp.int32, shape, dim)


def axis_weights(position):
    base = jnp.floor(position + 0.5)
    dist = position - base
    lower = 0.5 * (0.5 - dist) * (0.5 - dist)
    middle = 0.75 - dist * dist
    upper = 0.5 * (0.5 + dist) * (0.5 + dist)
    at = {e: base == float(e) for e in range(-1, 7)}
    return [
        jnp.where(at[e], middle, jnp.where(at[e + 1], lower, jnp.where(at[e - 1], upper, 0.0)))
        for e in range(6)
    ]


def split(values):
    high = values.astype(jnp.bfloat16)
    low = (values - high.astype(jnp.float32)).astype(jnp.bfloat16)
    return high, low


def kernel(
    nx, ny,
    counts_hbm, off_hbm, vel_hbm, aff_hbm, strain_hbm, mass_hbm, plastic_hbm,
    off, vel, aff, frame,
    counts, strain_in, mass_in, plastic_in, live_ref, mw_ref, hard_ref, wx, side_rows, plane_rows, pairs, bs, sides, us,
    gathered, counted,
    send_x, send_low, send_high, recv_x, recv_low, recv_high, diag_low, diag_high,
    load_sem, send_sem, recv_sem,
):
    ix = lax.axis_index("slope")
    iy = lax.axis_index("cross")

    def neighbour(dx, dy):
        return ix + dx, iy + dy

    def present(dx, dy):
        ok = None
        for d, i, n in ((dx, ix, nx), (dy, iy, ny)):
            if d != 0:
                here = (i + d >= 0) & (i + d < n)
                ok = here if ok is None else ok & here
        return ok

    inside = (ix > 0) & (ix < nx - 1) & (iy > 0) & (iy < ny - 1)

    def each_neighbour(act):
        @pl.when(inside)
        def _():
            for d in range(8):
                act(d)

        @pl.when(jnp.logical_not(inside))
        def _():
            for d, (dx, dy) in enumerate(DIRECTIONS):

                @pl.when(present(dx, dy))
                def _():
                    act(d)

    loads = [
        pltpu.make_async_copy(source, target, load_sem.at[i])
        for i, (source, target) in enumerate((
            (counts_hbm, counts), (mass_hbm, mass_in), (plastic_hbm, plastic_in), (off_hbm, off),
            (vel_hbm, vel), (aff_hbm, aff), (strain_hbm, strain_in),
        ))
    ]
    for load in loads:
        load.start()

    for ref in (recv_x, recv_low, recv_high, diag_low, diag_high):
        ref[...] = jnp.zeros(ref.shape, ref.dtype)
    barrier = pltpu.get_barrier_semaphore()
    around = jnp.int32(0)
    for dx, dy in DIRECTIONS:
        ok = present(dx, dy)
        around = around + jnp.where(ok, 1, 0).astype(jnp.int32)

        @pl.when(ok)
        def _():
            pl.semaphore_signal(barrier, inc=1, device_id=neighbour(dx, dy), device_id_type=MESH)

    for ref in (side_rows, plane_rows, us, bs):
        ref[...] = jnp.zeros(ref.shape, ref.dtype)
    for load in loads:
        load.wait()
    row = iota((ROWS, 128), 0)
    slot = (row % CHUNKS) * 128 + iota((ROWS, 128), 1)
    limit = jnp.zeros((ROWS, 128), jnp.int32)
    for k in range(BLOCKS):
        limit = jnp.where(row // CHUNKS == k, counts[k], limit)
    live = jnp.where(slot < limit, 1.0, 0.0).astype(jnp.float32)
    live_ref[...] = live
    mw_ref[...] = mass_in[...] * live
    hard_ref[...] = 4.0 * time_step * live * jnp.exp(hardening * (1.0 - plastic_in[...]))
    for i in range(9):
        frame[i] = strain_in[i] + (1.0 if i % 4 == 0 else 0.0)

    lane = iota((8, 128), 1)
    sub = iota((8, 128), 0)
    half = lane < 64
    r3 = lane % 8
    e2 = (lane % 64) // 8
    e3 = jnp.where(half, r3, (r3 + 4) % 8)
    ex = sub.astype(jnp.float32) - CENTRE
    ey = e2.astype(jnp.float32) - CENTRE
    ez = e3.astype(jnp.float32) - CENTRE
    own = half | (r3 >= 4)
    group = (lane % 64) // 16
    own_tile = half == (r3 >= 4)
    ez_even = r3.astype(jnp.float32) - CENTRE
    ez_odd = ((r3 + 4) % 8).astype(jnp.float32) - CENTRE
    zero = jnp.zeros((8, 128), jnp.float32)
    place_x = 4 * ix + sub
    place_y = 4 * iy + e2
    outside = (place_x >= 4 * nx) | (place_y >= 4 * ny)

    def copy_to(step, d):
        dx, dy = DIRECTIONS[d]
        if dy == 0:
            source, target = send_x, recv_x
        elif dx == 0:
            source, target = (send_low, recv_high) if dy < 0 else (send_high, recv_low)
        else:
            source, target = (send_low, diag_high) if dy < 0 else (send_high, diag_low)
        if dx == 0:
            here, there = pl.ds(0, 6), pl.ds(0, 6)
        else:
            here, there = pl.ds(0 if dx < 0 else 4, 2), pl.ds(4 if dx < 0 else 0, 2)
        return pltpu.make_async_remote_copy(
            src_ref=source.at[step, :, here, :], dst_ref=target.at[step, :, there, :],
            send_sem=send_sem, recv_sem=recv_sem.at[step],
            device_id=neighbour(dx, dy), device_id_type=MESH,
        )

    def passed(sem, rows):
        pltpu.make_async_copy(counted.at[pl.ds(0, rows), :], counted.at[pl.ds(0, rows), :], sem).wait()

    def each_edge(act):
        side_x = (ix == 0) | (ix == nx - 1)
        side_y = (iy == 0) | (iy == ny - 1)
        for at_x, at_y, rows in ((0, 0, 72), (1, 0, 48), (0, 1, 52), (1, 1, 32)):

            @pl.when((side_x == bool(at_x)) & (side_y == bool(at_y)))
            def _():
                act(rows)

    def terms(j):
        rows = pl.ds(8 * j, 8)
        o, f, v, c = (
            [ref[i, rows, :] for i in range(n)] for ref, n in ((off, 3), (frame, 9), (vel, 3), (aff, 9))
        )
        det = (
            f[0] * (f[4] * f[8] - f[5] * f[7])
            - f[1] * (f[3] * f[8] - f[5] * f[6])
            + f[2] * (f[3] * f[7] - f[4] * f[6])
        )
        bulk = lame_lambda * (det - 1.0) * det
        mw = mw_ref[rows, :]
        hard = hard_ref[rows, :]
        pull = [[None] * 3 for _ in range(3)]
        for a in range(3):
            for b in range(a, 3):
                stretch = f[3 * a] * f[3 * b] + f[3 * a + 1] * f[3 * b + 1] + f[3 * a + 2] * f[3 * b + 2]
                if a == b:
                    tau = hard * (shear_modulus * (stretch - 1.0) + bulk)
                else:
                    tau = hard * (shear_modulus * stretch)
                pull[a][b] = mw * c[3 * a + b] - tau
                if a != b:
                    pull[b][a] = mw * c[3 * b + a] - tau
        push = []
        for a in range(3):
            moved = (
                pull[a][0] * (o[0] - CENTRE) + pull[a][1] * (o[1] - CENTRE) + pull[a][2] * (o[2] - CENTRE)
            )
            push.append(mw * v[a] - moved)
        return mw, push, pull, [axis_weights(o[i]) for i in range(3)]

    def deposit_tile(j):
        mw, push, pull, weights = terms(j)
        for e in range(6):
            at = weights[0][e]
            wx[j, e] = at
            side = [mw]
            side += [push[a] + (e - CENTRE) * pull[a][0] for a in range(3)]
            side += [pull[a][b] for b in (1, 2) for a in range(3)]
            for i, value in enumerate(side):
                side_rows[j, pl.ds(8 * (6 * i + e), 8), :] = value * at
        for e in range(6):
            for z in range(6):
                value = weights[1][e] * weights[2][z]
                plane_rows[j, 0, pl.ds(8 * (8 * e + z), 8), :] = value
                plane_rows[j, 1, pl.ds(8 * (8 * e + (z + 4) % 8), 8), :] = value
        totals = []
        for odd in range(2):
            k = 2 * j + odd
            for c in range(CHUNKS):
                s = CHUNKS * odd + c
                lanes = pl.ds(128 * c, 128)
                high, low = split(plane_rows[j, odd, pl.ds(s, 48, stride=8), :])
                bs[k, 0:48, lanes] = high
                bs[k, 64:112, lanes] = low
                high, low = split(side_rows[j, pl.ds(s, 64, stride=8), :])
                sides[k, 0:64, lanes] = high
                sides[k, 64:128, lanes] = low
            dots = lax.dot_general(
                sides[k], bs[k], (((1,), (1,)), ((), ())), preferred_element_type=jnp.float32
            )
            totals.append(dots[:64] + dots[64:])
        for i in range(8):
            one, two = totals[0][8 * i : 8 * i + 8], totals[1][8 * i : 8 * i + 8]
            pairs[j, pl.ds(8 * i, 8), :] = jnp.where(half, one, two) + pltpu.roll(
                jnp.where(half, two, one), 64, 1
            )
        pair = [pairs[j, pl.ds(6 * i, 8), :] for i in range(10)]
        return [pair[0]] + [pair[1 + a] + ey * pair[4 + a] + ez * pair[7 + a] for a in range(3)]

    def rolled(value, shift):
        return value if shift % 128 == 0 else pltpu.roll(value, shift % 128, 1)

    def send(step, p, before, first, second):
        low, high = zero, zero
        for i in range(4):
            one = jnp.where(own, first[i], before[i])
            two = jnp.where(own, second[i], first[i])
            near, far = jnp.where(half, one, two), jnp.where(half, two, one)
            send_x[step, 4 * p + i] = near + rolled(far, 64)
            to_low = rolled(near, 16 * i) + rolled(far, 16 * i + 64)
            to_high = rolled(near, 16 * i - 32) + rolled(far, 16 * i + 32)
            low = jnp.where(group == i, to_low, low)
            high = jnp.where(group == i, to_high, high)
        send_low[step, p] = low
        send_high[step, p] = high

    def grid_speed(step, p, turn):
        below = recv_low[step, p] + diag_low[step, p]
        above = recv_high[step, p] + diag_high[step, p]
        total = []
        for i in range(4):
            from_low = rolled(below, turn - 16 * i)
            from_high = rolled(above, turn + 32 - 16 * i)
            extra = jnp.where(group == 0, from_low, jnp.where(group == 2, from_high, 0.0))
            total.append(rolled(send_x[step, 4 * p + i] + recv_x[step, 4 * p + i], turn) + extra)
        scale = 1.0 / jnp.maximum(total[0], mass_floor)
        speed_x = total[1] * scale + time_step * gravity_slope
        speed_y = total[2] * scale
        speed_z = total[3] * scale + time_step * gravity_vertical
        place_z = 16 * p + jnp.where(half, turn // 8, 8 - turn // 8) + r3
        speed_x = jnp.where(place_x < 2, jnp.maximum(speed_x, 0.0), speed_x)
        speed_x = jnp.where(place_x >= 4 * nx - 2, jnp.minimum(speed_x, 0.0), speed_x)
        speed_y = jnp.where(place_y < 2, jnp.maximum(speed_y, 0.0), speed_y)
        speed_y = jnp.where(place_y >= 4 * ny - 2, jnp.minimum(speed_y, 0.0), speed_y)
        speed_z = jnp.where(place_z >= 8 * TILES - 2, jnp.minimum(speed_z, 0.0), speed_z)
        still = outside | (place_z < 2)
        return [jnp.where(still, 0.0, speed) for speed in (speed_x, speed_y, speed_z)]

    def windows(k, speed, turned, beyond, beyond_turned):
        for a in range(3):
            first, second = (speed[a], turned[a]) if k % 4 < 2 else (turned[a], speed[a])
            if k % 2 == 0:
                window = jnp.where(half, first, second)
            elif k % 4 == 1:
                window = jnp.where(own_tile, first, second)
            else:
                window = jnp.where(
                    r3 >= 4,
                    jnp.where(half, first, second),
                    jnp.where(half, beyond[a], beyond_turned[a]),
                )
            for b, factor in enumerate((None, ex, ey, ez_odd if k % 2 else ez_even)):
                q = 3 * b + a
                value = window if factor is None else window * factor
                us[k, pl.ds(q, 8, stride=12), :] = value

    def gather(k):
        left = jnp.concatenate(split(us[k, 0:80, :]), axis=1)
        planes = bs[k]
        taken = lax.dot_general(
            left, jnp.concatenate([planes, planes], axis=0),
            (((1,), (0,)), ((), ())), preferred_element_type=jnp.float32,
        )
        for c in range(CHUNKS):
            s = CHUNKS * (k % 2) + c
            gathered[k // 2, pl.ds(s, 72, stride=8), :] = taken[:72, 128 * c : 128 * c + 128]

    def advance(j):
        rows = pl.ds(8 * j, 8)
        weights = [wx[j, e] for e in range(6)]

        def quantity(q):
            value = weights[0] * gathered[j, pl.ds(8 * q, 8), :]
            for e in range(1, 6):
                value = value + weights[e] * gathered[j, pl.ds(8 * (12 * e + q), 8), :]
            return value

        o = [off[i, rows, :] for i in range(3)]
        f = [frame[i, rows, :] for i in range(9)]
        v = [quantity(a) for a in range(3)]
        c = [None] * 9
        for a in range(3):
            for b in range(3):
                c[3 * a + b] = 4.0 * (quantity(3 + 3 * b + a) - v[a] * (o[b] - CENTRE))
        o = [o[a] + time_step * v[a] for a in range(3)]
        f = [
            f[3 * a + b]
            + time_step * (c[3 * a] * f[b] + c[3 * a + 1] * f[3 + b] + c[3 * a + 2] * f[6 + b])
            for a in range(3)
            for b in range(3)
        ]
        for ref, values in ((off, o), (vel, v), (aff, c), (frame, f)):
            for i, value in enumerate(values):
                ref[i, rows, :] = value
        return o, f, v, c

    def one_step(step, carry):
        fields = [deposit_tile(j) for j in range(TILES)]
        send(step, 0, [zero] * 4, fields[0], fields[1])
        send(step, 1, fields[1], fields[2], fields[3])

        @pl.when(step == 0)
        def _():
            pl.semaphore_wait(barrier, around)

        each_neighbour(lambda d: copy_to(step, d).start())

        each_edge(lambda rows: passed(recv_sem.at[step], rows))
        speed = [grid_speed(step, p, 0) for p in range(2)] + [[zero] * 3]
        turned = [grid_speed(step, p, 64) for p in range(2)] + [[zero] * 3]
        for k in range(BLOCKS):
            p = k // 4
            windows(k, speed[p], turned[p], speed[p + 1], turned[p + 1])
        for k in range(BLOCKS):
            gather(k)
        for j in range(TILES):
            advance(j)
        return carry

    lax.fori_loop(0, STEPS, one_step, 0)

    each_edge(lambda rows: passed(send_sem, STEPS * rows))
    live = live_ref[...]
    for ref, count in ((off, 3), (vel, 3), (aff, 9), (frame, 9)):
        for i in range(count):
            ref[i] = ref[i] * live


def write_out(off, vel, aff, frame, off_out, vel_out, aff_out, frame_out, sem):
    copies = [
        pltpu.make_async_copy(source, target, sem.at[i])
        for i, (source, target) in enumerate(
            ((aff, aff_out), (frame, frame_out), (off, off_out), (vel, vel_out))
        )
    ]
    for copy in copies:
        copy.start()
    for copy in copies:
        copy.wait()


def per_device(offsets, velocity, affine, strain, particle_mass, plastic_ratio, block_counts):
    nx, ny = lax.axis_size("slope"), lax.axis_size("cross")
    f32 = jnp.float32
    vmem = pl.BlockSpec(memory_space=pltpu.VMEM)
    hbm = pl.BlockSpec(memory_space=pltpu.HBM)
    outs = pl.pallas_call(
        functools.partial(kernel, nx, ny),
        out_shape=[jax.ShapeDtypeStruct((n, ROWS, 128), f32) for n in (3, 3, 9, 9)],
        in_specs=[hbm] * 7,
        out_specs=[vmem] * 4,
        scratch_shapes=[
            pltpu.SMEM((BLOCKS,), jnp.int32),
            pltpu.VMEM((9, ROWS, 128), f32),
            pltpu.VMEM((ROWS, 128), f32),
            pltpu.VMEM((ROWS, 128), f32),
            pltpu.VMEM((ROWS, 128), f32),
            pltpu.VMEM((ROWS, 128), f32),
            pltpu.VMEM((ROWS, 128), f32),
            pltpu.VMEM((TILES, 6, 8, 128), f32),
            pltpu.VMEM((TILES, 512, 128), f32),
            pltpu.VMEM((TILES, 2, 384, 128), f32),
            pltpu.VMEM((TILES, 64, 128), f32),
            pltpu.VMEM((BLOCKS, 128, 512), jnp.bfloat16),
            pltpu.VMEM((BLOCKS, 128, 512), jnp.bfloat16),
            pltpu.VMEM((BLOCKS, 96, 128), f32),
            pltpu.VMEM((TILES, 576, 128), f32),
            pltpu.VMEM((STEPS * 72, 128), f32),
            pltpu.VMEM((STEPS, 8, 8, 128), f32),
            pltpu.VMEM((STEPS, 2, 8, 128), f32),
            pltpu.VMEM((STEPS, 2, 8, 128), f32),
            pltpu.VMEM((STEPS, 8, 8, 128), f32),
            pltpu.VMEM((STEPS, 2, 8, 128), f32),
            pltpu.VMEM((STEPS, 2, 8, 128), f32),
            pltpu.VMEM((STEPS, 2, 8, 128), f32),
            pltpu.VMEM((STEPS, 2, 8, 128), f32),
            pltpu.SemaphoreType.DMA((7,)),
            pltpu.SemaphoreType.DMA,
            pltpu.SemaphoreType.DMA((STEPS,)),
        ],
        compiler_params=pltpu.CompilerParams(
            collective_id=0, has_side_effects=True, vmem_limit_bytes=VMEM_BYTES
        ),
    )(
        *(
            pltpu.with_memory_space_constraint(value, pltpu.HBM)
            for value in (
                block_counts.reshape(BLOCKS),
                offsets.reshape(3, ROWS, 128),
                velocity.reshape(3, ROWS, 128),
                affine.reshape(9, ROWS, 128),
                strain.reshape(9, ROWS, 128),
                particle_mass.reshape(ROWS, 128),
                plastic_ratio.reshape(ROWS, 128),
            )
        ),
    )
    outs = pl.pallas_call(
        write_out,
        out_shape=[jax.ShapeDtypeStruct(out.shape, f32) for out in outs],
        in_specs=[vmem] * 4,
        out_specs=[hbm] * 4,
        scratch_shapes=[pltpu.SemaphoreType.DMA((4,))],
        compiler_params=pltpu.CompilerParams(vmem_limit_bytes=VMEM_BYTES),
    )(*outs)
    return tuple(out.reshape(out.shape[0], 1, 1, ROWS * 128) for out in outs)


def solution(mesh):
    wide = P(None, "slope", "cross", None)
    flat = P("slope", "cross", None)
    return jax.shard_map(
        per_device,
        mesh=mesh,
        in_specs=(wide, wide, wide, wide, flat, flat, flat),
        out_specs=(wide, wide, wide, wide),
        check_vma=False,
    )
```
